32 devices in a mesh: dp: 8 (over y, x, core), mp: 4 (over z).
Axes of the slice: x: 2, y: 2, z: 4, core: 2. Of those that a mesh axis runs over, the one named last changes fastest.
Arguments:
- inputs: bfloat16 [2, 10240, 1024], P(None, 'dp', 'mp'), may hold values from -6 to 6
- cotangent: bfloat16 [2, 10240, 1024], P(None, 'dp', 'mp'), may hold values from -6 to 6
- boundary_flags: int32 [2, 10240], P(None, 'dp'), may hold values from 0 to 1, as said below
- segment_ids: int32 [2, 10240], P(None, 'dp'), may hold values from 0 to 3, as said below
- mamba_norm: bfloat16 [2, 1024], replicated, may hold values from 0.5 to 1.5
- mamba_z: bfloat16 [2, 1024, 2048], P(None, 'dp', 'mp'), may hold values from -0.1875 to 0.1875
- mamba_x: bfloat16 [2, 1024, 2048], P(None, 'dp', 'mp'), may hold values from -0.1875 to 0.1875
- mamba_bc: bfloat16 [2, 1024, 256], P(None, 'dp'), may hold values from -0.1875 to 0.1875
- mamba_dt: bfloat16 [2, 1024, 32], P(None, 'dp', 'mp'), may hold values from -0.1875 to 0.1875
- mamba_conv_x: bfloat16 [2, 4, 2048], replicated, may hold values from -3 to 3
- mamba_conv_bc: bfloat16 [2, 4, 256], replicated, may hold values from -3 to 3
- mamba_dt_bias: bfloat16 [2, 32], replicated, may hold values from -5 to -2
- mamba_a_log: bfloat16 [2, 32], replicated, may hold values from 0 to 2.5
- mamba_skip: bfloat16 [2, 32], replicated, may hold values from 0.5 to 1.5
- mamba_gate_norm: bfloat16 [2, 2048], replicated, may hold values from 0.5 to 1.5
- mamba_out: bfloat16 [2, 2048, 1024], P(None, 'mp', 'dp'), may hold values from -0.125 to 0.125
- router_qk: bfloat16 [2, 1024, 1024], P(None, 'dp', 'mp'), may hold values from -0.1875 to 0.1875
- group_up: bfloat16 [1024, 1536], P('dp', 'mp'), may hold values from -0.1875 to 0.1875
- group_down: bfloat16 [1536, 1024], P('dp', 'mp'), may hold values from -0.15625 to 0.15625
- attn_norms: bfloat16 [2, 1536], replicated, may hold values from 0.5 to 1.5
- attn_qkv: bfloat16 [3, 1536, 1536], P(None, 'dp', 'mp'), may hold values from -0.15625 to 0.15625
- attn_out: bfloat16 [1536, 1536], P('mp', 'dp'), may hold values from -0.625 to 0.625
- ffn_gate_up: bfloat16 [2, 1536, 4096], P(None, 'dp', 'mp'), may hold values from -0.15625 to 0.15625
- ffn_down: bfloat16 [4096, 1536], P('mp', 'dp'), may hold values from -0.09375 to 0.09375
Outputs:
- outputs: bfloat16 [2, 10240, 1024], P(None, 'dp', 'mp')
- grad_inputs: float32 [2, 10240, 1024], P(None, 'dp', 'mp')
- grad_mamba_norm: float32 [2, 1024], replicated
- grad_mamba_z: float32 [2, 1024, 2048], P(None, 'dp', 'mp')
- grad_mamba_x: float32 [2, 1024, 2048], P(None, 'dp', 'mp')
- grad_mamba_bc: float32 [2, 1024, 256], P(None, 'dp')
- grad_mamba_dt: float32 [2, 1024, 32], P(None, 'dp', 'mp')
- grad_mamba_conv_x: float32 [2, 4, 2048], replicated
- grad_mamba_conv_bc: float32 [2, 4, 256], replicated
- grad_mamba_dt_bias: float32 [2, 32], replicated
- grad_mamba_a_log: float32 [2, 32], replicated
- grad_mamba_skip: float32 [2, 32], replicated
- grad_mamba_gate_norm: float32 [2, 2048], replicated
- grad_mamba_out: float32 [2, 2048, 1024], P(None, 'mp', 'dp')
- grad_router_qk: float32 [2, 1024, 1024], P(None, 'dp', 'mp')
- grad_group_up: float32 [1024, 1536], P('dp', 'mp')
- grad_group_down: float32 [1536, 1024], P('dp', 'mp')
- grad_attn_norms: float32 [2, 1536], replicated
- grad_attn_qkv: float32 [3, 1536, 1536], P(None, 'dp', 'mp')
- grad_attn_out: float32 [1536, 1536], P('mp', 'dp')
- grad_ffn_gate_up: float32 [2, 1536, 4096], P(None, 'dp', 'mp')
- grad_ffn_down: float32 [4096, 1536], P('mp', 'dp')
The draws below stay inside these ranges and needn't reach their ends.
Inputs may be any that keep to these rules, and one draw needn't show every extreme that they name: `boundary_flags`: 1 at the first byte of every item; a sequence (1280 bytes of one micro-batch at one index of dp) has at most 320 ones, and in every micro-batch one sequence has exactly 320. `segment_ids`: each sequence of 1280 bytes packs 4 items numbered 0 to 3 in order, one of them 4 * 256 bytes long.
All inputs are finite; a program needn't handle non-finite values.
Results may differ from the reference program's by a relative error of at most 0.028.
Values may be sent and summed in bfloat16 or wider, within the bound.
No kernel may reach another device: no remote copies, remote signals or barrier semaphores. Data moves between devices by JAX's collectives and lax.ppermute only.
A program may use at most 448 MiB of HBM per device.

```python
import jax
import jax.numpy as jnp
from jax import lax

D = 1024
DI = 2048
HEADS = 32
STATE = 128
CONV = 4
DM = 1536
AHEADS = 24
FF = 4096
SEQ = 1280
MICRO = 2
CAP = 320
TOKENS = 10240


def item_layout(key):
    seq_count = MICRO * (TOKENS // SEQ)
    long_size = SEQ * 4 // 5
    short_total = SEQ - long_size
    half_rest = short_total // 2
    key_first, key_second, key_long = jax.random.split(key, 3)
    first_len = jax.random.randint(key_first, (seq_count,), 1, half_rest)
    second_len = jax.random.randint(key_second, (seq_count,), 1, half_rest)
    third_len = short_total - first_len - second_len
    long_at = jax.random.randint(key_long, (seq_count,), 0, 4)
    shorts = jnp.stack([first_len, second_len, third_len], 1)
    slot_ids = jnp.arange(4, dtype=jnp.int32)
    before = (slot_ids[None, :] > long_at[:, None]).astype(jnp.int32)
    short_index = jnp.clip(slot_ids[None, :] - before, 0, 2)
    picked = jnp.take_along_axis(shorts, short_index, 1)
    lengths = jnp.where(slot_ids[None, :] == long_at[:, None], long_size, picked)
    item_ends = jnp.cumsum(lengths, 1).astype(jnp.int32)
    places = jnp.arange(SEQ, dtype=jnp.int32)
    return jnp.sum((places[None, :, None] >= item_ends[:, None, :]).astype(jnp.int32), 2).astype(jnp.int32)


def draw_segment_ids(key, part):
    segment = item_layout(key)
    return segment.reshape(MICRO, TOKENS)


def draw_boundary_flags(key, part):
    segment = item_layout(key)
    key = jax.random.fold_in(key, 2)
    seq_count = segment.shape[0]
    per_micro = TOKENS // SEQ
    key_count, key_full, key_pick = jax.random.split(key, 3)
    targets = jax.random.randint(key_count, (seq_count,), CAP // 2, CAP + 1)
    fullest = jax.random.randint(key_full, (MICRO,), 0, per_micro)
    seq_ids = jnp.arange(seq_count, dtype=jnp.int32)
    full_owner = seq_ids // per_micro * per_micro + fullest[seq_ids // per_micro]
    targets = jnp.where(seq_ids == full_owner, CAP, targets)
    starts = jnp.concatenate([jnp.ones((seq_count, 1), jnp.bool_), segment[:, 1:] != segment[:, :-1]], 1)
    scores = jax.vmap(lambda k: jax.random.permutation(k, SEQ))(jax.random.split(key_pick, seq_count))
    scores = jnp.where(starts, SEQ + scores, scores)
    sorted_at = jnp.argsort(scores, axis=1)
    rank_of = jnp.argsort(sorted_at, axis=1)
    chosen = starts | (rank_of < (targets - 4)[:, None])
    return chosen.astype(jnp.int32).reshape(MICRO, TOKENS)


def raised(values, key, source, target, parts, factor):
    owner, partner = [(jnp.arange(values.shape[position]) // (values.shape[position] // parts)).reshape([-1 if axis == position else 1 for axis in range(values.ndim)]) for position in (source, target)]
    chosen = jax.random.permutation(key, parts)[partner]
    strong = (owner == chosen) | (owner == (partner + parts // 2) % parts)
    return jnp.where(strong, factor * values, values)


def block_levels(stream_key, extent, pieces, smallest, largest):
    loudness, own = 1.0, jax.random.fold_in(stream_key, 6)
    for position, shards_of in pieces:
        draws = jnp.exp(jax.random.uniform(jax.random.fold_in(own, position), (shards_of,), jnp.float32, smallest / len(pieces), largest / len(pieces)))
        loudness = loudness * jnp.repeat(draws, extent[position] // shards_of).reshape([-1 if axis == position else 1 for axis in range(len(extent))])
    return loudness


def bell_draw(rng, shape, width, limit, cuts=(), held_as=jnp.bfloat16):
    values = jax.random.normal(rng, shape, jnp.float32) * width
    if len(cuts) > 0:
        values = block_levels(rng, shape, cuts, -0.22, 0.18) * values
    return jnp.clip(values, min=-limit, max=limit).astype(held_as)


def heavy_noise(key, shape, scale, limit, cuts, heavy, kind=jnp.bfloat16):
    values = scale * jax.random.normal(key, shape, jnp.float32)
    if cuts:
        values = values * block_levels(key, shape, cuts, -0.22, 0.18)
    return jnp.clip(raised(values, jax.random.fold_in(key, 3), *heavy), -limit, limit).astype(kind)


def setup_inputs(seed: int = 0) -> dict:
    streams_of = jax.random.split(jax.random.key(seed), 25)
    inputs = heavy_noise(streams_of[0], (MICRO, TOKENS, D), 1.0, 6.0, ((1, 8), (2, 4)), (1, 2, 8, 2.0))
    cotangent = heavy_noise(streams_of[1], (MICRO, TOKENS, D), 1.0, 6.0, ((1, 8), (2, 4)), (1, 2, 8, 2.0))
    boundary_flags = draw_boundary_flags(jax.random.fold_in(streams_of[24], 71), 0)
    segment_ids = draw_segment_ids(jax.random.fold_in(streams_of[24], 71), 0)
    mamba_norm = jnp.clip(1.0 + 0.1 * jax.random.normal(streams_of[4], (2, D), jnp.float32), 0.5, 1.5).astype(jnp.bfloat16)
    mamba_z = bell_draw(streams_of[5], (2, D, DI), D ** -0.5, 0.1875, ((1, 8), (2, 4)))
    mamba_x = bell_draw(streams_of[6], (2, D, DI), D ** -0.5, 0.1875, ((1, 8), (2, 4)))
    mamba_bc = bell_draw(streams_of[7], (2, D, 2 * STATE), D ** -0.5, 0.1875, ((1, 8),))
    mamba_dt = bell_draw(streams_of[8], (2, D, HEADS), D ** -0.5, 0.1875, ((1, 8), (2, 4)))
    mamba_conv_x = bell_draw(streams_of[9], (2, CONV, DI), 0.5, 3.0)
    mamba_conv_bc = bell_draw(streams_of[10], (2, CONV, 2 * STATE), 0.5, 3.0)
    mamba_dt_bias = jnp.clip(jax.random.uniform(streams_of[11], (2, HEADS), jnp.float32, -5.0, -2.0), -5.0, -2.0).astype(jnp.bfloat16)
    mamba_a_log = jnp.clip(jax.random.uniform(streams_of[12], (2, HEADS), jnp.float32, 0.0, 2.5), 0.0, 2.5).astype(jnp.bfloat16)
    mamba_skip = jnp.clip(jax.random.uniform(streams_of[13], (2, HEADS), jnp.float32, 0.5, 1.5), 0.5, 1.5).astype(jnp.bfloat16)
    mamba_gate_norm = jnp.clip(1.0 + 0.1 * jax.random.normal(streams_of[14], (2, DI), jnp.float32), 0.5, 1.5).astype(jnp.bfloat16)
    mamba_out = bell_draw(streams_of[15], (2, DI, D), DI ** -0.5, 0.125, ((1, 4), (2, 8)))
    router_qk = bell_draw(streams_of[16], (2, D, D), D ** -0.5, 0.1875, ((1, 8), (2, 4)))
    group_up = bell_draw(streams_of[17], (D, DM), D ** -0.5, 0.1875, ((0, 8), (1, 4)))
    group_down = bell_draw(streams_of[18], (DM, D), DM ** -0.5, 0.15625, ((0, 8), (1, 4)))
    attn_norms = jnp.clip(1.0 + 0.1 * jax.random.normal(streams_of[19], (2, DM), jnp.float32), 0.5, 1.5).astype(jnp.bfloat16)
    attn_qkv = bell_draw(streams_of[20], (3, DM, DM), DM ** -0.5, 0.15625, ((1, 8), (2, 4)))
    attn_out = bell_draw(streams_of[21], (DM, DM), (DM // 16) ** -0.5, 0.625, ((0, 4), (1, 8)))
    ffn_gate_up = bell_draw(streams_of[22], (2, DM, FF), DM ** -0.5, 0.15625, ((1, 8), (2, 4)))
    ffn_down = bell_draw(streams_of[23], (FF, DM), FF ** -0.5, 0.09375, ((0, 4), (1, 8)))
    return dict(inputs=inputs, cotangent=cotangent, boundary_flags=boundary_flags, segment_ids=segment_ids, mamba_norm=mamba_norm, mamba_z=mamba_z, mamba_x=mamba_x, mamba_bc=mamba_bc, mamba_dt=mamba_dt, mamba_conv_x=mamba_conv_x, mamba_conv_bc=mamba_conv_bc, mamba_dt_bias=mamba_dt_bias, mamba_a_log=mamba_a_log, mamba_skip=mamba_skip, mamba_gate_norm=mamba_gate_norm, mamba_out=mamba_out, router_qk=router_qk, group_up=group_up, group_down=group_down, attn_norms=attn_norms, attn_qkv=attn_qkv, attn_out=attn_out, ffn_gate_up=ffn_gate_up, ffn_down=ffn_down)


EPSILON = 1e-06
HIGHEST = lax.Precision.HIGHEST

@jax.custom_vjp
def low(v):
    return lax.optimization_barrier(v.astype(jnp.bfloat16)).astype(jnp.float32)

@jax.custom_vjp
def low_back(v):
    return v

def low_keep(v):
    return (low(v), None)

def low_pass(kept, grad):
    return (grad,)

def back_keep(v):
    return (v, None)

def back_low(kept, grad):
    return (low(grad),)
low.defvjp(low_keep, low_pass)
low_back.defvjp(back_keep, back_low)

def rms_scale(values, gain):
    return values * lax.rsqrt(lax.optimization_barrier(jnp.mean(values * values, axis=-1, keepdims=True)) + EPSILON) * gain

def causal_conv(values, kernel, segment):
    tap_count = kernel.shape[0]
    length = values.shape[0]
    result = values * kernel[tap_count - 1]
    for offset in range(1, tap_count):
        shifted = jnp.concatenate([jnp.zeros((offset, values.shape[1]), values.dtype), values[:length - offset]], 0)
        shifted_seg = jnp.concatenate([jnp.full((offset,), -1, jnp.int32), segment[:length - offset].astype(jnp.int32)], 0)
        result = result + jnp.where((shifted_seg == segment)[:, None], shifted, 0.0) * kernel[tap_count - 1 - offset]
    return result

def state_scan(inputs, step_sizes, decays, in_map, out_map, segment):
    length, head_count, head_size = inputs.shape
    nstate = in_map.shape[1]
    blocksize = 256 if length % 256 == 0 else length
    block_count = length // blocksize
    lower_mask = jnp.tril(jnp.ones((blocksize, blocksize), jnp.bool_))

    def scan_block(carry, block_in):
        states, last_seg = carry
        block_x, block_step, block_decay, block_in_map, block_out_map, block_seg = block_in
        cumlog = jnp.cumsum(block_decay, axis=0)
        visible = ((block_seg[:, None] == block_seg[None, :]) & lower_mask)[:, :, None]
        log_gaps = cumlog[:, None, :] - cumlog[None, :, :]
        factors = jnp.where(visible, jnp.exp(jnp.where(visible, log_gaps, 0.0)), 0.0)
        intersection = jnp.dot(block_out_map, block_in_map.T, precision=HIGHEST)
        weights = intersection[:, :, None] * factors * block_step[None, :, :]
        outputs = jnp.einsum('ijh,jhp->ihp', weights, block_x, precision=HIGHEST)
        carried = (block_seg == last_seg).astype(block_x.dtype)
        reach_back = jnp.exp(cumlog) * carried[:, None]
        outputs = outputs + jnp.einsum('in,hpn->ihp', block_out_map, states, precision=HIGHEST) * reach_back[:, :, None]
        end_seg = block_seg[-1]
        to_end = jnp.where((block_seg == end_seg)[:, None], jnp.exp(cumlog[-1][None, :] - cumlog), 0.0) * block_step
        new_terms = jnp.einsum('jh,jn,jhp->hpn', to_end, block_in_map, block_x, precision=HIGHEST)
        kept_part = jnp.exp(cumlog[-1]) * (last_seg == end_seg).astype(block_x.dtype)
        states = states * kept_part[:, None, None] + new_terms
        return ((states, end_seg), outputs)

    def by_block(array):
        return array.reshape((block_count, blocksize) + array.shape[1:])
    start_carry = (jnp.zeros((head_count, head_size, nstate), inputs.dtype), jnp.array(-1, jnp.int32))
    end_carry, outputs = lax.scan(jax.checkpoint(scan_block), start_carry, (by_block(inputs), by_block(step_sizes), by_block(decays), by_block(in_map), by_block(out_map), by_block(segment.astype(jnp.int32))))
    return outputs.reshape(length, head_count, head_size)

def mamba_mixer(z_proj, x_proj, bc_proj, dt_proj, conv_x, conv_bc, dt_bias, decay_log, skip_gain, norm_gain, segment):
    length = x_proj.shape[0]
    head_count = dt_proj.shape[1]
    head_size = x_proj.shape[1] // head_count
    nstate = bc_proj.shape[1] // 2
    conv_out = jax.nn.silu(causal_conv(x_proj, conv_x, segment))
    maps_all = jax.nn.silu(causal_conv(bc_proj, conv_bc, segment))
    step_sizes = jax.nn.softplus(dt_proj + dt_bias)
    decays = -jnp.exp(decay_log) * step_sizes
    inputs = conv_out.reshape(length, head_count, head_size)
    outputs = state_scan(inputs, step_sizes, decays, maps_all[:, :nstate], maps_all[:, nstate:], segment) + skip_gain[None, :, None] * inputs
    gated = outputs.reshape(length, head_count * head_size) * jax.nn.silu(z_proj)
    return rms_scale(gated, norm_gain)

def rotate_pairs(values, head_count):
    length = values.shape[0]
    head_size = values.shape[1] // head_count
    half_size = head_size // 2
    frequency = 10000.0 ** (-jnp.arange(half_size, dtype=values.dtype) * (2.0 / head_size))
    angles = jnp.arange(length, dtype=values.dtype)[:, None] * frequency[None, :]
    cosines = jnp.cos(angles)[:, None, :]
    sines = jnp.sin(angles)[:, None, :]
    pairs_in = values.reshape(length, head_count, head_size)
    first_half = pairs_in[..., :half_size]
    second_half = pairs_in[..., half_size:]
    turned = jnp.concatenate([first_half * cosines - second_half * sines, first_half * sines + second_half * cosines], -1)
    return turned.reshape(length, head_count * head_size)

def attend(queries, key_proj, value_proj, group_seg, head_count):
    length = queries.shape[0]
    head_size = queries.shape[1] // head_count
    query_rot = low(rotate_pairs(queries, head_count)).reshape(length, head_count, head_size)
    key_rot = low(rotate_pairs(key_proj, head_count)).reshape(length, head_count, head_size)
    value_low = low(value_proj).reshape(length, head_count, head_size)
    places = jnp.arange(length)
    visible = (places[:, None] >= places[None, :]) & (group_seg[:, None] == group_seg[None, :])
    scores = low_back(jnp.einsum('ihd,jhd->hij', query_rot, key_rot, precision=HIGHEST) * head_size ** (-0.5))
    scores = jnp.where(visible[None], scores, -1e+30)
    weights = low(jax.nn.softmax(scores, axis=-1))
    mixed = low(low_back(jnp.einsum('hij,jhd->ihd', weights, value_low, precision=HIGHEST)))
    return mixed.reshape(length, head_count * head_size)

def pair_dots(queries, key_proj):
    previous = jnp.concatenate([jnp.zeros((1, key_proj.shape[1]), key_proj.dtype), key_proj[:-1]], 0)
    return jnp.stack([lax.optimization_barrier(jnp.sum(queries * previous, axis=1)), lax.optimization_barrier(jnp.sum(queries * queries, axis=1)), lax.optimization_barrier(jnp.sum(previous * previous, axis=1))], 0)

def boundary_prob(all_dots, starts):
    cosine = all_dots[0] * lax.rsqrt(all_dots[1] + EPSILON) * lax.rsqrt(all_dots[2] + EPSILON)
    return jnp.where(starts, 1.0, 0.5 * (1.0 - cosine))

def group_layout(flag_row, capacity):
    group_rank = (jnp.cumsum(flag_row) - 1).astype(jnp.int32)
    slot_ids = jnp.arange(capacity, dtype=jnp.int32)
    places = jnp.arange(flag_row.shape[0], dtype=jnp.int32)
    marked = (group_rank[None, :] == slot_ids[:, None]) & (flag_row[None, :] == 1)
    positions = lax.optimization_barrier(jnp.sum(jnp.where(marked, places[None, :], 0), axis=1)).astype(jnp.int32)
    slot_valid = jnp.any(marked, axis=1)
    return (group_rank, positions, slot_valid)

def smooth_groups(down_rows, group_probs):

    def combine(earlier, later):
        return (earlier[0] * later[0], later[0] * earlier[1] + later[1])
    decay_part = (1.0 - group_probs)[:, None]
    scanned = lax.associative_scan(combine, (decay_part, group_probs[:, None] * down_rows))
    return scanned[1]

def spread_groups(down_rows, prob_row, flag_row, group_rank, positions, slot_valid):
    group_probs = jnp.where(slot_valid, jnp.take(prob_row, positions), 1.0)
    smooth = smooth_groups(down_rows, group_probs)
    confidence = jnp.where(flag_row == 1, prob_row, 1.0 - prob_row)
    return confidence[:, None] * jnp.take(smooth, group_rank, axis=0)

def mamba_layer(residual, layer_index, params, segment):
    norm_w, proj_z, proj_x, proj_bc, proj_dt, conv_x, conv_bc, dt_bias, decay_log, skip_gain, gate_norm, proj_out = params
    normed = low(rms_scale(low(residual), norm_w[layer_index]))
    mixed = low(mamba_mixer(low_back(jnp.dot(normed, proj_z[layer_index], precision=HIGHEST)), low_back(jnp.dot(normed, proj_x[layer_index], precision=HIGHEST)), low_back(jnp.dot(normed, proj_bc[layer_index], precision=HIGHEST)), low_back(jnp.dot(normed, proj_dt[layer_index], precision=HIGHEST)), conv_x[layer_index], conv_bc[layer_index], dt_bias[layer_index], decay_log[layer_index], skip_gain[layer_index], gate_norm[layer_index], segment))
    return residual + low_back(jnp.dot(mixed, proj_out[layer_index], precision=HIGHEST))

def block_forward(params, residual, flag_row, segment):
    router_qk, group_up, group_down, attn_norms, attn_qkv, attn_out, ffn_gate_up, ffn_down = params[12:]
    mamba_params = params[:12]
    encoded = mamba_layer(residual, 0, mamba_params, segment)
    starts = jnp.concatenate([jnp.ones((1,), jnp.bool_), segment[1:] != segment[:-1]])
    group_rank, positions, slot_valid = group_layout(flag_row, CAP)
    shared = low(encoded)
    queries = low_back(jnp.dot(shared, router_qk[0], precision=HIGHEST))
    key_proj = low_back(jnp.dot(shared, router_qk[1], precision=HIGHEST))
    prob_row = boundary_prob(pair_dots(queries, key_proj), starts)
    group_rows = jnp.take(shared, positions, axis=0) * slot_valid[:, None].astype(shared.dtype)
    group_seg = jnp.where(slot_valid, jnp.take(segment, positions), -1)
    hidden = low_back(jnp.dot(group_rows, group_up, precision=HIGHEST))
    first_norm = low(rms_scale(low(hidden), attn_norms[0]))
    attended = attend(low_back(jnp.dot(first_norm, attn_qkv[0], precision=HIGHEST)), low_back(jnp.dot(first_norm, attn_qkv[1], precision=HIGHEST)), low_back(jnp.dot(first_norm, attn_qkv[2], precision=HIGHEST)), group_seg, AHEADS)
    hidden = hidden + low_back(jnp.dot(attended, attn_out, precision=HIGHEST))
    second_norm = low(rms_scale(low(hidden), attn_norms[1]))
    gate_proj = low_back(jnp.dot(second_norm, ffn_gate_up[0], precision=HIGHEST))
    up_proj = low_back(jnp.dot(second_norm, ffn_gate_up[1], precision=HIGHEST))
    active = low(jax.nn.silu(gate_proj) * up_proj)
    hidden = hidden + low_back(jnp.dot(active, ffn_down, precision=HIGHEST))
    down_rows = low_back(jnp.dot(low(hidden), group_down, precision=HIGHEST))
    decoder_in = encoded + spread_groups(down_rows, prob_row, flag_row, group_rank, positions, slot_valid)
    return mamba_layer(decoder_in, 1, mamba_params, segment)

def reference(inputs, cotangent, boundary_flags, segment_ids, mamba_norm, mamba_z, mamba_x, mamba_bc, mamba_dt, mamba_conv_x, mamba_conv_bc, mamba_dt_bias, mamba_a_log, mamba_skip, mamba_gate_norm, mamba_out, router_qk, group_up, group_down, attn_norms, attn_qkv, attn_out, ffn_gate_up, ffn_down):
    params = tuple((weight.astype(jnp.float32) for weight in (mamba_norm, mamba_z, mamba_x, mamba_bc, mamba_dt, mamba_conv_x, mamba_conv_bc, mamba_dt_bias, mamba_a_log, mamba_skip, mamba_gate_norm, mamba_out, router_qk, group_up, group_down, attn_norms, attn_qkv, attn_out, ffn_gate_up, ffn_down)))
    seq_count = inputs.shape[0] * (inputs.shape[1] // SEQ)
    inputs_all = inputs.astype(jnp.float32).reshape(seq_count, SEQ, D)
    cot_all = cotangent.astype(jnp.float32).reshape(seq_count, SEQ, D)
    flag_all = boundary_flags.reshape(seq_count, SEQ)
    segment_all = segment_ids.reshape(seq_count, SEQ)

    def one_sequence(totals, items_in):
        residual, cot_row, flag_row, segment_row = items_in
        result, pullback = jax.vjp(lambda weights, start: block_forward(weights, start, flag_row, segment_row), params, residual)
        weight_grads, input_grad = pullback(cot_row)
        totals = jax.tree.map(lambda a, b: a + b, totals, weight_grads)
        return (totals, (result, input_grad))
    zero_totals = jax.tree.map(jnp.zeros_like, params)
    totals, (results, input_grads) = lax.scan(one_sequence, zero_totals, (inputs_all, cot_all, flag_all, segment_all))
    return (results.reshape(inputs.shape).astype(jnp.bfloat16), input_grads.reshape(inputs.shape), totals[0], totals[1], totals[2], totals[3], totals[4], totals[5], totals[6], totals[7], totals[8], totals[9], totals[10], totals[11], totals[12], totals[13], totals[14], totals[15], totals[16], totals[17], totals[18], totals[19])
```

```python
import functools

import jax
import jax.numpy as jnp
from jax import lax
from jax.experimental import pallas as pl
from jax.experimental.pallas import tpu as pltpu
from jax.sharding import PartitionSpec as P

DM = 1536
AHEADS = 24
CAP = 320


EPSILON = 1e-06
HIGHEST = lax.Precision.HIGHEST


def boundary_prob(all_dots, starts):
    cosine = all_dots[0] * lax.rsqrt(all_dots[1] + EPSILON) * lax.rsqrt(all_dots[2] + EPSILON)
    return jnp.where(starts, 1.0, 0.5 * (1.0 - cosine))


def to_low(values):
    return values.astype(jnp.bfloat16)


def matmul(left, right):
    return jnp.dot(left, right, preferred_element_type=jnp.float32)


def left_product(left, right):
    return lax.dot_general(
        left, right, (((0,), (0,)), ((), ())), preferred_element_type=jnp.float32
    )


def right_product(left, right):
    return lax.dot_general(
        left, right, (((1,), (1,)), ((), ())), preferred_element_type=jnp.float32
    )


BLOCK = 128
LANES = 128
HEAD_SIZE = 64


def sigmoid(values):
    return 1.0 / (1.0 + jnp.exp(-values))


def split_product(values, ones_low):
    high = to_low(values)
    rest = to_low(values - high.astype(jnp.float32))
    return matmul(high, ones_low) + matmul(rest, ones_low)


def exact_product(left, right):
    return jnp.dot(left, right, precision=HIGHEST, preferred_element_type=jnp.float32)


def shifted_down(tail, block, steps):
    joined = jnp.concatenate([tail, block], 0)
    return pltpu.roll(joined, steps, 0)[8:]


def shifted_up(block, head, steps):
    joined = jnp.concatenate([block, head], 0)
    size = joined.shape[0]
    return pltpu.roll(joined, size - steps, 0)[: size - 8]


def filtered(tail, block, taps, columns):
    result = block * taps[3:4]
    for steps in range(1, 4):
        moved = shifted_down(tail, block, steps)
        result = result + moved * columns[:, steps - 1 : steps] * taps[3 - steps : 4 - steps]
    return result


def pair_columns(values, pair, first_half):
    return jnp.where(
        first_half, values[:, 2 * pair : 2 * pair + 1], values[:, 2 * pair + 1 : 2 * pair + 2]
    )


def stacked_halves(values, first_half):
    zero = jnp.zeros_like(values)
    return jnp.concatenate(
        [jnp.where(first_half, values, zero), jnp.where(first_half, zero, values)], 0
    )


def folded_rows(values):
    return jnp.sum(values.reshape(values.shape[0] // 8, 8, values.shape[1]), axis=0)


class Decay:
    def __init__(self, dt_raw, dt_bias, rate, columns, segment_row):
        rows = lax.broadcasted_iota(jnp.int32, (BLOCK, BLOCK), 0)
        cols = lax.broadcasted_iota(jnp.int32, (BLOCK, BLOCK), 1)
        self.lower = rows >= cols
        shifted = dt_raw + dt_bias
        self.steepness = sigmoid(shifted)
        self.step = jnp.maximum(shifted, 0.0) + jnp.log(1.0 + jnp.exp(-jnp.abs(shifted)))
        self.decay = rate * self.step
        self.total = exact_product(self.lower.astype(jnp.float32), self.decay)
        self.total_rows = self.total.T
        same = self.lower & (columns[:, 3:4] == segment_row)
        self.mask = jnp.where(same, 0.0, -1e30)
        last = self.total[BLOCK - 1 : BLOCK]
        self.reach = jnp.exp(self.total) * columns[:, 4:5]
        self.to_end = jnp.exp(last - self.total) * columns[:, 5:6]
        self.kept = jnp.exp(last) * columns[BLOCK - 1 : BLOCK, 4:5]

    def factor(self, head):
        return jnp.exp(
            self.total[:, head : head + 1] - self.total_rows[head : head + 1] + self.mask
        )


def zx_lanes(pair, per_block):
    block, tile = divmod(pair, per_block)
    start = (2 * block * per_block + tile) * LANES
    shift = per_block * LANES
    return slice(start, start + LANES), slice(start + shift, start + shift + LANES)


def mix_kernel(
    per_block,
    zx_ref,
    bcdt_ref,
    columns_ref,
    segment_ref,
    taps_ref,
    map_taps_ref,
    heads_ref,
    channels_ref,
    mixed_ref,
    y_ref,
    square_ref,
    states_ref,
    state,
    tail_x,
    tail_maps,
    ends,
):
    pairs = channels_ref.shape[1] // LANES

    @pl.when(pl.program_id(0) == 0)
    def _():
        state[...] = jnp.zeros_like(state)
        tail_x[...] = jnp.zeros_like(tail_x)
        tail_maps[...] = jnp.zeros_like(tail_maps)

    columns = columns_ref[...]
    first_half = lax.broadcasted_iota(jnp.int32, (1, LANES), 1) < HEAD_SIZE
    maps_in = bcdt_ref[:, : 2 * LANES]
    maps = filtered(tail_maps[...], maps_in, map_taps_ref[...], columns)
    maps = maps * sigmoid(maps)
    in_map = to_low(maps[:, :LANES])
    out_map = to_low(maps[:, LANES:])
    heads = heads_ref[...]
    decay = Decay(
        bcdt_ref[:, 2 * LANES :], heads[0:1], heads[1:2], columns, segment_ref[0, 0:1, :]
    )
    meeting = right_product(out_map, in_map)
    low_state = to_low(state[...])
    states_ref[...] = low_state
    y_ref[...] = matmul(out_map, low_state)
    squares = jnp.zeros((BLOCK, LANES), jnp.float32)
    for pair in range(pairs):
        lanes = slice(pair * LANES, (pair + 1) * LANES)
        z_lanes, x_lanes = zx_lanes(pair, per_block)
        block = zx_ref[:, x_lanes]
        pre = filtered(tail_x[:, lanes], block, taps_ref[:, lanes], columns)
        tail_x[:, lanes] = block[BLOCK - 8 :]
        value = pre * sigmoid(pre)
        scaled = value * pair_columns(decay.step, pair, first_half)
        ends[:, lanes] = to_low(scaled * pair_columns(decay.to_end, pair, first_half))
        weights = jnp.concatenate(
            [to_low(meeting * decay.factor(2 * pair + half)) for half in range(2)], 1
        )
        y = matmul(weights, stacked_halves(to_low(scaled), first_half))
        y = y + y_ref[:, lanes] * pair_columns(decay.reach, pair, first_half)
        y_ref[:, lanes] = y
        gate_in = zx_ref[:, z_lanes]
        gated = (y + channels_ref[0:1, lanes] * value) * (gate_in * sigmoid(gate_in))
        squares = squares + gated * gated
        mixed_ref[:, lanes] = to_low(gated * channels_ref[1:2, lanes])
        state[:, lanes] = state[:, lanes] * pair_columns(decay.kept, pair, first_half)
    square_ref[...] = jnp.sum(squares, axis=1, keepdims=True)
    state[...] += left_product(in_map, ends[...])
    tail_maps[...] = bcdt_ref[BLOCK - 8 :, : 2 * LANES]


def mix_back_kernel(
    per_block,
    grad_ref,
    zx_ref,
    zx_tail_ref,
    bcdt_ref,
    maps_tail_ref,
    y_ref,
    states_ref,
    columns_ref,
    later_ref,
    segment_ref,
    taps_ref,
    map_taps_ref,
    heads_ref,
    channels_ref,
    owner_ref,
    grad_zx_ref,
    grad_maps_ref,
    grad_dt_ref,
    grad_taps_ref,
    grad_map_taps_ref,
    grad_heads_ref,
    grad_channels_ref,
    grad_state,
    head_x,
    head_maps,
    ends,
    reached,
    pulled,
    balance,
    step_part,
):
    pairs = channels_ref.shape[1] // LANES
    step = pl.program_id(0)
    first_chunk = step == pl.num_programs(0) - 1

    @pl.when(step == 0)
    def _():
        grad_state[...] = jnp.zeros_like(grad_state)
        head_x[...] = jnp.zeros_like(head_x)
        head_maps[...] = jnp.zeros_like(head_maps)
        grad_taps_ref[...] = jnp.zeros_like(grad_taps_ref)
        grad_map_taps_ref[...] = jnp.zeros_like(grad_map_taps_ref)
        grad_heads_ref[...] = jnp.zeros_like(grad_heads_ref)
        grad_channels_ref[...] = jnp.zeros_like(grad_channels_ref)

    columns = columns_ref[...]
    later = later_ref[...]
    first_half = lax.broadcasted_iota(jnp.int32, (1, LANES), 1) < HEAD_SIZE
    tail_maps = jnp.where(first_chunk, 0.0, maps_tail_ref[:, : 2 * LANES])
    maps_in = bcdt_ref[:, : 2 * LANES]
    maps_pre = filtered(tail_maps, maps_in, map_taps_ref[...], columns)
    maps_open = sigmoid(maps_pre)
    maps = maps_pre * maps_open
    in_map = to_low(maps[:, :LANES])
    out_map = to_low(maps[:, LANES:])
    heads = heads_ref[...]
    decay = Decay(
        bcdt_ref[:, 2 * LANES :], heads[0:1], heads[1:2], columns, segment_ref[0, 0:1, :]
    )
    meeting = right_product(out_map, in_map)
    low_grad_state = to_low(grad_state[...])
    pulled[...] = matmul(in_map, low_grad_state)
    scale = later[:, 3:4]
    coefficient = later[:, 4:5]
    grad_meeting = jnp.zeros((BLOCK, BLOCK), jnp.float32)
    for pair in range(pairs):
        lanes = slice(pair * LANES, (pair + 1) * LANES)
        z_lanes, x_lanes = zx_lanes(pair, per_block)
        tail = jnp.where(first_chunk, 0.0, zx_tail_ref[:, x_lanes])
        block = zx_ref[:, x_lanes]
        taps = taps_ref[:, lanes]
        pre = filtered(tail, block, taps, columns)
        opened = sigmoid(pre)
        value = pre * opened
        slope = opened + value * (1.0 - opened)
        gate_in = zx_ref[:, z_lanes]
        gate_open = sigmoid(gate_in)
        gate = gate_in * gate_open
        skip = channels_ref[0:1, lanes]
        gain = channels_ref[1:2, lanes]
        y = y_ref[:, lanes]
        whole = y + skip * value
        gated = whole * gate
        grad_mixed = grad_ref[:, lanes]
        grad_gated = scale * (grad_mixed * gain) - coefficient * gated
        grad_channels_ref[8:16, lanes] += folded_rows(grad_mixed * gated * scale)
        grad_y = grad_gated * gate
        grad_zx_ref[:, z_lanes] = to_low(
            grad_gated * whole * (gate_open + gate * (1.0 - gate_open))
        )
        grad_channels_ref[0:8, lanes] += folded_rows(grad_y * value)
        low_grad_y = to_low(grad_y)
        reached[:, lanes] = to_low(grad_y * pair_columns(decay.reach, pair, first_half))
        step_wide = pair_columns(decay.step, pair, first_half)
        scaled = value * step_wide
        low_scaled = to_low(scaled)
        end_wide = pair_columns(decay.to_end, pair, first_half)
        ends[:, lanes] = to_low(scaled * end_wide)
        stacked = stacked_halves(low_grad_y, first_half)
        grad_weights = right_product(stacked, low_scaled)
        parts = []
        for half in range(2):
            factor = decay.factor(2 * pair + half)
            grad_meeting = (
                grad_meeting + factor * grad_weights[half * BLOCK : (half + 1) * BLOCK]
            )
            parts.append(to_low(meeting * factor))
        from_end = pulled[:, lanes] * end_wide
        grad_scaled = left_product(jnp.concatenate(parts, 0), stacked) + from_end
        wide_scaled = low_scaled.astype(jnp.float32)
        balance[:BLOCK, lanes] = low_grad_y.astype(jnp.float32) * y - wide_scaled * grad_scaled
        step_part[:, lanes] = to_low(grad_scaled * value)
        kept = pair_columns(decay.kept, pair, first_half)
        kept_state = grad_state[:, lanes] * kept
        balance[BLOCK : BLOCK + 8, lanes] = folded_rows(wide_scaled * from_end) + folded_rows(
            kept_state * states_ref[:, lanes].astype(jnp.float32)
        )
        grad_state[:, lanes] = kept_state
        grad_pre = (grad_scaled * step_wide + grad_y * skip) * slope
        grad_taps_ref[24:32, lanes] += folded_rows(grad_pre * block)
        grad_x = grad_pre * taps[3:4]
        head = head_x[:, lanes]
        for steps in range(1, 4):
            moved = shifted_down(tail, block, steps)
            grad_taps_ref[24 - 8 * steps : 32 - 8 * steps, lanes] += folded_rows(
                grad_pre * columns[:, steps - 1 : steps] * moved
            )
            grad_x = grad_x + (
                shifted_up(grad_pre, head, steps)
                * later[:, steps - 1 : steps]
                * taps[3 - steps : 4 - steps]
            )
        grad_zx_ref[:, x_lanes] = to_low(grad_x)
        head_x[:, lanes] = grad_pre[:8]

    owner = owner_ref[...]
    grad_total = split_product(balance[:BLOCK, :], owner)
    end_rows = split_product(balance[BLOCK : BLOCK + 8, :], owner)
    end_total = jnp.sum(end_rows, axis=0, keepdims=True)
    rows = lax.broadcasted_iota(jnp.int32, (BLOCK, LANES), 0)
    grad_total = grad_total + jnp.where(rows == BLOCK - 1, end_total, 0.0)
    upper = jnp.where(rows <= lax.broadcasted_iota(jnp.int32, (BLOCK, LANES), 1), 1.0, 0.0)
    grad_decay = exact_product(upper, grad_total)
    grad_step = matmul(step_part[...], owner) + grad_decay * heads[1:2]
    grad_raw = grad_step * decay.steepness
    grad_dt_ref[...] = grad_raw
    grad_heads_ref[0:8, :] += folded_rows(grad_raw)
    grad_heads_ref[8:16, :] += folded_rows(grad_decay * decay.decay)

    low_meeting = to_low(grad_meeting)
    grad_out_map = matmul(low_meeting, in_map) + right_product(reached[...], states_ref[...])
    grad_in_map = left_product(low_meeting, out_map) + right_product(ends[...], low_grad_state)
    grad_state[...] += left_product(out_map, reached[...])
    grad_pre = jnp.concatenate([grad_in_map, grad_out_map], 1) * (
        maps_open + maps * (1.0 - maps_open)
    )
    map_taps = map_taps_ref[...]
    grad_map_taps_ref[24:32, :] += folded_rows(grad_pre * maps_in)
    grad_maps = grad_pre * map_taps[3:4]
    head = head_maps[...]
    for steps in range(1, 4):
        moved = shifted_down(tail_maps, maps_in, steps)
        grad_map_taps_ref[24 - 8 * steps : 32 - 8 * steps, :] += folded_rows(
            grad_pre * columns[:, steps - 1 : steps] * moved
        )
        grad_maps = grad_maps + (
            shifted_up(grad_pre, head, steps)
            * later[:, steps - 1 : steps]
            * map_taps[3 - steps : 4 - steps]
        )
    grad_maps_ref[...] = grad_maps
    head_maps[...] = grad_pre[:8]


def whole_block(*shape):
    return pl.BlockSpec(shape, lambda step: (0,) * len(shape))


def mix_settings(length, channels, work):
    return dict(
        compiler_params=pltpu.CompilerParams(
            dimension_semantics=("arbitrary",), vmem_limit_bytes=48 * 1024 * 1024
        ),
        cost_estimate=pl.CostEstimate(
            flops=work * length * channels * BLOCK,
            bytes_accessed=length * channels * 16,
            transcendentals=length * channels * 4,
        ),
    )


def mix_forward(
    per_block, zx_proj, bcdt, columns, segment_rows, taps, map_taps, heads, channels
):
    length = zx_proj.shape[0]
    width = channels.shape[1]
    chunks = length // BLOCK

    def rows(size):
        return pl.BlockSpec((BLOCK, size), lambda step: (step, 0))

    return pl.pallas_call(
        functools.partial(mix_kernel, per_block),
        grid=(chunks,),
        in_specs=[
            rows(2 * width),
            rows(3 * LANES),
            rows(8),
            pl.BlockSpec((1, 8, BLOCK), lambda step: (step, 0, 0)),
            whole_block(4, width),
            whole_block(4, 2 * LANES),
            whole_block(8, LANES),
            whole_block(8, width),
        ],
        out_specs=[rows(width), rows(width), rows(1), rows(width)],
        out_shape=[
            jax.ShapeDtypeStruct((length, width), jnp.bfloat16),
            jax.ShapeDtypeStruct((length, width), jnp.float32),
            jax.ShapeDtypeStruct((length, 1), jnp.float32),
            jax.ShapeDtypeStruct((chunks * LANES, width), jnp.bfloat16),
        ],
        scratch_shapes=[
            pltpu.VMEM((LANES, width), jnp.float32),
            pltpu.VMEM((8, width), jnp.float32),
            pltpu.VMEM((8, 2 * LANES), jnp.float32),
            pltpu.VMEM((BLOCK, width), jnp.bfloat16),
        ],
        **mix_settings(length, width, 8),
    )(zx_proj, bcdt, columns, segment_rows, taps, map_taps, heads, channels)


def mix_backward(
    per_block,
    grad_mixed,
    zx_proj,
    bcdt,
    y,
    states,
    columns,
    later,
    segment_rows,
    taps,
    map_taps,
    heads,
    channels,
    owner,
):
    length, width = grad_mixed.shape
    chunks = length // BLOCK
    eighths = BLOCK // 8

    def rows(size):
        return pl.BlockSpec((BLOCK, size), lambda step: (chunks - 1 - step, 0))

    def before(size):
        return pl.BlockSpec(
            (8, size), lambda step: (jnp.maximum((chunks - 1 - step) * eighths - 1, 0), 0)
        )

    low = jnp.bfloat16
    wide = jnp.float32
    return pl.pallas_call(
        functools.partial(mix_back_kernel, per_block),
        grid=(chunks,),
        in_specs=[
            rows(width),
            rows(2 * width),
            before(2 * width),
            rows(3 * LANES),
            before(3 * LANES),
            rows(width),
            rows(width),
            rows(8),
            rows(8),
            pl.BlockSpec((1, 8, BLOCK), lambda step: (chunks - 1 - step, 0, 0)),
            whole_block(4, width),
            whole_block(4, 2 * LANES),
            whole_block(8, LANES),
            whole_block(8, width),
            whole_block(width, LANES),
        ],
        out_specs=[
            rows(2 * width),
            rows(2 * LANES),
            rows(LANES),
            whole_block(32, width),
            whole_block(32, 2 * LANES),
            whole_block(16, LANES),
            whole_block(16, width),
        ],
        out_shape=[
            jax.ShapeDtypeStruct((length, 2 * width), low),
            jax.ShapeDtypeStruct((length, 2 * LANES), wide),
            jax.ShapeDtypeStruct((length, LANES), wide),
            jax.ShapeDtypeStruct((32, width), wide),
            jax.ShapeDtypeStruct((32, 2 * LANES), wide),
            jax.ShapeDtypeStruct((16, LANES), wide),
            jax.ShapeDtypeStruct((16, width), wide),
        ],
        scratch_shapes=[
            pltpu.VMEM((LANES, width), wide),
            pltpu.VMEM((8, width), wide),
            pltpu.VMEM((8, 2 * LANES), wide),
            pltpu.VMEM((BLOCK, width), low),
            pltpu.VMEM((BLOCK, width), low),
            pltpu.VMEM((BLOCK, width), wide),
            pltpu.VMEM((BLOCK + 8, width), wide),
            pltpu.VMEM((BLOCK, width), low),
        ],
        **mix_settings(length, width, 24),
    )(
        grad_mixed,
        zx_proj,
        zx_proj,
        bcdt,
        bcdt,
        y,
        states,
        columns,
        later,
        segment_rows,
        taps,
        map_taps,
        heads,
        channels,
        owner,
    )


def item_columns(segment):
    length = segment.shape[0]
    back = []
    ahead = []
    for steps in range(1, 4):
        same = segment[steps:] == segment[:-steps]
        none = jnp.zeros((steps,), jnp.bool_)
        back.append(jnp.concatenate([none, same]))
        ahead.append(jnp.concatenate([same, none]))
    blocks = segment.reshape(-1, BLOCK)
    last = blocks[:, BLOCK - 1]
    before = jnp.concatenate([jnp.full((1,), -1, segment.dtype), last[:-1]])
    carried = (blocks == before[:, None]).reshape(-1)
    ending = (blocks == last[:, None]).reshape(-1)
    wide = jnp.float32
    nothing = jnp.zeros((length,), wide)
    columns = jnp.stack(
        [b.astype(wide) for b in back]
        + [segment.astype(wide), carried.astype(wide), ending.astype(wide), nothing, nothing],
        1,
    )
    rows = jnp.broadcast_to(blocks.astype(wide)[:, None, :], (blocks.shape[0], 8, BLOCK))
    return columns, [a.astype(wide) for a in ahead], rows


SLOTS = 384


def smooth_kernel(probs_ref, down_ref, encoded_ref, confidence_ref, rank_ref, out_ref, smooth_ref, high, rest):
    count = down_ref.shape[0]

    @pl.when(pl.program_id(0) == 0)
    def _():
        high[count:, :] = jnp.zeros((SLOTS - count, high.shape[1]), jnp.bfloat16)
        rest[count:, :] = jnp.zeros((SLOTS - count, high.shape[1]), jnp.bfloat16)

        def tile(index, previous):
            start = pl.multiple_of(index * 8, 8)
            rows = down_ref[pl.ds(start, 8), :]
            done = []
            for r in range(8):
                prob = probs_ref[start + r]
                previous = prob * rows[r : r + 1] + (1.0 - prob) * previous
                done.append(previous)
            smooth_ref[pl.ds(start, 8), :] = jnp.concatenate(done, 0)
            return previous

        lax.fori_loop(0, count // 8, tile, jnp.zeros((1, down_ref.shape[1]), jnp.float32))
        smooth = smooth_ref[...]
        low = to_low(smooth)
        high[:count, :] = low
        rest[:count, :] = to_low(smooth - low.astype(jnp.float32))

    slots = lax.broadcasted_iota(jnp.int32, (BLOCK, SLOTS), 1)
    chosen = jnp.where(slots == rank_ref[...], 1.0, 0.0).astype(jnp.bfloat16)
    spread = matmul(chosen, high[...]) + matmul(chosen, rest[...])
    out_ref[...] = encoded_ref[...] + confidence_ref[...] * spread


def smooth_back_kernel(
    probs_ref,
    grad_ref,
    confidence_ref,
    rank_ref,
    smooth_ref,
    down_ref,
    grad_down_ref,
    grad_confidence_ref,
    grad_probs_ref,
    total,
    low,
):
    count = down_ref.shape[0]
    width = down_ref.shape[1]
    step = pl.program_id(0)

    @pl.when(step == 0)
    def _():
        total[...] = jnp.zeros_like(total)
        low[:count, :] = to_low(smooth_ref[...])
        low[count:, :] = jnp.zeros((SLOTS - count, width), jnp.bfloat16)

    slots = lax.broadcasted_iota(jnp.int32, (BLOCK, SLOTS), 1)
    chosen = jnp.where(slots == rank_ref[...], 1.0, 0.0).astype(jnp.bfloat16)
    gradient = grad_ref[...]
    total[...] += left_product(chosen, to_low(confidence_ref[...] * gradient))
    grad_confidence_ref[...] = jnp.sum(gradient * matmul(chosen, low[...]), axis=1, keepdims=True)

    @pl.when(step == pl.num_programs(0) - 1)
    def _():
        tiles = count // 16

        def tile(index, later):
            index = tiles - 1 - index
            start = pl.multiple_of(index * 16, 16)
            rows = total[pl.ds(start, 16), :]
            done = [None] * 16
            kept = [None] * 16
            for r in range(15, -1, -1):
                later = rows[r : r + 1] + (1.0 - probs_ref[start + r + 1]) * later
                kept[r] = later
                done[r] = probs_ref[start + r] * later
            grad_down_ref[pl.ds(start, 16), :] = to_low(jnp.concatenate(done, 0))
            total[pl.ds(start, 16), :] = jnp.concatenate(kept, 0)
            return later

        lax.fori_loop(0, tiles, tile, jnp.zeros((1, width), jnp.float32))
        smooth = smooth_ref[...]
        places = lax.broadcasted_iota(jnp.int32, (count, 1), 0)
        before = jnp.where(places == 0, 0.0, pltpu.roll(smooth, 1, 0))
        grad_probs_ref[...] = jnp.sum(
            total[:count, :] * (down_ref[...] - before), axis=1, keepdims=True
        )


def byte_rows(size):
    return pl.BlockSpec((BLOCK, size), lambda step: (step, 0))


def kernel_settings(flops, traffic):
    return dict(
        compiler_params=pltpu.CompilerParams(
            dimension_semantics=("arbitrary",), vmem_limit_bytes=48 * 1024 * 1024
        ),
        cost_estimate=pl.CostEstimate(flops=flops, bytes_accessed=traffic, transcendentals=0),
    )


def smooth_forward(probs, down_rows, encoded, confidence, rank):
    length, width = encoded.shape
    count = down_rows.shape[0]
    wide = jnp.float32
    return pl.pallas_call(
        smooth_kernel,
        grid=(length // BLOCK,),
        in_specs=[
            pl.BlockSpec(memory_space=pltpu.SMEM),
            whole_block(count, width),
            byte_rows(width),
            byte_rows(1),
            byte_rows(1),
        ],
        out_specs=[byte_rows(width), whole_block(count, width)],
        out_shape=[
            jax.ShapeDtypeStruct((length, width), wide),
            jax.ShapeDtypeStruct((count, width), wide),
        ],
        scratch_shapes=[pltpu.VMEM((SLOTS, width), jnp.bfloat16)] * 2,
        **kernel_settings(4 * length * SLOTS * width, length * width * 8),
    )(probs, down_rows, encoded, confidence, rank)


def smooth_backward(probs, gradient, confidence, rank, smooth, down_rows):
    length, width = gradient.shape
    count = down_rows.shape[0]
    wide = jnp.float32
    return pl.pallas_call(
        smooth_back_kernel,
        grid=(length // BLOCK,),
        in_specs=[
            pl.BlockSpec(memory_space=pltpu.SMEM),
            byte_rows(width),
            byte_rows(1),
            byte_rows(1),
            whole_block(count, width),
            whole_block(count, width),
        ],
        out_specs=[whole_block(count, width), byte_rows(1), whole_block(count, 1)],
        out_shape=[
            jax.ShapeDtypeStruct((count, width), jnp.bfloat16),
            jax.ShapeDtypeStruct((length, 1), wide),
            jax.ShapeDtypeStruct((count, 1), wide),
        ],
        scratch_shapes=[pltpu.VMEM((SLOTS, width), wide), pltpu.VMEM((SLOTS, width), jnp.bfloat16)],
        **kernel_settings(4 * length * SLOTS * width, length * width * 4),
    )(probs, gradient, confidence, rank, smooth, down_rows)


def turned(values, cosines, sines):
    lane = lax.broadcasted_iota(jnp.int32, values.shape, 1) % HEAD_SIZE
    swapped = jnp.where(
        lane < HEAD_SIZE // 2,
        pltpu.roll(values, LANES - HEAD_SIZE // 2, 1),
        pltpu.roll(values, HEAD_SIZE // 2, 1),
    )
    return values * cosines + swapped * sines


def attend_mask(items_ref, items_row_ref):
    size = items_ref.shape[0]
    rows = lax.broadcasted_iota(jnp.int32, (size, size), 0)
    cols = lax.broadcasted_iota(jnp.int32, (size, size), 1)
    return (rows >= cols) & (items_ref[...] == items_row_ref[0:1, :])


def softmaxed(queries, keys, visible):
    scores = right_product(queries, keys) * HEAD_SIZE ** (-0.5)
    scores = jnp.where(visible, scores, -1e30)
    weights = jnp.exp(scores - jnp.max(scores, axis=1, keepdims=True))
    return weights / jnp.sum(weights, axis=1, keepdims=True)


def half_lanes(values, half):
    lane = lax.broadcasted_iota(jnp.int32, (1, LANES), 1) // HEAD_SIZE
    return jnp.where(lane == half, values, jnp.zeros_like(values))


HEADS_PER_BLOCK = 3
BLOCK_WIDTH = 2 * LANES


def unpacked(block, cosines, sines):
    width = HEADS_PER_BLOCK * HEAD_SIZE
    size = block.shape[1]
    queries = block[:, :BLOCK_WIDTH]
    keys = pltpu.roll(block, size - width, 1)[:, :BLOCK_WIDTH]
    values = pltpu.roll(block, size - 2 * width, 1)[:, :BLOCK_WIDTH]
    tiles = []
    for tile in range(2):
        lanes = slice(tile * LANES, (tile + 1) * LANES)
        tiles.append(
            (
                to_low(turned(queries[:, lanes], cosines, sines)),
                to_low(turned(keys[:, lanes], cosines, sines)),
                to_low(values[:, lanes]),
            )
        )
    return tiles


def attend_kernel(qkv_ref, cos_ref, sin_ref, items_ref, items_row_ref, out_ref):
    visible = attend_mask(items_ref, items_row_ref)
    tiles = unpacked(qkv_ref[...], cos_ref[...], sin_ref[...])
    for tile, (queries, keys, values) in enumerate(tiles):
        mixed = 0.0
        for half in range(2 - tile):
            weights = softmaxed(half_lanes(queries, half), keys, visible)
            mixed = mixed + matmul(to_low(weights), half_lanes(values, half))
        out_ref[:, tile * LANES : (tile + 1) * LANES] = to_low(mixed)


def attend_back_kernel(
    qkv_ref, grad_ref, cos_ref, sin_ref, items_ref, items_row_ref, grad_qkv_ref
):
    visible = attend_mask(items_ref, items_row_ref)
    cosines = cos_ref[...]
    sines = sin_ref[...]
    scale = HEAD_SIZE ** (-0.5)
    tiles = unpacked(qkv_ref[...], cosines, sines)
    grads = ([], [], [])
    for tile, (queries, keys, values) in enumerate(tiles):
        gradient = to_low(grad_ref[:, tile * LANES : (tile + 1) * LANES])
        grad_q = 0.0
        grad_k = 0.0
        grad_v = 0.0
        for half in range(2 - tile):
            own_queries = half_lanes(queries, half)
            own_grad = half_lanes(gradient, half)
            weights = softmaxed(own_queries, keys, visible)
            grad_weights = right_product(own_grad, values)
            grad_v = grad_v + left_product(to_low(weights), own_grad)
            inner = jnp.sum(grad_weights * weights, axis=1, keepdims=True)
            grad_scores = to_low(jnp.where(visible, weights * (grad_weights - inner), 0.0))
            grad_q = grad_q + matmul(grad_scores, half_lanes(keys, half))
            grad_k = grad_k + left_product(grad_scores, own_queries)
        grads[0].append(turned(grad_q * scale, cosines, -sines))
        grads[1].append(turned(grad_k * scale, cosines, -sines))
        grads[2].append(grad_v)
    size = qkv_ref.shape[1]
    width = HEADS_PER_BLOCK * HEAD_SIZE
    filling = jnp.zeros((qkv_ref.shape[0], size - BLOCK_WIDTH), jnp.float32)
    packed = 0.0
    for kind, both in enumerate(grads):
        wide = jnp.concatenate(both + [filling], 1)
        packed = packed + (pltpu.roll(wide, kind * width, 1) if kind else wide)
    grad_qkv_ref[...] = to_low(packed)


def turn_tables(count):
    half = HEAD_SIZE // 2
    lane = jnp.arange(LANES) % HEAD_SIZE
    frequency = 10000.0 ** (-(lane % half).astype(jnp.float32) * (2.0 / HEAD_SIZE))
    angles = jnp.arange(count, dtype=jnp.float32)[:, None] * frequency[None, :]
    return jnp.cos(angles), jnp.where(lane < half, -1.0, 1.0)[None, :] * jnp.sin(angles)


def attend(qkv, gradient, tables, group_items, depths):
    count, width = qkv.shape
    size = width // depths

    def tiles(columns):
        return pl.BlockSpec((count, columns), lambda step: (0, step))

    backward = gradient is not None
    items = group_items.astype(jnp.int32)
    out = size if backward else BLOCK_WIDTH
    return pl.pallas_call(
        attend_back_kernel if backward else attend_kernel,
        grid=(depths,),
        in_specs=[tiles(size)]
        + [tiles(BLOCK_WIDTH)] * backward
        + [whole_block(count, LANES)] * 2
        + [whole_block(count, 1), whole_block(8, count)],
        out_specs=tiles(out),
        out_shape=jax.ShapeDtypeStruct((count, depths * out), jnp.bfloat16),
        **kernel_settings(8 * count * count * width, count * width * 16),
    )(
        qkv,
        *([gradient] if backward else []),
        *tables,
        items[:, None],
        jnp.broadcast_to(items[None, :], (8, count)),
    )


def active_kernel(pair_ref, out_ref):
    size = out_ref.shape[1]
    gate = pair_ref[:, :size]
    out_ref[...] = to_low(gate * sigmoid(gate) * pair_ref[:, size:])


def active_back_kernel(pair_ref, grad_ref, out_ref):
    size = grad_ref.shape[1]
    gate = pair_ref[:, :size]
    upper = pair_ref[:, size:]
    opened = sigmoid(gate)
    gradient = grad_ref[...]
    out_ref[:, :size] = to_low(
        gradient * upper * (opened + gate * opened * (1.0 - opened))
    )
    out_ref[:, size:] = to_low(gradient * gate * opened)


def activate(pairs, gradient, depths):
    count, width = pairs.shape
    size = width // depths // 2

    def tiles(columns):
        return pl.BlockSpec((count, columns), lambda step: (0, step))

    backward = gradient is not None
    out = 2 * size if backward else size
    return pl.pallas_call(
        active_back_kernel if backward else active_kernel,
        grid=(depths,),
        in_specs=[tiles(2 * size)] + [tiles(size)] * backward,
        out_specs=tiles(out),
        out_shape=jax.ShapeDtypeStruct((count, depths * out), jnp.bfloat16),
        **kernel_settings(count * width * 8, count * width * 8),
    )(pairs, *([gradient] if backward else []))


def dots_kernel(depths, qk_ref, out_ref, tail):
    size = qk_ref.shape[1] // depths // 2

    @pl.when(pl.program_id(0) == 0)
    def _():
        tail[...] = jnp.zeros_like(tail)

    sums = [0.0, 0.0, 0.0]
    for k in range(depths):
        queries = qk_ref[:, 2 * k * size : (2 * k + 1) * size]
        keys = qk_ref[:, (2 * k + 1) * size : (2 * k + 2) * size]
        lanes = slice(k * size, (k + 1) * size)
        previous = shifted_down(tail[:, lanes], keys, 1)
        tail[:, lanes] = keys[BLOCK - 8 :]
        sums[0] = sums[0] + queries * previous
        sums[1] = sums[1] + queries * queries
        sums[2] = sums[2] + previous * previous
    for kind in range(3):
        out_ref[:, kind : kind + 1] = jnp.sum(sums[kind], axis=1, keepdims=True)
    out_ref[:, 3:] = jnp.zeros((BLOCK, 5), jnp.float32)


def dots_back_kernel(depths, qk_ref, tail_ref, grad_ref, later_ref, out_ref, head):
    size = qk_ref.shape[1] // depths // 2
    step = pl.program_id(0)
    first_block = step == pl.num_programs(0) - 1

    @pl.when(step == 0)
    def _():
        head[...] = jnp.zeros_like(head)

    for k in range(depths):
        query_lanes = slice(2 * k * size, (2 * k + 1) * size)
        key_lanes = slice((2 * k + 1) * size, (2 * k + 2) * size)
        lanes = slice(k * size, (k + 1) * size)
        queries = qk_ref[:, query_lanes]
        keys = qk_ref[:, key_lanes]
        tail = jnp.where(first_block, 0.0, tail_ref[:, key_lanes])
        previous = shifted_down(tail, keys, 1)
        following = shifted_up(queries, head[:, lanes], 1)
        head[:, lanes] = queries[:8]
        out_ref[:, query_lanes] = to_low(
            grad_ref[:, 0:1] * previous + 2.0 * grad_ref[:, 1:2] * queries
        )
        out_ref[:, key_lanes] = to_low(
            later_ref[:, 0:1] * following + 2.0 * later_ref[:, 2:3] * keys
        )


def pair_dots(qk, depths):
    length, width = qk.shape
    return pl.pallas_call(
        functools.partial(dots_kernel, depths),
        grid=(length // BLOCK,),
        in_specs=[byte_rows(width)],
        out_specs=byte_rows(8),
        out_shape=jax.ShapeDtypeStruct((length, 8), jnp.float32),
        scratch_shapes=[pltpu.VMEM((8, width // 2), jnp.float32)],
        **kernel_settings(length * width * 4, length * width * 4),
    )(qk)


def pair_dots_back(qk, gradient, depths):
    length, width = qk.shape
    chunks = length // BLOCK
    eighths = BLOCK // 8
    later = jnp.concatenate([gradient[1:], jnp.zeros((1, 8), jnp.float32)], 0)

    def rows(size):
        return pl.BlockSpec((BLOCK, size), lambda step: (chunks - 1 - step, 0))

    return pl.pallas_call(
        functools.partial(dots_back_kernel, depths),
        grid=(chunks,),
        in_specs=[
            rows(width),
            pl.BlockSpec(
                (8, width), lambda step: (jnp.maximum((chunks - 1 - step) * eighths - 1, 0), 0)
            ),
            rows(8),
            rows(8),
        ],
        out_specs=rows(width),
        out_shape=jax.ShapeDtypeStruct((length, width), jnp.bfloat16),
        scratch_shapes=[pltpu.VMEM((8, width // 2), jnp.float32)],
        **kernel_settings(length * width * 4, length * width * 8),
    )(qk, qk, gradient, later)


def core_swap(values):
    size = lax.axis_size("dp")
    return lax.ppermute(values, "dp", [(d, d ^ 1) for d in range(size)])


def chip_swap(values, bit):
    size = lax.axis_size("dp")
    return lax.ppermute(values, "dp", [(d, d ^ (bit * 2)) for d in range(size)])


def depth_swap(values, offset):
    if offset == 0:
        return values
    size = lax.axis_size("mp")
    return lax.ppermute(values, "mp", [(d, d ^ offset) for d in range(size)])


class Place:
    def __init__(self):
        dp_index = lax.axis_index("dp")
        self.core = dp_index % 2
        self.chip = dp_index // 2
        self.depth = lax.axis_index("mp")
        self.chips = lax.axis_size("dp") // 2
        self.depths = lax.axis_size("mp")
        bits = []
        while 2 ** len(bits) < self.chips:
            bits.append(2 ** len(bits))
        self.bits = bits


def both_cores(place, own, other, axis):
    first = place.core == 0
    return jnp.concatenate([jnp.where(first, own, other), jnp.where(first, other, own)], axis)


def pick(values, index, size, axis):
    return lax.dynamic_slice_in_dim(values, index * size, size, axis)


def reorder(values, count, shift, axis=-1):
    axis = axis % values.ndim
    size = values.shape[axis] // count
    return jnp.concatenate([pick(values, r ^ shift, size, axis) for r in range(count)], axis)


def relative_to_chip(place, values):
    if place.chips == place.depths:
        return reorder(values, place.chips, place.chip ^ place.depth)
    return reorder(reorder(values, place.depths, place.depth), place.chips, place.chip)


def chip_to_relative(place, values):
    if place.chips == place.depths:
        return reorder(values, place.chips, place.chip ^ place.depth)
    return reorder(reorder(values, place.chips, place.chip), place.depths, place.depth)


def depth_to_chip(place, values):
    return reorder(values, place.chips, place.chip)


def split_columns(place, shards):
    axis = shards[0].ndim - 1

    def columns(core):
        return jnp.concatenate([pick(s, core, s.shape[-1] // 2, axis) for s in shards], axis)

    other = core_swap(columns(1 - place.core))
    return both_cores(place, columns(place.core), other, axis - 1)


def split_rows(place, shard):
    half = shard.shape[-2] // 2
    own = pick(shard, place.core, half, shard.ndim - 2)
    other = core_swap(pick(shard, 1 - place.core, half, shard.ndim - 2))
    return both_cores(place, own, other, shard.ndim - 1)


def join_columns(place, block):
    half = block.shape[-2] // 2
    own = pick(block, place.core, half, block.ndim - 2)
    other = core_swap(pick(block, 1 - place.core, half, block.ndim - 2))
    return both_cores(place, own, other, block.ndim - 1)


def join_rows(place, block):
    half = block.shape[-1] // 2
    own = pick(block, place.core, half, block.ndim - 1)
    other = core_swap(pick(block, 1 - place.core, half, block.ndim - 1))
    return both_cores(place, own, other, block.ndim - 2)


def padded_rows(rows):
    return -(-rows // LANES) * LANES


def assemble_kernel(places, items, size, *refs):
    sources = refs[: len(places)]
    outs = refs[len(places) :]
    rows = sources[0].shape[1]
    for (r, first, count), ref in zip(places, sources):

        @pl.when(pl.program_id(0) == r)
        def _(first=first, count=count, ref=ref):
            offset = 0
            for (kind, width), out_ref in zip(items, outs):
                if kind == "folded":
                    half = rows // 2
                    for k in range(count):
                        j = (first + k) * (width + width // 2)
                        out_ref[:, j : j + width] = ref[k, :half, offset : offset + width]
                        out_ref[:, j + width : j + width + width // 2] = ref[
                            k, half:, offset : offset + width // 2
                        ]
                    offset += width
                    continue
                for k in range(count):
                    i = (first + k) * size if kind == "rows" else 0
                    j = (first + k) * width if kind == "columns" else 0
                    out_ref[i : i + rows, j : j + width] = ref[k, :, offset : offset + width]
                    if size > rows:
                        out_ref[i + rows : i + size, j : j + width] = jnp.zeros(
                            (size - rows, width), jnp.bfloat16
                        )
                offset += width


def assemble(place, pieces, items, filled):
    chips, depths = place.chips, place.depths
    rows = pieces[0][2].shape[1]
    size = padded_rows(rows) if filled else rows
    if any(width % LANES for _, width in items):
        matrices = []
        offset = 0
        for kind, width in items:
            arrays = [
                jnp.pad(a[:, :, offset : offset + width], ((0, 0), (0, size - rows), (0, 0)))
                for _, _, a in pieces
            ]
            if kind == "rows":
                arrays = [a.reshape(depths * size, width) for a in arrays]
                matrices.append(jnp.concatenate(arrays, 1))
            else:
                arrays = [jnp.concatenate([a[k] for k in range(depths)], 1) for a in arrays]
                matrices.append(jnp.concatenate(arrays, 0))
            offset += width
        return matrices
    shapes = []
    blocks = []
    for kind, width in items:
        if kind == "rows":
            shapes.append((depths * size, chips * width))
            blocks.append(pl.BlockSpec((depths * size, width), lambda i: (0, i)))
        elif kind == "folded":
            whole = depths * (width + width // 2)
            shapes.append((chips * size // 2, whole))
            blocks.append(pl.BlockSpec((size // 2, whole), lambda i: (i, 0)))
        else:
            shapes.append((chips * size, depths * width))
            blocks.append(pl.BlockSpec((size, depths * width), lambda i: (i, 0)))
    places = [(r, first, array.shape[0]) for r, first, array in pieces]
    return pl.pallas_call(
        functools.partial(assemble_kernel, places, items, size),
        grid=(chips,),
        in_specs=[whole_block(*array.shape) for _, _, array in pieces],
        out_specs=blocks,
        out_shape=[jax.ShapeDtypeStruct(shape, jnp.bfloat16) for shape in shapes],
        **kernel_settings(0, sum(4 * a * b for a, b in shapes)),
    )(*[array for _, _, array in pieces])


def held_for(values, earlier):
    if not earlier:
        return values
    return lax.optimization_barrier((values, *earlier))[0]


class Gather:
    def __init__(self, place):
        self.place = place
        self.near = []
        self.far = []

    def hold(self, values, waits=()):
        return held_for(values, sum(self.near[-1:] + self.far[-2:-1], list(waits)))

    def pieces(self, shard, waits):
        place = self.place
        shard = self.hold(shard, waits)
        stack = lax.all_gather(shard, "mp", axis=0)
        if place.chips == 4:
            half = place.depths // 2
            along = [chip_swap(stack, bit) for bit in (1, 2)]
            across = [chip_swap(along[0][:half], 2), chip_swap(along[1][half:], 1)]
            self.near.append([stack])
            self.far.append(along)
            return [
                (0, 0, stack),
                (1, 0, along[0]),
                (2, 0, along[1]),
                (3, 0, across[0]),
                (3, half, across[1]),
            ]
        pieces = {0: stack}
        for bit in place.bits:
            for r, piece in list(pieces.items()):
                pieces[r ^ bit] = chip_swap(piece, bit)
        self.near.append([stack])
        return [(r, 0, pieces[r]) for r in range(place.chips)]

    def matrices(self, shards, waits=(), filled=False):
        rows = shards[0][1].shape[0]
        folded = [kind == "folded" for kind, _ in shards]
        for index, (kind, shard) in enumerate(shards):
            if kind == "folded":
                third = shard.shape[1] // 3
                if 2 * shard.shape[0] == rows and third % LANES == 0:
                    last = jnp.pad(shard[:, 2 * third :], ((0, 0), (0, third)))
                    shard = jnp.concatenate([shard[:, : 2 * third], last], 0)
                else:
                    kind = "columns"
                shards = shards[:index] + [(kind, shard)] + shards[index + 1 :]
        if len({shard.shape[0] for _, shard in shards}) > 1:
            return [
                self.matrices([item], waits, filled or flag)[0]
                for item, flag in zip(shards, folded)
            ]
        items = [(kind, shard.shape[1]) for kind, shard in shards]
        packed = jnp.concatenate([shard for _, shard in shards], 1)
        return assemble(self.place, self.pieces(packed, waits), items, filled)


def gather_chips(place, shard, bits):
    pieces = {0: shard}
    for bit in bits:
        for r, piece in list(pieces.items()):
            pieces[r ^ bit] = chip_swap(piece, bit)
    return jnp.concatenate([pieces[r] for r in range(place.chips)], -2)


def send_order(place, bits):
    order = [0]
    for bit in reversed(bits):
        order = order + [r ^ bit for r in order]
    return order


def chosen(step, values):
    result = 0
    for index, value in enumerate(values):
        result = result + jnp.where(step == index, value, 0)
    return result


def products_kernel(kinds, rows, *refs):
    out_ref = refs[-1]
    offset = 0
    for index, kind in enumerate(kinds):
        chip_side = refs[2 * index][...]
        depth_side = refs[2 * index + 1][...]
        if kind == "columns":
            block = left_product(chip_side, depth_side)
        else:
            block = left_product(depth_side, chip_side)
        width = block.shape[1]
        out_ref[0, :, offset : offset + width] = to_low(block[:rows])
        offset += width


class Scatter:
    def __init__(self, place):
        self.place = place
        self.near = []
        self.far = []

    def blocks(self, items, rows, chips, depths):
        place = self.place
        steps = [(r, k) for r in chips for k in depths]
        sizes = []
        aligned = True
        for kind, chip_side, depth_side in items:
            a = chip_side.shape[1] // place.chips
            b = depth_side.shape[1] // place.depths
            sizes.append((a, b, b if kind == "columns" else a))
            aligned = aligned and a % LANES == 0 and b % LANES == 0
        if not aligned:
            parts = []
            for (kind, chip_side, depth_side), (a, b, _) in zip(items, sizes):
                if kind == "columns":
                    whole = left_product(chip_side, depth_side)
                    whole = whole.reshape(place.chips, a, place.depths, b).transpose(0, 2, 1, 3)
                else:
                    whole = left_product(depth_side, chip_side)
                    whole = whole.reshape(place.depths, b, place.chips, a).transpose(2, 0, 1, 3)
                parts.append(to_low(whole[:, :, :rows]))
            whole = jnp.concatenate(parts, 3)
            return jnp.stack([jnp.stack([whole[r, k] for k in depths]) for r in chips])
        width = sum(size[2] for size in sizes)
        specs = []
        for (kind, chip_side, depth_side), (a, b, _) in zip(items, sizes):
            count = chip_side.shape[0]
            specs.append(
                pl.BlockSpec((count, a), lambda s: (0, chosen(s, [r for r, _ in steps])))
            )
            specs.append(
                pl.BlockSpec((count, b), lambda s: (0, chosen(s, [k for _, k in steps])))
            )
        count = items[0][1].shape[0]
        out = pl.pallas_call(
            functools.partial(products_kernel, [kind for kind, _, _ in items], rows),
            grid=(len(steps),),
            in_specs=specs,
            out_specs=pl.BlockSpec((1, rows, width), lambda s: (s, 0, 0)),
            out_shape=jax.ShapeDtypeStruct((len(steps), rows, width), jnp.bfloat16),
            **kernel_settings(
                2 * len(steps) * count * rows * width, len(steps) * (rows + count) * width * 2
            ),
        )(*[side for _, *sides in items for side in sides])
        return out.reshape(len(chips), len(depths), rows, width)

    def own(self, items, all_rows, waits=(), reduced=False):
        if len(set(all_rows)) > 1:
            parts = [self.own([item], [n], waits, reduced)[0] for item, n in zip(items, all_rows)]
            return parts
        place = self.place
        rows = all_rows[0]
        kind, chip_side, depth_side = items[0]
        chip_side = held_for(chip_side, sum(self.near[-2:-1] + self.far[-3:-2], list(waits)))
        items = [(kind, chip_side, depth_side)] + list(items[1:])
        half = place.depths // 2
        orders = (place.bits[::-1], place.bits)
        depth_sets = (range(half), range(half, place.depths))
        middle = place.chips // 2
        order_lists = [send_order(place, bits) for bits in orders]
        sents = [
            self.blocks(items, rows, order[middle:], ks)
            for order, ks in zip(order_lists, depth_sets)
        ]
        kepts = [
            self.blocks(items, rows, order[:middle], ks)
            for order, ks in zip(order_lists, depth_sets)
        ]
        got = []
        for step in range(len(place.bits)):
            got = [chip_swap(sent, bits[step]) for sent, bits in zip(sents, orders)]
            sums = [a.astype(jnp.float32) + b.astype(jnp.float32) for a, b in zip(kepts, got)]
            middle = middle // 2
            sents = [to_low(total[middle:]) for total in sums]
            kepts = [total[:middle] for total in sums] if middle else sums
            if step == 0:
                self.near.append(sents)
        by_depth = jnp.concatenate([total[0] for total in kepts], 0)
        if reduced:
            going = to_low(by_depth)
            self.far.append([going])
            total = lax.psum_scatter(going, "mp", scatter_dimension=0).astype(jnp.float32)
        else:
            blocks = [
                lax.dynamic_index_in_dim(by_depth, place.depth ^ k, 0, keepdims=False)
                for k in range(place.depths)
            ]
            going = [to_low(block) for block in blocks[1:]]
            arrived = [depth_swap(block, k + 1) for k, block in enumerate(going)]
            self.far.append(going)
            total = blocks[0]
            for values in arrived:
                total = total + values.astype(jnp.float32)
        parts = []
        offset = 0
        for kind, chip_side, depth_side in items:
            side = (depth_side, place.depths) if kind == "columns" else (chip_side, place.chips)
            width = side[0].shape[1] // side[1]
            parts.append(total[:, offset : offset + width])
            offset += width
        return parts


def scatter_rest(place, kept, sent, bits, chip_axis, over_depth=True):
    for step, bit in enumerate(bits):
        if step > 0:
            half = kept.shape[chip_axis] // 2
            sent = to_low(lax.slice_in_dim(kept, half, 2 * half, axis=chip_axis))
            kept = lax.slice_in_dim(kept, 0, half, axis=chip_axis)
        kept = kept + chip_swap(sent, bit).astype(jnp.float32)
    if not over_depth:
        return kept
    axis = 1 - chip_axis
    size = kept.shape[axis] // place.depths
    total = lax.slice_in_dim(kept, 0, size, axis=axis)
    for k in range(1, place.depths):
        block = to_low(lax.slice_in_dim(kept, k * size, (k + 1) * size, axis=axis))
        total = total + depth_swap(block, k).astype(jnp.float32)
    return total


def core_sum(partial):
    return partial + core_swap(to_low(partial)).astype(jnp.float32)


def core_sum_exact(partial):
    return partial + core_swap(partial)


def parity_part(place, values):
    size = values.shape[1] // (2 * place.chips)
    split = values.reshape(values.shape[0], place.chips, 2, size)
    own = lax.dynamic_index_in_dim(split, place.core, 2, keepdims=False)
    own = jnp.pad(own, ((0, 0), (0, 0), (0, padded_rows(size) - size)))
    return own.reshape(values.shape[0], -1)


def parity_join(place, own, size):
    rows = own.shape[0]
    own = own.reshape(rows, place.chips, -1)[:, :, :size]
    other = core_swap(own)
    return both_cores(place, own[:, :, None], other[:, :, None], 2).reshape(rows, -1)


def other_rows(place, values):
    micro, length, width = values.shape
    halves = values.reshape(micro, 2, length // 2, width)
    return core_swap(lax.dynamic_index_in_dim(halves, 1 - place.core, 1, keepdims=True))


def own_sequence(place, values, other):
    micro, length, width = values.shape
    halves = values.reshape(micro, 2, length // 2, width)
    own = lax.dynamic_index_in_dim(halves, place.core, 1, keepdims=True)
    half = both_cores(place, own, other, 1).reshape(micro * 2, length // 2, width)
    blocks = [
        depth_swap(lax.dynamic_index_in_dim(half, place.depth ^ k, 0, keepdims=False), k)
        for k in range(place.depths)
    ]
    rows = relative_to_chip(place, jnp.concatenate(blocks, 1))
    return both_cores(place, rows, core_swap(rows), 0)


def back_to_all(place, values, micro):
    length = values.shape[0]
    rows = chip_to_relative(place, pick(values, place.core, length // 2, 0))
    width = rows.shape[1] // place.depths
    blocks = [
        depth_swap(rows[:, k * width : (k + 1) * width], k)[None] for k in range(place.depths)
    ]
    by_sequence = reorder(jnp.concatenate(blocks, 0), place.depths, place.depth, 0)
    by_sequence = by_sequence.reshape(micro, 2, length // 2, width)
    own = lax.dynamic_index_in_dim(by_sequence, place.core, 1, keepdims=False)
    other = core_swap(lax.dynamic_index_in_dim(by_sequence, 1 - place.core, 1, keepdims=False))
    return both_cores(place, own, other, 1)


def own_row(place, values):
    both = both_cores(place, values[None], core_swap(values)[None], 0)
    both = jnp.swapaxes(both, 0, 1).reshape((-1,) + values.shape[1:])
    return lax.dynamic_index_in_dim(both, place.depth, 0, keepdims=False)


def own_channels(place, values):
    size = values.shape[-1] // (2 * place.depths)
    return jnp.concatenate(
        [
            pick(values, k * 2 + place.core, size, values.ndim - 1)
            for k in range(place.depths)
        ],
        -1,
    )


def all_channels(place, values):
    size = values.shape[-1] // place.depths
    full = jnp.zeros(values.shape[:-1] + (2 * values.shape[-1],), values.dtype)
    for k in range(place.depths):
        block = values[..., k * size : (k + 1) * size]
        full = lax.dynamic_update_slice_in_dim(
            full, block, (k * 2 + place.core) * size, values.ndim - 1
        )
    return full


def sum_everywhere(place, values):
    values = core_sum_exact(values)
    for bit in place.bits:
        values = values + chip_swap(values, bit)
    offset = 1
    while offset < place.depths:
        values = values + depth_swap(values, offset)
        offset *= 2
    return values


def norm_forward(values, gain):
    low = to_low(values)
    wide = low.astype(jnp.float32)
    scale = lax.rsqrt(jnp.mean(wide * wide, axis=-1, keepdims=True) + EPSILON)
    return to_low(wide * scale * gain), (low, scale)


def norm_backward(gradient, memory, gain):
    low, scale = memory
    wide = low.astype(jnp.float32)
    weighted = gradient * gain
    inner = jnp.mean(weighted * wide, axis=-1, keepdims=True)
    grad_gain = jnp.sum(gradient * (wide * scale), axis=0)
    return scale * weighted - wide * (scale * scale * scale * inner), grad_gain


def mamba_forward(place, residual, weights, params, items):
    w_zx, w_bcdt, w_out = weights
    norm, taps, map_taps, heads, channels, owner = params
    columns, ahead, segment_rows = items
    normed_low, norm_memory = norm_forward(residual, norm)
    zx_proj = matmul(normed_low, w_zx)
    bcdt = matmul(normed_low, w_bcdt)
    per_block = channels.shape[1] // place.depths // LANES
    mixed, y, squares, states = mix_forward(
        per_block, zx_proj, bcdt, columns, segment_rows, taps, map_taps, heads, channels
    )
    scale = lax.rsqrt(core_sum_exact(squares) / (2 * mixed.shape[1]) + EPSILON)
    result = residual + core_sum(matmul(mixed, w_out)) * scale
    return (result, (normed_low, mixed, norm_memory, scale, zx_proj, bcdt, y, states))


def mamba_backward(place, gradient, weights, params, items, memory, scatter, more, reduced):
    w_zx, w_bcdt, w_out = weights
    norm, taps, map_taps, heads, channels, owner = params
    columns, ahead, segment_rows = items
    normed_low, mixed, norm_memory, scale, zx_proj, bcdt, y, states = memory
    spread = to_low(gradient)
    grad_mixed = right_product(spread, w_out)
    width = mixed.shape[1]
    inner = core_sum_exact(
        jnp.sum(grad_mixed * mixed.astype(jnp.float32), axis=1, keepdims=True)
    )
    coefficient = scale * scale * scale * inner / (2 * width)
    nothing = jnp.zeros_like(scale[:, 0])
    later = jnp.stack(ahead + [scale[:, 0], coefficient[:, 0], nothing, nothing, nothing], 1)
    grad_zx, grad_maps, grad_dt, grad_taps, grad_map_taps, grad_heads, grad_channels = (
        mix_backward(
            width // place.depths // LANES,
            grad_mixed,
            zx_proj,
            bcdt,
            y,
            states,
            columns,
            later,
            segment_rows,
            taps,
            map_taps,
            heads,
            channels,
            owner,
        )
    )
    head_count = width // HEAD_SIZE
    grad_maps = core_sum_exact(grad_maps)
    own_maps = to_low(pick(grad_maps, place.core, LANES, 1))
    low_dt = to_low(grad_dt)
    grad_bcdt = jnp.concatenate([own_maps, low_dt], 1)
    own_bcdt = jnp.concatenate([pick(w_bcdt, place.core, LANES, 1), w_bcdt[:, 2 * LANES :]], 1)
    partial = right_product(grad_zx, w_zx) + right_product(grad_bcdt, own_bcdt)
    grad_in, grad_norm = norm_backward(core_sum(partial), norm_memory, norm)
    small_from = jnp.concatenate([own_maps, low_dt[:, :head_count]], 1)
    scaled = to_low(spread.astype(jnp.float32) * scale)
    rows = normed_low.shape[1] // place.chips
    weight_grads = scatter.own(
        [("columns", normed_low, grad_zx), ("rows", scaled, mixed)] + more,
        [rows, width // place.depths] + [rows] * len(more),
        [partial],
        reduced,
    )
    by_tap = grad_taps.reshape(4, 8, -1).sum(1)
    map_by_tap = grad_map_taps.reshape(4, 8, -1).sum(1)
    head_sums = grad_heads.reshape(2, 8, -1).sum(1)[:, :head_count]
    channel_sums = grad_channels.reshape(2, 8, -1).sum(1)
    small_grads = (
        0.5 * grad_norm,
        by_tap,
        map_by_tap,
        head_sums[0],
        head_sums[1],
        channel_sums[0].reshape(head_count, HEAD_SIZE).sum(1),
        channel_sums[1],
    )
    return (gradient + grad_in, weight_grads, small_grads, (normed_low, small_from))


def small_scatter(place, pairs, half_maps, heads):
    bits = place.bits[::-1]
    order = send_order(place, bits)
    wholes = [left_product(normed, small_from) for normed, small_from in pairs]
    whole = jnp.concatenate(wholes, 1)
    size = whole.shape[0] // place.chips
    ordered = [whole[r * size : (r + 1) * size] for r in order]
    half = place.chips // 2
    kept = jnp.concatenate(ordered[:half], 0)
    sent = to_low(jnp.concatenate(ordered[half:], 0))
    block = scatter_rest(place, kept, sent, bits, 0, over_depth=False)
    offset = 1
    while offset < place.depths:
        block = block + depth_swap(block, offset)
        offset *= 2
    width = block.shape[1] // len(pairs)
    layers = jnp.stack([block[:, n * width : (n + 1) * width] for n in range(len(pairs))])
    own_dt = pick(layers[:, :, half_maps:], place.depth, heads // place.depths, 2)
    return join_columns(place, layers[:, :, :half_maps]), join_columns(place, own_dt)


def one_device(
    inputs,
    cotangent,
    boundary_flags,
    segment_ids,
    mamba_norm,
    mamba_z,
    mamba_x,
    mamba_bc,
    mamba_dt,
    mamba_conv_x,
    mamba_conv_bc,
    mamba_dt_bias,
    mamba_a_log,
    mamba_skip,
    mamba_gate_norm,
    mamba_out,
    router_qk,
    group_up,
    group_down,
    attn_norms,
    attn_qkv,
    attn_out,
    ffn_gate_up,
    ffn_down,
):
    place = Place()
    micro = inputs.shape[0]
    wide = jnp.float32

    zx_shard = split_columns(place, [mamba_z[0], mamba_x[0]])
    gather = Gather(place)
    (enc_zx,) = gather.matrices([("columns", zx_shard)])
    residual_low = own_sequence(place, inputs, other_rows(place, inputs))
    residual = residual_low.astype(wide)

    mamba_bc, mamba_dt, mamba_out, router_qk, _ = lax.optimization_barrier(
        (mamba_bc, mamba_dt, mamba_out, router_qk, zx_shard)
    )
    out_shard = split_rows(place, mamba_out)
    router_shard = split_columns(place, [router_qk[0], router_qk[1]])
    enc_out, w_router, w_up = gather.matrices(
        [("rows", out_shard[0]), ("columns", router_shard), ("folded", group_up)]
    )
    dt_shard = split_columns(place, [mamba_dt])
    dt_shard = jnp.concatenate([depth_swap(dt_shard, k) for k in range(place.depths)], -1)
    dt_shard = reorder(dt_shard, place.depths, place.depth)
    bc_shard = both_cores(place, mamba_bc, core_swap(mamba_bc), 1)
    fill = jnp.zeros(dt_shard.shape[:2] + (LANES - dt_shard.shape[2],), jnp.bfloat16)
    w_bcdt = gather_chips(place, jnp.concatenate([bc_shard, dt_shard, fill], -1), place.bits)
    enc_weights = (enc_zx, w_bcdt[0], enc_out)
    qkv_shard = split_columns(place, [attn_qkv[0], attn_qkv[1], attn_qkv[2]])
    qkv_fill = -qkv_shard.shape[1] % LANES
    (w_qkv,) = gather.matrices([("columns", jnp.pad(qkv_shard, ((0, 0), (0, qkv_fill))))])
    w_attn_out, w_down = gather.matrices(
        [("rows", split_rows(place, attn_out)), ("columns", group_down)], filled=True
    )
    boundary_flags, segment_ids = lax.optimization_barrier(
        (boundary_flags, segment_ids, w_bcdt)
    )[:2]
    flag_row = own_row(place, boundary_flags)
    segment = own_row(place, segment_ids)

    mamba_params = []
    for layer in range(2):
        taps = own_channels(place, mamba_conv_x[layer]).astype(wide)
        width = taps.shape[1]
        bias = own_channels(place, mamba_dt_bias[layer]).astype(wide)
        rate = -jnp.exp(own_channels(place, mamba_a_log[layer]).astype(wide))
        skip = own_channels(place, mamba_skip[layer]).astype(wide)
        gain = own_channels(place, mamba_gate_norm[layer]).astype(wide)
        heads = jnp.pad(jnp.stack([bias, rate]), ((0, 6), (0, LANES - bias.shape[0])))
        channels = jnp.pad(jnp.stack([jnp.repeat(skip, HEAD_SIZE), gain]), ((0, 6), (0, 0)))
        owner = (
            jnp.arange(width)[:, None] // HEAD_SIZE == jnp.arange(LANES)[None, :]
        ).astype(jnp.bfloat16)
        mamba_params.append(
            (
                reorder(mamba_norm[layer], place.chips, place.chip).astype(wide),
                taps,
                mamba_conv_bc[layer].astype(wide),
                heads,
                channels,
                owner,
            )
        )
    items = item_columns(segment)
    norm_gains = reorder(attn_norms, place.chips, place.chip).astype(wide)

    starts = jnp.concatenate([jnp.ones((1,), jnp.bool_), segment[1:] != segment[:-1]])
    group_rank = jnp.cumsum(flag_row) - 1
    slots = jnp.arange(CAP, dtype=jnp.int32)
    marked = (group_rank[None, :] == slots[:, None]) & (flag_row[None, :] == 1)
    marked_low = marked.astype(jnp.bfloat16)
    slot_valid = jnp.any(marked, axis=1)
    encoded, enc_memory = mamba_forward(
        place, residual, enc_weights, mamba_params[0], items
    )

    ffn_shard = split_columns(place, [ffn_gate_up[0], ffn_gate_up[1]])
    (w_gate_up,) = gather.matrices([("columns", ffn_shard)], [enc_memory[4]])
    (w_ffn_down,) = gather.matrices([("rows", split_rows(place, ffn_down))], [enc_memory[1]])

    shared = to_low(encoded)
    length = shared.shape[0]
    qk = matmul(shared, w_router)
    all_dots = core_sum_exact(pair_dots(qk, place.depths))
    prob_row, prob_back = jax.vjp(lambda values: boundary_prob(values.T, starts), all_dots)


    group_rows = to_low(matmul(marked_low, shared))
    group_seg = jnp.sum(jnp.where(marked, segment[None, :] + 1, 0), axis=1) - 1
    own_rows = parity_part(place, group_rows)
    hidden = depth_to_chip(place, core_sum(matmul(own_rows, w_up)))

    dec_shard = split_columns(place, [mamba_z[1], mamba_x[1]])
    dec_zx, dec_out = gather.matrices(
        [("columns", dec_shard), ("rows", out_shard[1])], [qk]
    )
    dec_weights = (dec_zx, w_bcdt[1], dec_out)

    first_low, first_memory = norm_forward(hidden, norm_gains[0])
    qkv = matmul(first_low, w_qkv)
    tables = turn_tables(CAP)
    attended_low = attend(qkv, None, tables, group_seg, place.depths)
    hidden_one = hidden + core_sum(matmul(attended_low, w_attn_out))

    cotangent = gather.hold(cotangent, [hidden_one])
    cot_row = own_sequence(place, cotangent, other_rows(place, cotangent)).astype(wide)

    second_low, second_memory = norm_forward(hidden_one, norm_gains[1])
    gate_up = matmul(second_low, w_gate_up)
    active_low = activate(gate_up, None, place.depths)
    hidden_two = hidden_one + core_sum(matmul(active_low, w_ffn_down))
    third_low = parity_part(place, to_low(hidden_two))
    down_rows = depth_to_chip(place, core_sum(matmul(third_low, w_down)))

    group_probs = jnp.sum(jnp.where(marked, prob_row[None, :], 0.0), axis=1)
    group_probs = jnp.pad(jnp.where(slot_valid, group_probs, 1.0), (0, 8))
    confidence = jnp.where(flag_row == 1, prob_row, 1.0 - prob_row)[:, None]
    rank_column = group_rank[:, None]
    decoder_in, smooth = smooth_forward(group_probs, down_rows, encoded, confidence, rank_column)
    decoded, dec_memory = mamba_forward(
        place, decoder_in, dec_weights, mamba_params[1], items
    )
    outputs = back_to_all(place, to_low(decoded), micro)

    scatter = Scatter(place)
    gradient, dec_grads, dec_smalls, dec_maps = mamba_backward(
        place,
        cot_row,
        dec_weights,
        mamba_params[1],
        items,
        dec_memory,
        scatter,
        [],
        True,
    )
    grad_down, grad_confidence, grad_slots = smooth_backward(
        group_probs, gradient, confidence, rank_column, smooth, down_rows
    )
    grad_probs = jnp.where(flag_row == 1, grad_confidence[:, 0], -grad_confidence[:, 0])
    grad_probs = grad_probs + jnp.sum(jnp.where(marked, grad_slots, 0.0), axis=0)

    dm_rows = hidden.shape[1] // place.chips
    down_low = depth_to_chip(place, grad_down)
    grad_third = to_low(right_product(down_low, w_down))
    grad_hidden = parity_join(place, grad_third, dm_rows // 2).astype(wide)
    spread = to_low(grad_hidden)
    grad_pairs = activate(gate_up, right_product(spread, w_ffn_down), place.depths)
    (own_ffn_down,) = scatter.own(
        [("rows", spread, active_low)], [active_low.shape[1] // place.depths], [grad_pairs], True
    )
    partial = right_product(grad_pairs, w_gate_up)
    (own_gate_up,) = scatter.own(
        [("columns", second_low, grad_pairs)], [dm_rows], [partial], True
    )
    grad_second, grad_norm_two = norm_backward(core_sum(partial), second_memory, norm_gains[1])
    grad_hidden = grad_hidden + grad_second

    spread = to_low(grad_hidden)
    grad_attended = right_product(spread, w_attn_out)
    grad_qkv = attend(qkv, grad_attended, tables, group_seg, place.depths)
    own_attn_out, own_down = scatter.own(
        [("rows", spread, attended_low), ("columns", third_low, down_low)],
        [HEADS_PER_BLOCK * HEAD_SIZE, dm_rows // 2],
        [grad_qkv],
    )
    partial = right_product(grad_qkv, w_qkv)
    (own_qkv,) = scatter.own([("columns", first_low, grad_qkv)], [dm_rows], [partial])
    grad_first, grad_norm_one = norm_backward(core_sum(partial), first_memory, norm_gains[0])
    grad_hidden = grad_hidden + grad_first

    hidden_low = depth_to_chip(place, to_low(grad_hidden))
    d_rows = shared.shape[1] // place.chips
    partial = to_low(right_product(hidden_low, w_up))
    (own_up,) = scatter.own([("columns", own_rows, hidden_low)], [d_rows // 2], [partial])
    grad_rows = parity_join(place, partial, d_rows // 2)
    grad_shared = left_product(marked_low, grad_rows)
    (grad_dots,) = prob_back(grad_probs)
    grad_qk = pair_dots_back(qk, grad_dots, place.depths)
    partial = right_product(grad_qk, w_router)
    grad_shared = grad_shared + core_sum(partial)
    gradient = gradient + grad_shared

    gradient, enc_grads, enc_smalls, enc_maps = mamba_backward(
        place,
        gradient,
        enc_weights,
        mamba_params[0],
        items,
        enc_memory,
        scatter,
        [("columns", shared, grad_qk)],
        False,
    )
    grad_inputs = back_to_all(place, to_low(gradient), micro).astype(wide)

    parts = []
    for smalls in (enc_smalls, dec_smalls):
        parts += [
            reorder(smalls[0], place.chips, place.chip),
            all_channels(place, smalls[1]),
            smalls[2],
            all_channels(place, smalls[3]),
            all_channels(place, smalls[4]),
            all_channels(place, smalls[5]),
            all_channels(place, smalls[6]),
        ]
    parts.append(0.5 * reorder(grad_norm_one, place.chips, place.chip))
    parts.append(0.5 * reorder(grad_norm_two, place.chips, place.chip))
    flat = jnp.concatenate([part.reshape(-1) for part in parts])
    fill = -flat.shape[0] % 1024
    flat = jnp.pad(flat, (0, fill)).reshape(-1, 128)
    flat = sum_everywhere(place, flat).reshape(-1)
    summed = []
    offset = 0
    for part in parts:
        summed.append(flat[offset : offset + part.size].reshape(part.shape))
        offset += part.size
    smalls = [jnp.stack([summed[n], summed[7 + n]]) for n in range(7)]

    head_count = mamba_dt.shape[2] * place.depths // 2
    grad_bc, grad_dt = small_scatter(place, [enc_maps, dec_maps], LANES, head_count)

    def kinds(blocks, count):
        return join_columns(place, jnp.stack(jnp.split(blocks, count, 1)))

    enc_parts = kinds(enc_grads[0], 2)
    dec_parts = kinds(dec_grads[0], 2)
    qkv_width = qkv_shard.shape[1]
    return (
        outputs,
        grad_inputs,
        smalls[0],
        jnp.stack([enc_parts[0], dec_parts[0]]),
        jnp.stack([enc_parts[1], dec_parts[1]]),
        grad_bc,
        grad_dt,
        smalls[1],
        smalls[2],
        smalls[3],
        smalls[4],
        smalls[5],
        smalls[6],
        join_rows(place, jnp.stack([enc_grads[1], dec_grads[1]])),
        kinds(enc_grads[2], 2),
        own_up,
        own_down,
        jnp.stack([summed[14], summed[15]]),
        kinds(own_qkv[:, :qkv_width], 3),
        join_rows(place, own_attn_out),
        kinds(own_gate_up, 2),
        join_rows(place, own_ffn_down),
    )


def solution(mesh):
    in_specs = (
        P(None, "dp", "mp"),
        P(None, "dp", "mp"),
        P(None, "dp"),
        P(None, "dp"),
        P(),
        P(None, "dp", "mp"),
        P(None, "dp", "mp"),
        P(None, "dp", None),
        P(None, "dp", "mp"),
        P(),
        P(),
        P(),
        P(),
        P(),
        P(),
        P(None, "mp", "dp"),
        P(None, "dp", "mp"),
        P("dp", "mp"),
        P("dp", "mp"),
        P(),
        P(None, "dp", "mp"),
        P("mp", "dp"),
        P(None, "dp", "mp"),
        P("mp", "dp"),
    )
    out_specs = (
        P(None, "dp", "mp"),
        P(None, "dp", "mp"),
        P(),
        P(None, "dp", "mp"),
        P(None, "dp", "mp"),
        P(None, "dp", None),
        P(None, "dp", "mp"),
        P(),
        P(),
        P(),
        P(),
        P(),
        P(),
        P(None, "mp", "dp"),
        P(None, "dp", "mp"),
        P("dp", "mp"),
        P("dp", "mp"),
        P(),
        P(None, "dp", "mp"),
        P("mp", "dp"),
        P(None, "dp", "mp"),
        P("mp", "dp"),
    )
    return jax.shard_map(
        one_device, mesh=mesh, in_specs=in_specs, out_specs=out_specs, check_vma=False
    )
```

```python
import functools

import jax
import jax.numpy as jnp
from jax import lax
from jax.experimental import pallas as pl
from jax.experimental.pallas import tpu as pltpu
from jax.sharding import PartitionSpec as P

DM = 1536
AHEADS = 24
CAP = 320


EPSILON = 1e-06
HIGHEST = lax.Precision.HIGHEST


def boundary_prob(all_dots, starts):
    cosine = all_dots[0] * lax.rsqrt(all_dots[1] + EPSILON) * lax.rsqrt(all_dots[2] + EPSILON)
    return jnp.where(starts, 1.0, 0.5 * (1.0 - cosine))


def to_low(values):
    return values.astype(jnp.bfloat16)


def matmul(left, right):
    return jnp.dot(left, right, preferred_element_type=jnp.float32)


def left_product(left, right):
    return lax.dot_general(
        left, right, (((0,), (0,)), ((), ())), preferred_element_type=jnp.float32
    )


def right_product(left, right):
    return lax.dot_general(
        left, right, (((1,), (1,)), ((), ())), preferred_element_type=jnp.float32
    )


BLOCK = 128
LANES = 128
HEAD_SIZE = 64


def sigmoid(values):
    return 1.0 / (1.0 + jnp.exp(-values))


def split_product(values, ones_low):
    high = to_low(values)
    rest = to_low(values - high.astype(jnp.float32))
    return matmul(high, ones_low) + matmul(rest, ones_low)


def exact_product(left, right):
    return jnp.dot(left, right, precision=HIGHEST, preferred_element_type=jnp.float32)


def shifted_down(tail, block, steps):
    joined = jnp.concatenate([tail, block], 0)
    return pltpu.roll(joined, steps, 0)[8:]


def shifted_up(block, head, steps):
    joined = jnp.concatenate([block, head], 0)
    size = joined.shape[0]
    return pltpu.roll(joined, size - steps, 0)[: size - 8]


def filtered(tail, block, taps, columns):
    result = block * taps[3:4]
    for steps in range(1, 4):
        moved = shifted_down(tail, block, steps)
        result = result + moved * columns[:, steps - 1 : steps] * taps[3 - steps : 4 - steps]
    return result


def pair_columns(values, pair, first_half):
    return jnp.where(
        first_half, values[:, 2 * pair : 2 * pair + 1], values[:, 2 * pair + 1 : 2 * pair + 2]
    )


def stacked_halves(values, first_half):
    zero = jnp.zeros_like(values)
    return jnp.concatenate(
        [jnp.where(first_half, values, zero), jnp.where(first_half, zero, values)], 0
    )


def folded_rows(values):
    return jnp.sum(values.reshape(values.shape[0] // 8, 8, values.shape[1]), axis=0)


class Decay:
    def __init__(self, dt_raw, dt_bias, rate, columns, segment_row):
        rows = lax.broadcasted_iota(jnp.int32, (BLOCK, BLOCK), 0)
        cols = lax.broadcasted_iota(jnp.int32, (BLOCK, BLOCK), 1)
        self.lower = rows >= cols
        shifted = dt_raw + dt_bias
        self.steepness = sigmoid(shifted)
        self.step = jnp.maximum(shifted, 0.0) + jnp.log(1.0 + jnp.exp(-jnp.abs(shifted)))
        self.decay = rate * self.step
        self.total = exact_product(self.lower.astype(jnp.float32), self.decay)
        self.total_rows = self.total.T
        same = self.lower & (columns[:, 3:4] == segment_row)
        self.mask = jnp.where(same, 0.0, -1e30)
        last = self.total[BLOCK - 1 : BLOCK]
        self.reach = jnp.exp(self.total) * columns[:, 4:5]
        self.to_end = jnp.exp(last - self.total) * columns[:, 5:6]
        self.kept = jnp.exp(last) * columns[BLOCK - 1 : BLOCK, 4:5]

    def factor(self, head):
        return jnp.exp(
            self.total[:, head : head + 1] - self.total_rows[head : head + 1] + self.mask
        )


def zx_lanes(pair, per_block):
    block, tile = divmod(pair, per_block)
    start = (2 * block * per_block + tile) * LANES
    shift = per_block * LANES
    return slice(start, start + LANES), slice(start + shift, start + shift + LANES)


def mix_kernel(
    per_block,
    zx_ref,
    bcdt_ref,
    columns_ref,
    segment_ref,
    taps_ref,
    map_taps_ref,
    heads_ref,
    channels_ref,
    mixed_ref,
    y_ref,
    square_ref,
    states_ref,
    state,
    tail_x,
    tail_maps,
    ends,
):
    pairs = channels_ref.shape[1] // LANES

    @pl.when(pl.program_id(0) == 0)
    def _():
        state[...] = jnp.zeros_like(state)
        tail_x[...] = jnp.zeros_like(tail_x)
        tail_maps[...] = jnp.zeros_like(tail_maps)

    columns = columns_ref[...]
    first_half = lax.broadcasted_iota(jnp.int32, (1, LANES), 1) < HEAD_SIZE
    maps_in = bcdt_ref[:, : 2 * LANES]
    maps = filtered(tail_maps[...], maps_in, map_taps_ref[...], columns)
    maps = maps * sigmoid(maps)
    in_map = to_low(maps[:, :LANES])
    out_map = to_low(maps[:, LANES:])
    heads = heads_ref[...]
    decay = Decay(
        bcdt_ref[:, 2 * LANES :], heads[0:1], heads[1:2], columns, segment_ref[0, 0:1, :]
    )
    meeting = right_product(out_map, in_map)
    low_state = to_low(state[...])
    states_ref[...] = low_state
    y_ref[...] = matmul(out_map, low_state)
    squares = jnp.zeros((BLOCK, LANES), jnp.float32)
    for pair in range(pairs):
        lanes = slice(pair * LANES, (pair + 1) * LANES)
        z_lanes, x_lanes = zx_lanes(pair, per_block)
        block = zx_ref[:, x_lanes]
        pre = filtered(tail_x[:, lanes], block, taps_ref[:, lanes], columns)
        tail_x[:, lanes] = block[BLOCK - 8 :]
        value = pre * sigmoid(pre)
        scaled = value * pair_columns(decay.step, pair, first_half)
        ends[:, lanes] = to_low(scaled * pair_columns(decay.to_end, pair, first_half))
        weights = jnp.concatenate(
            [to_low(meeting * decay.factor(2 * pair + half)) for half in range(2)], 1
        )
        y = matmul(weights, stacked_halves(to_low(scaled), first_half))
        y = y + y_ref[:, lanes] * pair_columns(decay.reach, pair, first_half)
        y_ref[:, lanes] = y
        gate_in = zx_ref[:, z_lanes]
        gated = (y + channels_ref[0:1, lanes] * value) * (gate_in * sigmoid(gate_in))
        squares = squares + gated * gated
        mixed_ref[:, lanes] = to_low(gated * channels_ref[1:2, lanes])
        state[:, lanes] = state[:, lanes] * pair_columns(decay.kept, pair, first_half)
    square_ref[...] = jnp.sum(squares, axis=1, keepdims=True)
    state[...] += left_product(in_map, ends[...])
    tail_maps[...] = bcdt_ref[BLOCK - 8 :, : 2 * LANES]


def mix_back_kernel(
    per_block,
    grad_ref,
    zx_ref,
    zx_tail_ref,
    bcdt_ref,
    maps_tail_ref,
    y_ref,
    states_ref,
    columns_ref,
    later_ref,
    segment_ref,
    taps_ref,
    map_taps_ref,
    heads_ref,
    channels_ref,
    owner_ref,
    grad_zx_ref,
    grad_maps_ref,
    grad_dt_ref,
    grad_taps_ref,
    grad_map_taps_ref,
    grad_heads_ref,
    grad_channels_ref,
    grad_state,
    head_x,
    head_maps,
    ends,
    reached,
    pulled,
    balance,
    step_part,
):
    pairs = channels_ref.shape[1] // LANES
    step = pl.program_id(0)
    first_chunk = step == pl.num_programs(0) - 1

    @pl.when(step == 0)
    def _():
        grad_state[...] = jnp.zeros_like(grad_state)
        head_x[...] = jnp.zeros_like(head_x)
        head_maps[...] = jnp.zeros_like(head_maps)
        grad_taps_ref[...] = jnp.zeros_like(grad_taps_ref)
        grad_map_taps_ref[...] = jnp.zeros_like(grad_map_taps_ref)
        grad_heads_ref[...] = jnp.zeros_like(grad_heads_ref)
        grad_channels_ref[...] = jnp.zeros_like(grad_channels_ref)

    columns = columns_ref[...]
    later = later_ref[...]
    first_half = lax.broadcasted_iota(jnp.int32, (1, LANES), 1) < HEAD_SIZE
    tail_maps = jnp.where(first_chunk, 0.0, maps_tail_ref[:, : 2 * LANES])
    maps_in = bcdt_ref[:, : 2 * LANES]
    maps_pre = filtered(tail_maps, maps_in, map_taps_ref[...], columns)
    maps_open = sigmoid(maps_pre)
    maps = maps_pre * maps_open
    in_map = to_low(maps[:, :LANES])
    out_map = to_low(maps[:, LANES:])
    heads = heads_ref[...]
    decay = Decay(
        bcdt_ref[:, 2 * LANES :], heads[0:1], heads[1:2], columns, segment_ref[0, 0:1, :]
    )
    meeting = right_product(out_map, in_map)
    low_grad_state = to_low(grad_state[...])
    pulled[...] = matmul(in_map, low_grad_state)
    scale = later[:, 3:4]
    coefficient = later[:, 4:5]
    grad_meeting = jnp.zeros((BLOCK, BLOCK), jnp.float32)
    for pair in range(pairs):
        lanes = slice(pair * LANES, (pair + 1) * LANES)
        z_lanes, x_lanes = zx_lanes(pair, per_block)
        tail = jnp.where(first_chunk, 0.0, zx_tail_ref[:, x_lanes])
        block = zx_ref[:, x_lanes]
        taps = taps_ref[:, lanes]
        pre = filtered(tail, block, taps, columns)
        opened = sigmoid(pre)
        value = pre * opened
        slope = opened + value * (1.0 - opened)
        gate_in = zx_ref[:, z_lanes]
        gate_open = sigmoid(gate_in)
        gate = gate_in * gate_open
        skip = channels_ref[0:1, lanes]
        gain = channels_ref[1:2, lanes]
        y = y_ref[:, lanes]
        whole = y + skip * value
        gated = whole * gate
        grad_mixed = grad_ref[:, lanes]
        grad_gated = scale * (grad_mixed * gain) - coefficient * gated
        grad_channels_ref[8:16, lanes] += folded_rows(grad_mixed * gated * scale)
        grad_y = grad_gated * gate
        grad_zx_ref[:, z_lanes] = to_low(
            grad_gated * whole * (gate_open + gate * (1.0 - gate_open))
        )
        grad_channels_ref[0:8, lanes] += folded_rows(grad_y * value)
        low_grad_y = to_low(grad_y)
        reached[:, lanes] = to_low(grad_y * pair_columns(decay.reach, pair, first_half))
        step_wide = pair_columns(decay.step, pair, first_half)
        scaled = value * step_wide
        low_scaled = to_low(scaled)
        end_wide = pair_columns(decay.to_end, pair, first_half)
        ends[:, lanes] = to_low(scaled * end_wide)
        stacked = stacked_halves(low_grad_y, first_half)
        grad_weights = right_product(stacked, low_scaled)
        parts = []
        for half in range(2):
            factor = decay.factor(2 * pair + half)
            grad_meeting = (
                grad_meeting + factor * grad_weights[half * BLOCK : (half + 1) * BLOCK]
            )
            parts.append(to_low(meeting * factor))
        from_end = pulled[:, lanes] * end_wide
        grad_scaled = left_product(jnp.concatenate(parts, 0), stacked) + from_end
        wide_scaled = low_scaled.astype(jnp.float32)
        balance[:BLOCK, lanes] = low_grad_y.astype(jnp.float32) * y - wide_scaled * grad_scaled
        step_part[:, lanes] = to_low(grad_scaled * value)
        kept = pair_columns(decay.kept, pair, first_half)
        kept_state = grad_state[:, lanes] * kept
        balance[BLOCK : BLOCK + 8, lanes] = folded_rows(wide_scaled * from_end) + folded_rows(
            kept_state * states_ref[:, lanes].astype(jnp.float32)
        )
        grad_state[:, lanes] = kept_state
        grad_pre = (grad_scaled * step_wide + grad_y * skip) * slope
        grad_taps_ref[24:32, lanes] += folded_rows(grad_pre * block)
        grad_x = grad_pre * taps[3:4]
        head = head_x[:, lanes]
        for steps in range(1, 4):
            moved = shifted_down(tail, block, steps)
            grad_taps_ref[24 - 8 * steps : 32 - 8 * steps, lanes] += folded_rows(
                grad_pre * columns[:, steps - 1 : steps] * moved
            )
            grad_x = grad_x + (
                shifted_up(grad_pre, head, steps)
                * later[:, steps - 1 : steps]
                * taps[3 - steps : 4 - steps]
            )
        grad_zx_ref[:, x_lanes] = to_low(grad_x)
        head_x[:, lanes] = grad_pre[:8]

    owner = owner_ref[...]
    grad_total = split_product(balance[:BLOCK, :], owner)
    end_rows = split_product(balance[BLOCK : BLOCK + 8, :], owner)
    end_total = jnp.sum(end_rows, axis=0, keepdims=True)
    rows = lax.broadcasted_iota(jnp.int32, (BLOCK, LANES), 0)
    grad_total = grad_total + jnp.where(rows == BLOCK - 1, end_total, 0.0)
    upper = jnp.where(rows <= lax.broadcasted_iota(jnp.int32, (BLOCK, LANES), 1), 1.0, 0.0)
    grad_decay = exact_product(upper, grad_total)
    grad_step = matmul(step_part[...], owner) + grad_decay * heads[1:2]
    grad_raw = grad_step * decay.steepness
    grad_dt_ref[...] = grad_raw
    grad_heads_ref[0:8, :] += folded_rows(grad_raw)
    grad_heads_ref[8:16, :] += folded_rows(grad_decay * decay.decay)

    low_meeting = to_low(grad_meeting)
    grad_out_map = matmul(low_meeting, in_map) + right_product(reached[...], states_ref[...])
    grad_in_map = left_product(low_meeting, out_map) + right_product(ends[...], low_grad_state)
    grad_state[...] += left_product(out_map, reached[...])
    grad_pre = jnp.concatenate([grad_in_map, grad_out_map], 1) * (
        maps_open + maps * (1.0 - maps_open)
    )
    map_taps = map_taps_ref[...]
    grad_map_taps_ref[24:32, :] += folded_rows(grad_pre * maps_in)
    grad_maps = grad_pre * map_taps[3:4]
    head = head_maps[...]
    for steps in range(1, 4):
        moved = shifted_down(tail_maps, maps_in, steps)
        grad_map_taps_ref[24 - 8 * steps : 32 - 8 * steps, :] += folded_rows(
            grad_pre * columns[:, steps - 1 : steps] * moved
        )
        grad_maps = grad_maps + (
            shifted_up(grad_pre, head, steps)
            * later[:, steps - 1 : steps]
            * map_taps[3 - steps : 4 - steps]
        )
    grad_maps_ref[...] = grad_maps
    head_maps[...] = grad_pre[:8]


def whole_block(*shape):
    return pl.BlockSpec(shape, lambda step: (0,) * len(shape))


def mix_settings(length, channels, work):
    return dict(
        compiler_params=pltpu.CompilerParams(
            dimension_semantics=("arbitrary",), vmem_limit_bytes=48 * 1024 * 1024
        ),
        cost_estimate=pl.CostEstimate(
            flops=work * length * channels * BLOCK,
            bytes_accessed=length * channels * 16,
            transcendentals=length * channels * 4,
        ),
    )


def mix_forward(
    per_block, zx_proj, bcdt, columns, segment_rows, taps, map_taps, heads, channels
):
    length = zx_proj.shape[0]
    width = channels.shape[1]
    chunks = length // BLOCK

    def rows(size):
        return pl.BlockSpec((BLOCK, size), lambda step: (step, 0))

    return pl.pallas_call(
        functools.partial(mix_kernel, per_block),
        grid=(chunks,),
        in_specs=[
            rows(2 * width),
            rows(3 * LANES),
            rows(8),
            pl.BlockSpec((1, 8, BLOCK), lambda step: (step, 0, 0)),
            whole_block(4, width),
            whole_block(4, 2 * LANES),
            whole_block(8, LANES),
            whole_block(8, width),
        ],
        out_specs=[rows(width), rows(width), rows(1), rows(width)],
        out_shape=[
            jax.ShapeDtypeStruct((length, width), jnp.bfloat16),
            jax.ShapeDtypeStruct((length, width), jnp.float32),
            jax.ShapeDtypeStruct((length, 1), jnp.float32),
            jax.ShapeDtypeStruct((chunks * LANES, width), jnp.bfloat16),
        ],
        scratch_shapes=[
            pltpu.VMEM((LANES, width), jnp.float32),
            pltpu.VMEM((8, width), jnp.float32),
            pltpu.VMEM((8, 2 * LANES), jnp.float32),
            pltpu.VMEM((BLOCK, width), jnp.bfloat16),
        ],
        **mix_settings(length, width, 8),
    )(zx_proj, bcdt, columns, segment_rows, taps, map_taps, heads, channels)


def mix_backward(
    per_block,
    grad_mixed,
    zx_proj,
    bcdt,
    y,
    states,
    columns,
    later,
    segment_rows,
    taps,
    map_taps,
    heads,
    channels,
    owner,
):
    length, width = grad_mixed.shape
    chunks = length // BLOCK
    eighths = BLOCK // 8

    def rows(size):
        return pl.BlockSpec((BLOCK, size), lambda step: (chunks - 1 - step, 0))

    def before(size):
        return pl.BlockSpec(
            (8, size), lambda step: (jnp.maximum((chunks - 1 - step) * eighths - 1, 0), 0)
        )

    low = jnp.bfloat16
    wide = jnp.float32
    return pl.pallas_call(
        functools.partial(mix_back_kernel, per_block),
        grid=(chunks,),
        in_specs=[
            rows(width),
            rows(2 * width),
            before(2 * width),
            rows(3 * LANES),
            before(3 * LANES),
            rows(width),
            rows(width),
            rows(8),
            rows(8),
            pl.BlockSpec((1, 8, BLOCK), lambda step: (chunks - 1 - step, 0, 0)),
            whole_block(4, width),
            whole_block(4, 2 * LANES),
            whole_block(8, LANES),
            whole_block(8, width),
            whole_block(width, LANES),
        ],
        out_specs=[
            rows(2 * width),
            rows(2 * LANES),
            rows(LANES),
            whole_block(32, width),
            whole_block(32, 2 * LANES),
            whole_block(16, LANES),
            whole_block(16, width),
        ],
        out_shape=[
            jax.ShapeDtypeStruct((length, 2 * width), low),
            jax.ShapeDtypeStruct((length, 2 * LANES), wide),
            jax.ShapeDtypeStruct((length, LANES), wide),
            jax.ShapeDtypeStruct((32, width), wide),
            jax.ShapeDtypeStruct((32, 2 * LANES), wide),
            jax.ShapeDtypeStruct((16, LANES), wide),
            jax.ShapeDtypeStruct((16, width), wide),
        ],
        scratch_shapes=[
            pltpu.VMEM((LANES, width), wide),
            pltpu.VMEM((8, width), wide),
            pltpu.VMEM((8, 2 * LANES), wide),
            pltpu.VMEM((BLOCK, width), low),
            pltpu.VMEM((BLOCK, width), low),
            pltpu.VMEM((BLOCK, width), wide),
            pltpu.VMEM((BLOCK + 8, width), wide),
            pltpu.VMEM((BLOCK, width), low),
        ],
        **mix_settings(length, width, 24),
    )(
        grad_mixed,
        zx_proj,
        zx_proj,
        bcdt,
        bcdt,
        y,
        states,
        columns,
        later,
        segment_rows,
        taps,
        map_taps,
        heads,
        channels,
        owner,
    )


def item_columns(segment):
    length = segment.shape[0]
    back = []
    ahead = []
    for steps in range(1, 4):
        same = segment[steps:] == segment[:-steps]
        none = jnp.zeros((steps,), jnp.bool_)
        back.append(jnp.concatenate([none, same]))
        ahead.append(jnp.concatenate([same, none]))
    blocks = segment.reshape(-1, BLOCK)
    last = blocks[:, BLOCK - 1]
    before = jnp.concatenate([jnp.full((1,), -1, segment.dtype), last[:-1]])
    carried = (blocks == before[:, None]).reshape(-1)
    ending = (blocks == last[:, None]).reshape(-1)
    wide = jnp.float32
    nothing = jnp.zeros((length,), wide)
    columns = jnp.stack(
        [b.astype(wide) for b in back]
        + [segment.astype(wide), carried.astype(wide), ending.astype(wide), nothing, nothing],
        1,
    )
    rows = jnp.broadcast_to(blocks.astype(wide)[:, None, :], (blocks.shape[0], 8, BLOCK))
    return columns, [a.astype(wide) for a in ahead], rows


SLOTS = 384


def smooth_kernel(probs_ref, down_ref, encoded_ref, confidence_ref, rank_ref, out_ref, smooth_ref, high, rest):
    count = down_ref.shape[0]

    @pl.when(pl.program_id(0) == 0)
    def _():
        high[count:, :] = jnp.zeros((SLOTS - count, high.shape[1]), jnp.bfloat16)
        rest[count:, :] = jnp.zeros((SLOTS - count, high.shape[1]), jnp.bfloat16)

        def tile(index, previous):
            start = pl.multiple_of(index * 8, 8)
            rows = down_ref[pl.ds(start, 8), :]
            done = []
            for r in range(8):
                prob = probs_ref[start + r]
                previous = prob * rows[r : r + 1] + (1.0 - prob) * previous
                done.append(previous)
            smooth_ref[pl.ds(start, 8), :] = jnp.concatenate(done, 0)
            return previous

        lax.fori_loop(0, count // 8, tile, jnp.zeros((1, down_ref.shape[1]), jnp.float32))
        smooth = smooth_ref[...]
        low = to_low(smooth)
        high[:count, :] = low
        rest[:count, :] = to_low(smooth - low.astype(jnp.float32))

    slots = lax.broadcasted_iota(jnp.int32, (BLOCK, SLOTS), 1)
    chosen = jnp.where(slots == rank_ref[...], 1.0, 0.0).astype(jnp.bfloat16)
    spread = matmul(chosen, high[...]) + matmul(chosen, rest[...])
    out_ref[...] = encoded_ref[...] + confidence_ref[...] * spread


def smooth_back_kernel(
    probs_ref,
    grad_ref,
    confidence_ref,
    rank_ref,
    smooth_ref,
    down_ref,
    grad_down_ref,
    grad_confidence_ref,
    grad_probs_ref,
    total,
    low,
):
    count = down_ref.shape[0]
    width = down_ref.shape[1]
    step = pl.program_id(0)

    @pl.when(step == 0)
    def _():
        total[...] = jnp.zeros_like(total)
        low[:count, :] = to_low(smooth_ref[...])
        low[count:, :] = jnp.zeros((SLOTS - count, width), jnp.bfloat16)

    slots = lax.broadcasted_iota(jnp.int32, (BLOCK, SLOTS), 1)
    chosen = jnp.where(slots == rank_ref[...], 1.0, 0.0).astype(jnp.bfloat16)
    gradient = grad_ref[...]
    total[...] += left_product(chosen, to_low(confidence_ref[...] * gradient))
    grad_confidence_ref[...] = jnp.sum(gradient * matmul(chosen, low[...]), axis=1, keepdims=True)

    @pl.when(step == pl.num_programs(0) - 1)
    def _():
        tiles = count // 16

        def tile(index, later):
            index = tiles - 1 - index
            start = pl.multiple_of(index * 16, 16)
            rows = total[pl.ds(start, 16), :]
            done = [None] * 16
            kept = [None] * 16
            for r in range(15, -1, -1):
                later = rows[r : r + 1] + (1.0 - probs_ref[start + r + 1]) * later
                kept[r] = later
                done[r] = probs_ref[start + r] * later
            grad_down_ref[pl.ds(start, 16), :] = to_low(jnp.concatenate(done, 0))
            total[pl.ds(start, 16), :] = jnp.concatenate(kept, 0)
            return later

        lax.fori_loop(0, tiles, tile, jnp.zeros((1, width), jnp.float32))
        smooth = smooth_ref[...]
        places = lax.broadcasted_iota(jnp.int32, (count, 1), 0)
        before = jnp.where(places == 0, 0.0, pltpu.roll(smooth, 1, 0))
        grad_probs_ref[...] = jnp.sum(
            total[:count, :] * (down_ref[...] - before), axis=1, keepdims=True
        )


def byte_rows(size):
    return pl.BlockSpec((BLOCK, size), lambda step: (step, 0))


def kernel_settings(flops, traffic):
    return dict(
        compiler_params=pltpu.CompilerParams(
            dimension_semantics=("arbitrary",), vmem_limit_bytes=48 * 1024 * 1024
        ),
        cost_estimate=pl.CostEstimate(flops=flops, bytes_accessed=traffic, transcendentals=0),
    )


def smooth_forward(probs, down_rows, encoded, confidence, rank):
    length, width = encoded.shape
    count = down_rows.shape[0]
    wide = jnp.float32
    return pl.pallas_call(
        smooth_kernel,
        grid=(length // BLOCK,),
        in_specs=[
            pl.BlockSpec(memory_space=pltpu.SMEM),
            whole_block(count, width),
            byte_rows(width),
            byte_rows(1),
            byte_rows(1),
        ],
        out_specs=[byte_rows(width), whole_block(count, width)],
        out_shape=[
            jax.ShapeDtypeStruct((length, width), wide),
            jax.ShapeDtypeStruct((count, width), wide),
        ],
        scratch_shapes=[pltpu.VMEM((SLOTS, width), jnp.bfloat16)] * 2,
        **kernel_settings(4 * length * SLOTS * width, length * width * 8),
    )(probs, down_rows, encoded, confidence, rank)


def smooth_backward(probs, gradient, confidence, rank, smooth, down_rows):
    length, width = gradient.shape
    count = down_rows.shape[0]
    wide = jnp.float32
    return pl.pallas_call(
        smooth_back_kernel,
        grid=(length // BLOCK,),
        in_specs=[
            pl.BlockSpec(memory_space=pltpu.SMEM),
            byte_rows(width),
            byte_rows(1),
            byte_rows(1),
            whole_block(count, width),
            whole_block(count, width),
        ],
        out_specs=[whole_block(count, width), byte_rows(1), whole_block(count, 1)],
        out_shape=[
            jax.ShapeDtypeStruct((count, width), jnp.bfloat16),
            jax.ShapeDtypeStruct((length, 1), wide),
            jax.ShapeDtypeStruct((count, 1), wide),
        ],
        scratch_shapes=[pltpu.VMEM((SLOTS, width), wide), pltpu.VMEM((SLOTS, width), jnp.bfloat16)],
        **kernel_settings(4 * length * SLOTS * width, length * width * 4),
    )(probs, gradient, confidence, rank, smooth, down_rows)


def turned(values, cosines, sines):
    lane = lax.broadcasted_iota(jnp.int32, values.shape, 1) % HEAD_SIZE
    swapped = jnp.where(
        lane < HEAD_SIZE // 2,
        pltpu.roll(values, LANES - HEAD_SIZE // 2, 1),
        pltpu.roll(values, HEAD_SIZE // 2, 1),
    )
    return values * cosines + swapped * sines


def attend_mask(items_ref, items_row_ref):
    size = items_ref.shape[0]
    rows = lax.broadcasted_iota(jnp.int32, (size, size), 0)
    cols = lax.broadcasted_iota(jnp.int32, (size, size), 1)
    return (rows >= cols) & (items_ref[...] == items_row_ref[0:1, :])


def softmaxed(queries, keys, visible):
    scores = right_product(queries, keys) * HEAD_SIZE ** (-0.5)
    scores = jnp.where(visible, scores, -1e30)
    weights = jnp.exp(scores - jnp.max(scores, axis=1, keepdims=True))
    return weights / jnp.sum(weights, axis=1, keepdims=True)


def half_lanes(values, half):
    lane = lax.broadcasted_iota(jnp.int32, (1, LANES), 1) // HEAD_SIZE
    return jnp.where(lane == half, values, jnp.zeros_like(values))


HEADS_PER_BLOCK = 3
BLOCK_WIDTH = 2 * LANES


def unpacked(block, cosines, sines):
    width = HEADS_PER_BLOCK * HEAD_SIZE
    size = block.shape[1]
    queries = block[:, :BLOCK_WIDTH]
    keys = pltpu.roll(block, size - width, 1)[:, :BLOCK_WIDTH]
    values = pltpu.roll(block, size - 2 * width, 1)[:, :BLOCK_WIDTH]
    tiles = []
    for tile in range(2):
        lanes = slice(tile * LANES, (tile + 1) * LANES)
        tiles.append(
            (
                to_low(turned(queries[:, lanes], cosines, sines)),
                to_low(turned(keys[:, lanes], cosines, sines)),
                to_low(values[:, lanes]),
            )
        )
    return tiles


def attend_kernel(qkv_ref, cos_ref, sin_ref, items_ref, items_row_ref, out_ref):
    visible = attend_mask(items_ref, items_row_ref)
    tiles = unpacked(qkv_ref[...], cos_ref[...], sin_ref[...])
    for tile, (queries, keys, values) in enumerate(tiles):
        mixed = 0.0
        for half in range(2 - tile):
            weights = softmaxed(half_lanes(queries, half), keys, visible)
            mixed = mixed + matmul(to_low(weights), half_lanes(values, half))
        out_ref[:, tile * LANES : (tile + 1) * LANES] = to_low(mixed)


def attend_back_kernel(
    qkv_ref, grad_ref, cos_ref, sin_ref, items_ref, items_row_ref, grad_qkv_ref
):
    visible = attend_mask(items_ref, items_row_ref)
    cosines = cos_ref[...]
    sines = sin_ref[...]
    scale = HEAD_SIZE ** (-0.5)
    tiles = unpacked(qkv_ref[...], cosines, sines)
    grads = ([], [], [])
    for tile, (queries, keys, values) in enumerate(tiles):
        gradient = to_low(grad_ref[:, tile * LANES : (tile + 1) * LANES])
        grad_q = 0.0
        grad_k = 0.0
        grad_v = 0.0
        for half in range(2 - tile):
            own_queries = half_lanes(queries, half)
            own_grad = half_lanes(gradient, half)
            weights = softmaxed(own_queries, keys, visible)
            grad_weights = right_product(own_grad, values)
            grad_v = grad_v + left_product(to_low(weights), own_grad)
            inner = jnp.sum(grad_weights * weights, axis=1, keepdims=True)
            grad_scores = to_low(jnp.where(visible, weights * (grad_weights - inner), 0.0))
            grad_q = grad_q + matmul(grad_scores, half_lanes(keys, half))
            grad_k = grad_k + left_product(grad_scores, own_queries)
        grads[0].append(turned(grad_q * scale, cosines, -sines))
        grads[1].append(turned(grad_k * scale, cosines, -sines))
        grads[2].append(grad_v)
    size = qkv_ref.shape[1]
    width = HEADS_PER_BLOCK * HEAD_SIZE
    filling = jnp.zeros((qkv_ref.shape[0], size - BLOCK_WIDTH), jnp.float32)
    packed = 0.0
    for kind, both in enumerate(grads):
        wide = jnp.concatenate(both + [filling], 1)
        packed = packed + (pltpu.roll(wide, kind * width, 1) if kind else wide)
    grad_qkv_ref[...] = to_low(packed)


def turn_tables(count):
    half = HEAD_SIZE // 2
    lane = jnp.arange(LANES) % HEAD_SIZE
    frequency = 10000.0 ** (-(lane % half).astype(jnp.float32) * (2.0 / HEAD_SIZE))
    angles = jnp.arange(count, dtype=jnp.float32)[:, None] * frequency[None, :]
    return jnp.cos(angles), jnp.where(lane < half, -1.0, 1.0)[None, :] * jnp.sin(angles)


def attend(qkv, gradient, tables, group_items, depths):
    count, width = qkv.shape
    size = width // depths

    def tiles(columns):
        return pl.BlockSpec((count, columns), lambda step: (0, step))

    backward = gradient is not None
    items = group_items.astype(jnp.int32)
    out = size if backward else BLOCK_WIDTH
    return pl.pallas_call(
        attend_back_kernel if backward else attend_kernel,
        grid=(depths,),
        in_specs=[tiles(size)]
        + [tiles(BLOCK_WIDTH)] * backward
        + [whole_block(count, LANES)] * 2
        + [whole_block(count, 1), whole_block(8, count)],
        out_specs=tiles(out),
        out_shape=jax.ShapeDtypeStruct((count, depths * out), jnp.bfloat16),
        **kernel_settings(8 * count * count * width, count * width * 16),
    )(
        qkv,
        *([gradient] if backward else []),
        *tables,
        items[:, None],
        jnp.broadcast_to(items[None, :], (8, count)),
    )


def active_kernel(pair_ref, out_ref):
    size = out_ref.shape[1]
    gate = pair_ref[:, :size]
    out_ref[...] = to_low(gate * sigmoid(gate) * pair_ref[:, size:])


def active_back_kernel(pair_ref, grad_ref, out_ref):
    size = grad_ref.shape[1]
    gate = pair_ref[:, :size]
    upper = pair_ref[:, size:]
    opened = sigmoid(gate)
    gradient = grad_ref[...]
    out_ref[:, :size] = to_low(
        gradient * upper * (opened + gate * opened * (1.0 - opened))
    )
    out_ref[:, size:] = to_low(gradient * gate * opened)


def activate(pairs, gradient, depths):
    count, width = pairs.shape
    size = width // depths // 2

    def tiles(columns):
        return pl.BlockSpec((count, columns), lambda step: (0, step))

    backward = gradient is not None
    out = 2 * size if backward else size
    return pl.pallas_call(
        active_back_kernel if backward else active_kernel,
        grid=(depths,),
        in_specs=[tiles(2 * size)] + [tiles(size)] * backward,
        out_specs=tiles(out),
        out_shape=jax.ShapeDtypeStruct((count, depths * out), jnp.bfloat16),
        **kernel_settings(count * width * 8, count * width * 8),
    )(pairs, *([gradient] if backward else []))


def dots_kernel(depths, qk_ref, out_ref, tail):
    size = qk_ref.shape[1] // depths // 2

    @pl.when(pl.program_id(0) == 0)
    def _():
        tail[...] = jnp.zeros_like(tail)

    sums = [0.0, 0.0, 0.0]
    for k in range(depths):
        queries = qk_ref[:, 2 * k * size : (2 * k + 1) * size]
        keys = qk_ref[:, (2 * k + 1) * size : (2 * k + 2) * size]
        lanes = slice(k * size, (k + 1) * size)
        previous = shifted_down(tail[:, lanes], keys, 1)
        tail[:, lanes] = keys[BLOCK - 8 :]
        sums[0] = sums[0] + queries * previous
        sums[1] = sums[1] + queries * queries
        sums[2] = sums[2] + previous * previous
    for kind in range(3):
        out_ref[:, kind : kind + 1] = jnp.sum(sums[kind], axis=1, keepdims=True)
    out_ref[:, 3:] = jnp.zeros((BLOCK, 5), jnp.float32)


def dots_back_kernel(depths, qk_ref, tail_ref, grad_ref, later_ref, out_ref, head):
    size = qk_ref.shape[1] // depths // 2
    step = pl.program_id(0)
    first_block = step == pl.num_programs(0) - 1

    @pl.when(step == 0)
    def _():
        head[...] = jnp.zeros_like(head)

    for k in range(depths):
        query_lanes = slice(2 * k * size, (2 * k + 1) * size)
        key_lanes = slice((2 * k + 1) * size, (2 * k + 2) * size)
        lanes = slice(k * size, (k + 1) * size)
        queries = qk_ref[:, query_lanes]
        keys = qk_ref[:, key_lanes]
        tail = jnp.where(first_block, 0.0, tail_ref[:, key_lanes])
        previous = shifted_down(tail, keys, 1)
        following = shifted_up(queries, head[:, lanes], 1)
        head[:, lanes] = queries[:8]
        out_ref[:, query_lanes] = to_low(
            grad_ref[:, 0:1] * previous + 2.0 * grad_ref[:, 1:2] * queries
        )
        out_ref[:, key_lanes] = to_low(
            later_ref[:, 0:1] * following + 2.0 * later_ref[:, 2:3] * keys
        )


def pair_dots(qk, depths):
    length, width = qk.shape
    return pl.pallas_call(
        functools.partial(dots_kernel, depths),
        grid=(length // BLOCK,),
        in_specs=[byte_rows(width)],
        out_specs=byte_rows(8),
        out_shape=jax.ShapeDtypeStruct((length, 8), jnp.float32),
        scratch_shapes=[pltpu.VMEM((8, width // 2), jnp.float32)],
        **kernel_settings(length * width * 4, length * width * 4),
    )(qk)


def pair_dots_back(qk, gradient, depths):
    length, width = qk.shape
    chunks = length // BLOCK
    eighths = BLOCK // 8
    later = jnp.concatenate([gradient[1:], jnp.zeros((1, 8), jnp.float32)], 0)

    def rows(size):
        return pl.BlockSpec((BLOCK, size), lambda step: (chunks - 1 - step, 0))

    return pl.pallas_call(
        functools.partial(dots_back_kernel, depths),
        grid=(chunks,),
        in_specs=[
            rows(width),
            pl.BlockSpec(
                (8, width), lambda step: (jnp.maximum((chunks - 1 - step) * eighths - 1, 0), 0)
            ),
            rows(8),
            rows(8),
        ],
        out_specs=rows(width),
        out_shape=jax.ShapeDtypeStruct((length, width), jnp.bfloat16),
        scratch_shapes=[pltpu.VMEM((8, width // 2), jnp.float32)],
        **kernel_settings(length * width * 4, length * width * 8),
    )(qk, qk, gradient, later)


def core_swap(values):
    size = lax.axis_size("dp")
    return lax.ppermute(values, "dp", [(d, d ^ 1) for d in range(size)])


def chip_swap(values, bit):
    size = lax.axis_size("dp")
    return lax.ppermute(values, "dp", [(d, d ^ (bit * 2)) for d in range(size)])


def depth_swap(values, offset):
    if offset == 0:
        return values
    size = lax.axis_size("mp")
    return lax.ppermute(values, "mp", [(d, d ^ offset) for d in range(size)])


class Place:
    def __init__(self):
        dp_index = lax.axis_index("dp")
        self.core = dp_index % 2
        self.chip = dp_index // 2
        self.depth = lax.axis_index("mp")
        self.chips = lax.axis_size("dp") // 2
        self.depths = lax.axis_size("mp")
        bits = []
        while 2 ** len(bits) < self.chips:
            bits.append(2 ** len(bits))
        self.bits = bits


def both_cores(place, own, other, axis):
    first = place.core == 0
    return jnp.concatenate([jnp.where(first, own, other), jnp.where(first, other, own)], axis)


def pick(values, index, size, axis):
    return lax.dynamic_slice_in_dim(values, index * size, size, axis)


def reorder(values, count, shift, axis=-1):
    axis = axis % values.ndim
    size = values.shape[axis] // count
    return jnp.concatenate([pick(values, r ^ shift, size, axis) for r in range(count)], axis)


def relative_to_chip(place, values):
    if place.chips == place.depths:
        return reorder(values, place.chips, place.chip ^ place.depth)
    return reorder(reorder(values, place.depths, place.depth), place.chips, place.chip)


def chip_to_relative(place, values):
    if place.chips == place.depths:
        return reorder(values, place.chips, place.chip ^ place.depth)
    return reorder(reorder(values, place.chips, place.chip), place.depths, place.depth)


def depth_to_chip(place, values):
    return reorder(values, place.chips, place.chip)


def split_columns(place, shards):
    axis = shards[0].ndim - 1

    def columns(core):
        return jnp.concatenate([pick(s, core, s.shape[-1] // 2, axis) for s in shards], axis)

    other = core_swap(columns(1 - place.core))
    return both_cores(place, columns(place.core), other, axis - 1)


def split_rows(place, shard):
    half = shard.shape[-2] // 2
    own = pick(shard, place.core, half, shard.ndim - 2)
    other = core_swap(pick(shard, 1 - place.core, half, shard.ndim - 2))
    return both_cores(place, own, other, shard.ndim - 1)


def join_columns(place, block):
    half = block.shape[-2] // 2
    own = pick(block, place.core, half, block.ndim - 2)
    other = core_swap(pick(block, 1 - place.core, half, block.ndim - 2))
    return both_cores(place, own, other, block.ndim - 1)


def join_rows(place, block):
    half = block.shape[-1] // 2
    own = pick(block, place.core, half, block.ndim - 1)
    other = core_swap(pick(block, 1 - place.core, half, block.ndim - 1))
    return both_cores(place, own, other, block.ndim - 2)


def padded_rows(rows):
    return -(-rows // LANES) * LANES


def assemble_kernel(places, items, size, *refs):
    sources = refs[: len(places)]
    outs = refs[len(places) :]
    rows = sources[0].shape[1]
    for (r, first, count), ref in zip(places, sources):

        @pl.when(pl.program_id(0) == r)
        def _(first=first, count=count, ref=ref):
            offset = 0
            for (kind, width), out_ref in zip(items, outs):
                if kind == "folded":
                    half = rows // 2
                    for k in range(count):
                        j = (first + k) * (width + width // 2)
                        out_ref[:, j : j + width] = ref[k, :half, offset : offset + width]
                        out_ref[:, j + width : j + width + width // 2] = ref[
                            k, half:, offset : offset + width // 2
                        ]
                    offset += width
                    continue
                for k in range(count):
                    i = (first + k) * size if kind == "rows" else 0
                    j = (first + k) * width if kind == "columns" else 0
                    out_ref[i : i + rows, j : j + width] = ref[k, :, offset : offset + width]
                    if size > rows:
                        out_ref[i + rows : i + size, j : j + width] = jnp.zeros(
                            (size - rows, width), jnp.bfloat16
                        )
                offset += width


def assemble(place, pieces, items, filled):
    chips, depths = place.chips, place.depths
    rows = pieces[0][2].shape[1]
    size = padded_rows(rows) if filled else rows
    if any(width % LANES for _, width in items):
        matrices = []
        offset = 0
        for kind, width in items:
            arrays = [
                jnp.pad(a[:, :, offset : offset + width], ((0, 0), (0, size - rows), (0, 0)))
                for _, _, a in pieces
            ]
            if kind == "rows":
                arrays = [a.reshape(depths * size, width) for a in arrays]
                matrices.append(jnp.concatenate(arrays, 1))
            else:
                arrays = [jnp.concatenate([a[k] for k in range(depths)], 1) for a in arrays]
                matrices.append(jnp.concatenate(arrays, 0))
            offset += width
        return matrices
    shapes = []
    blocks = []
    for kind, width in items:
        if kind == "rows":
            shapes.append((depths * size, chips * width))
            blocks.append(pl.BlockSpec((depths * size, width), lambda i: (0, i)))
        elif kind == "folded":
            whole = depths * (width + width // 2)
            shapes.append((chips * size // 2, whole))
            blocks.append(pl.BlockSpec((size // 2, whole), lambda i: (i, 0)))
        else:
            shapes.append((chips * size, depths * width))
            blocks.append(pl.BlockSpec((size, depths * width), lambda i: (i, 0)))
    places = [(r, first, array.shape[0]) for r, first, array in pieces]
    return pl.pallas_call(
        functools.partial(assemble_kernel, places, items, size),
        grid=(chips,),
        in_specs=[whole_block(*array.shape) for _, _, array in pieces],
        out_specs=blocks,
        out_shape=[jax.ShapeDtypeStruct(shape, jnp.bfloat16) for shape in shapes],
        **kernel_settings(0, sum(4 * a * b for a, b in shapes)),
    )(*[array for _, _, array in pieces])


def held_for(values, earlier):
    if not earlier:
        return values
    return lax.optimization_barrier((values, *earlier))[0]


class Gather:
    def __init__(self, place):
        self.place = place
        self.near = []
        self.far = []

    def hold(self, values, waits=()):
        return held_for(values, sum(self.near[-1:] + self.far[-2:-1], list(waits)))

    def pieces(self, shard, waits):
        place = self.place
        shard = self.hold(shard, waits)
        stack = lax.all_gather(shard, "mp", axis=0)
        if place.chips == 4:
            half = place.depths // 2
            along = [chip_swap(stack, bit) for bit in (1, 2)]
            across = [chip_swap(along[0][:half], 2), chip_swap(along[1][half:], 1)]
            self.near.append([stack])
            self.far.append(along)
            return [
                (0, 0, stack),
                (1, 0, along[0]),
                (2, 0, along[1]),
                (3, 0, across[0]),
                (3, half, across[1]),
            ]
        pieces = {0: stack}
        for bit in place.bits:
            for r, piece in list(pieces.items()):
                pieces[r ^ bit] = chip_swap(piece, bit)
        self.near.append([stack])
        return [(r, 0, pieces[r]) for r in range(place.chips)]

    def matrices(self, shards, waits=(), filled=False):
        rows = shards[0][1].shape[0]
        folded = [kind == "folded" for kind, _ in shards]
        for index, (kind, shard) in enumerate(shards):
            if kind == "folded":
                third = shard.shape[1] // 3
                if 2 * shard.shape[0] == rows and third % LANES == 0:
                    last = jnp.pad(shard[:, 2 * third :], ((0, 0), (0, third)))
                    shard = jnp.concatenate([shard[:, : 2 * third], last], 0)
                else:
                    kind = "columns"
                shards = shards[:index] + [(kind, shard)] + shards[index + 1 :]
        if len({shard.shape[0] for _, shard in shards}) > 1:
            return [
                self.matrices([item], waits, filled or flag)[0]
                for item, flag in zip(shards, folded)
            ]
        items = [(kind, shard.shape[1]) for kind, shard in shards]
        packed = jnp.concatenate([shard for _, shard in shards], 1)
        return assemble(self.place, self.pieces(packed, waits), items, filled)


def gather_chips(place, shard, bits):
    pieces = {0: shard}
    for bit in bits:
        for r, piece in list(pieces.items()):
            pieces[r ^ bit] = chip_swap(piece, bit)
    return jnp.concatenate([pieces[r] for r in range(place.chips)], -2)


def send_order(place, bits):
    order = [0]
    for bit in reversed(bits):
        order = order + [r ^ bit for r in order]
    return order


def chosen(step, values):
    result = 0
    for index, value in enumerate(values):
        result = result + jnp.where(step == index, value, 0)
    return result


def products_kernel(kinds, rows, *refs):
    out_ref = refs[-1]
    offset = 0
    for index, kind in enumerate(kinds):
        chip_side = refs[2 * index][...]
        depth_side = refs[2 * index + 1][...]
        if kind == "columns":
            block = left_product(chip_side, depth_side)
        else:
            block = left_product(depth_side, chip_side)
        width = block.shape[1]
        out_ref[0, :, offset : offset + width] = to_low(block[:rows])
        offset += width


class Scatter:
    def __init__(self, place):
        self.place = place
        self.near = []
        self.far = []

    def blocks(self, items, rows, chips, depths):
        place = self.place
        steps = [(r, k) for r in chips for k in depths]
        sizes = []
        aligned = True
        for kind, chip_side, depth_side in items:
            a = chip_side.shape[1] // place.chips
            b = depth_side.shape[1] // place.depths
            sizes.append((a, b, b if kind == "columns" else a))
            aligned = aligned and a % LANES == 0 and b % LANES == 0
        if not aligned:
            parts = []
            for (kind, chip_side, depth_side), (a, b, _) in zip(items, sizes):
                if kind == "columns":
                    whole = left_product(chip_side, depth_side)
                    whole = whole.reshape(place.chips, a, place.depths, b).transpose(0, 2, 1, 3)
                else:
                    whole = left_product(depth_side, chip_side)
                    whole = whole.reshape(place.depths, b, place.chips, a).transpose(2, 0, 1, 3)
                parts.append(to_low(whole[:, :, :rows]))
            whole = jnp.concatenate(parts, 3)
            return jnp.stack([jnp.stack([whole[r, k] for k in depths]) for r in chips])
        width = sum(size[2] for size in sizes)
        specs = []
        for (kind, chip_side, depth_side), (a, b, _) in zip(items, sizes):
            count = chip_side.shape[0]
            specs.append(
                pl.BlockSpec((count, a), lambda s: (0, chosen(s, [r for r, _ in steps])))
            )
            specs.append(
                pl.BlockSpec((count, b), lambda s: (0, chosen(s, [k for _, k in steps])))
            )
        count = items[0][1].shape[0]
        out = pl.pallas_call(
            functools.partial(products_kernel, [kind for kind, _, _ in items], rows),
            grid=(len(steps),),
            in_specs=specs,
            out_specs=pl.BlockSpec((1, rows, width), lambda s: (s, 0, 0)),
            out_shape=jax.ShapeDtypeStruct((len(steps), rows, width), jnp.bfloat16),
            **kernel_settings(
                2 * len(steps) * count * rows * width, len(steps) * (rows + count) * width * 2
            ),
        )(*[side for _, *sides in items for side in sides])
        return out.reshape(len(chips), len(depths), rows, width)

    def own(self, items, all_rows, waits=(), reduced=False):
        if len(set(all_rows)) > 1:
            parts = [self.own([item], [n], waits, reduced)[0] for item, n in zip(items, all_rows)]
            return parts
        place = self.place
        rows = all_rows[0]
        kind, chip_side, depth_side = items[0]
        chip_side = held_for(chip_side, sum(self.near[-2:-1] + self.far[-3:-2], list(waits)))
        items = [(kind, chip_side, depth_side)] + list(items[1:])
        half = place.depths // 2
        orders = (place.bits[::-1], place.bits)
        depth_sets = (range(half), range(half, place.depths))
        middle = place.chips // 2
        order_lists = [send_order(place, bits) for bits in orders]
        sents = [
            self.blocks(items, rows, order[middle:], ks)
            for order, ks in zip(order_lists, depth_sets)
        ]
        kepts = [
            self.blocks(items, rows, order[:middle], ks)
            for order, ks in zip(order_lists, depth_sets)
        ]
        got = []
        for step in range(len(place.bits)):
            got = [chip_swap(sent, bits[step]) for sent, bits in zip(sents, orders)]
            sums = [a.astype(jnp.float32) + b.astype(jnp.float32) for a, b in zip(kepts, got)]
            middle = middle // 2
            sents = [to_low(total[middle:]) for total in sums]
            kepts = [total[:middle] for total in sums] if middle else sums
            if step == 0:
                self.near.append(sents)
        by_depth = jnp.concatenate([total[0] for total in kepts], 0)
        if reduced:
            going = to_low(by_depth)
            self.far.append([going])
            total = lax.psum_scatter(going, "mp", scatter_dimension=0).astype(jnp.float32)
        else:
            blocks = [
                lax.dynamic_index_in_dim(by_depth, place.depth ^ k, 0, keepdims=False)
                for k in range(place.depths)
            ]
            going = [to_low(block) for block in blocks[1:]]
            arrived = [depth_swap(block, k + 1) for k, block in enumerate(going)]
            self.far.append(going)
            total = blocks[0]
            for values in arrived:
                total = total + values.astype(jnp.float32)
        parts = []
        offset = 0
        for kind, chip_side, depth_side in items:
            side = (depth_side, place.depths) if kind == "columns" else (chip_side, place.chips)
            width = side[0].shape[1] // side[1]
            parts.append(total[:, offset : offset + width])
            offset += width
        return parts


def core_sum(partial):
    return partial + core_swap(to_low(partial)).astype(jnp.float32)


def core_sum_exact(partial):
    return partial + core_swap(partial)


def parity_part(place, values):
    size = values.shape[1] // (2 * place.chips)
    split = values.reshape(values.shape[0], place.chips, 2, size)
    own = lax.dynamic_index_in_dim(split, place.core, 2, keepdims=False)
    own = jnp.pad(own, ((0, 0), (0, 0), (0, padded_rows(size) - size)))
    return own.reshape(values.shape[0], -1)


def parity_join(place, own, size):
    rows = own.shape[0]
    own = own.reshape(rows, place.chips, -1)[:, :, :size]
    other = core_swap(own)
    return both_cores(place, own[:, :, None], other[:, :, None], 2).reshape(rows, -1)


def other_rows(place, values):
    micro, length, width = values.shape
    halves = values.reshape(micro, 2, length // 2, width)
    return core_swap(lax.dynamic_index_in_dim(halves, 1 - place.core, 1, keepdims=True))


def own_sequence(place, values, other):
    micro, length, width = values.shape
    halves = values.reshape(micro, 2, length // 2, width)
    own = lax.dynamic_index_in_dim(halves, place.core, 1, keepdims=True)
    half = both_cores(place, own, other, 1).reshape(micro * 2, length // 2, width)
    blocks = [
        depth_swap(lax.dynamic_index_in_dim(half, place.depth ^ k, 0, keepdims=False), k)
        for k in range(place.depths)
    ]
    rows = relative_to_chip(place, jnp.concatenate(blocks, 1))
    return both_cores(place, rows, core_swap(rows), 0)


def back_to_all(place, values, micro):
    length = values.shape[0]
    rows = chip_to_relative(place, pick(values, place.core, length // 2, 0))
    width = rows.shape[1] // place.depths
    blocks = [
        depth_swap(rows[:, k * width : (k + 1) * width], k)[None] for k in range(place.depths)
    ]
    by_sequence = reorder(jnp.concatenate(blocks, 0), place.depths, place.depth, 0)
    by_sequence = by_sequence.reshape(micro, 2, length // 2, width)
    own = lax.dynamic_index_in_dim(by_sequence, place.core, 1, keepdims=False)
    other = core_swap(lax.dynamic_index_in_dim(by_sequence, 1 - place.core, 1, keepdims=False))
    return both_cores(place, own, other, 1)


def own_row(place, values):
    both = both_cores(place, values[None], core_swap(values)[None], 0)
    both = jnp.swapaxes(both, 0, 1).reshape((-1,) + values.shape[1:])
    return lax.dynamic_index_in_dim(both, place.depth, 0, keepdims=False)


def own_channels(place, values):
    size = values.shape[-1] // (2 * place.depths)
    return jnp.concatenate(
        [
            pick(values, k * 2 + place.core, size, values.ndim - 1)
            for k in range(place.depths)
        ],
        -1,
    )


def all_channels(place, values):
    size = values.shape[-1] // place.depths
    full = jnp.zeros(values.shape[:-1] + (2 * values.shape[-1],), values.dtype)
    for k in range(place.depths):
        block = values[..., k * size : (k + 1) * size]
        full = lax.dynamic_update_slice_in_dim(
            full, block, (k * 2 + place.core) * size, values.ndim - 1
        )
    return full


def norm_forward(values, gain):
    low = to_low(values)
    wide = low.astype(jnp.float32)
    scale = lax.rsqrt(jnp.mean(wide * wide, axis=-1, keepdims=True) + EPSILON)
    return to_low(wide * scale * gain), (low, scale)


def norm_backward(gradient, memory, gain):
    low, scale = memory
    wide = low.astype(jnp.float32)
    weighted = gradient * gain
    inner = jnp.mean(weighted * wide, axis=-1, keepdims=True)
    grad_gain = jnp.sum(gradient * (wide * scale), axis=0)
    return scale * weighted - wide * (scale * scale * scale * inner), grad_gain


def mamba_forward(place, residual, weights, params, items):
    w_zx, w_bcdt, w_out = weights
    norm, taps, map_taps, heads, channels, owner = params
    columns, ahead, segment_rows = items
    normed_low, norm_memory = norm_forward(residual, norm)
    zx_proj = matmul(normed_low, w_zx)
    bcdt = matmul(normed_low, w_bcdt)
    per_block = channels.shape[1] // place.depths // LANES
    mixed, y, squares, states = mix_forward(
        per_block, zx_proj, bcdt, columns, segment_rows, taps, map_taps, heads, channels
    )
    scale = lax.rsqrt(core_sum_exact(squares) / (2 * mixed.shape[1]) + EPSILON)
    result = residual + core_sum(matmul(mixed, w_out)) * scale
    return (result, (normed_low, mixed, norm_memory, scale, zx_proj, bcdt, y, states))


def mamba_backward(place, gradient, weights, params, items, memory, scatter, more, reduced):
    w_zx, w_bcdt, w_out = weights
    norm, taps, map_taps, heads, channels, owner = params
    columns, ahead, segment_rows = items
    normed_low, mixed, norm_memory, scale, zx_proj, bcdt, y, states = memory
    spread = to_low(gradient)
    grad_mixed = right_product(spread, w_out)
    width = mixed.shape[1]
    inner = core_sum_exact(
        jnp.sum(grad_mixed * mixed.astype(jnp.float32), axis=1, keepdims=True)
    )
    coefficient = scale * scale * scale * inner / (2 * width)
    nothing = jnp.zeros_like(scale[:, 0])
    later = jnp.stack(ahead + [scale[:, 0], coefficient[:, 0], nothing, nothing, nothing], 1)
    grad_zx, grad_maps, grad_dt, grad_taps, grad_map_taps, grad_heads, grad_channels = (
        mix_backward(
            width // place.depths // LANES,
            grad_mixed,
            zx_proj,
            bcdt,
            y,
            states,
            columns,
            later,
            segment_rows,
            taps,
            map_taps,
            heads,
            channels,
            owner,
        )
    )
    head_count = width // HEAD_SIZE
    grad_maps = core_sum_exact(grad_maps)
    own_maps = to_low(pick(grad_maps, place.core, LANES, 1))
    low_dt = to_low(grad_dt)
    grad_bcdt = jnp.concatenate([own_maps, low_dt], 1)
    own_bcdt = jnp.concatenate([pick(w_bcdt, place.core, LANES, 1), w_bcdt[:, 2 * LANES :]], 1)
    partial = right_product(grad_zx, w_zx) + right_product(grad_bcdt, own_bcdt)
    grad_in, grad_norm = norm_backward(core_sum(partial), norm_memory, norm)
    small_from = jnp.concatenate([own_maps, low_dt[:, :head_count]], 1)
    scaled = to_low(spread.astype(jnp.float32) * scale)
    rows = normed_low.shape[1] // place.chips
    weight_grads = scatter.own(
        [("columns", normed_low, grad_zx), ("rows", scaled, mixed)] + more,
        [rows, width // place.depths] + [rows] * len(more),
        [partial],
        reduced,
    )
    by_tap = grad_taps.reshape(4, 8, -1).sum(1)
    map_by_tap = grad_map_taps.reshape(4, 8, -1).sum(1)
    head_sums = grad_heads.reshape(2, 8, -1).sum(1)[:, :head_count]
    channel_sums = grad_channels.reshape(2, 8, -1).sum(1)
    small_grads = (
        0.5 * grad_norm,
        by_tap,
        map_by_tap,
        head_sums[0],
        head_sums[1],
        channel_sums[0].reshape(head_count, HEAD_SIZE).sum(1),
        channel_sums[1],
    )
    return (gradient + grad_in, weight_grads, small_grads, (normed_low, small_from))


def small_scatter(place, pairs, half_maps, waits):
    wholes = []
    for normed, small_from in pairs:
        whole = left_product(normed, small_from)
        maps = jnp.zeros((whole.shape[0], 2 * half_maps), jnp.float32)
        maps = lax.dynamic_update_slice_in_dim(
            maps, whole[:, :half_maps], place.core * half_maps, 1
        )
        wholes += [maps, all_channels(place, whole[:, half_maps:])]
    rows = reorder(jnp.concatenate(wholes, 1), place.chips, place.chip, 0)
    rows = lax.psum(lax.psum_scatter(rows, "dp", scatter_dimension=0, tiled=True), "mp")
    rows = held_for(rows, waits)
    width = rows.shape[1] // 2
    layers = jnp.stack([rows[:, :width], rows[:, width:]])
    steps = layers[:, :, 2 * half_maps :]
    return layers[:, :, : 2 * half_maps], pick(
        steps, place.depth, steps.shape[2] // place.depths, 2
    )


def one_device(
    inputs,
    cotangent,
    boundary_flags,
    segment_ids,
    mamba_norm,
    mamba_z,
    mamba_x,
    mamba_bc,
    mamba_dt,
    mamba_conv_x,
    mamba_conv_bc,
    mamba_dt_bias,
    mamba_a_log,
    mamba_skip,
    mamba_gate_norm,
    mamba_out,
    router_qk,
    group_up,
    group_down,
    attn_norms,
    attn_qkv,
    attn_out,
    ffn_gate_up,
    ffn_down,
):
    place = Place()
    micro = inputs.shape[0]
    wide = jnp.float32

    zx_shard = split_columns(place, [mamba_z[0], mamba_x[0]])
    gather = Gather(place)
    (enc_zx,) = gather.matrices([("columns", zx_shard)])
    residual_low = own_sequence(place, inputs, other_rows(place, inputs))
    residual = residual_low.astype(wide)

    mamba_bc, mamba_dt, mamba_out, router_qk, _ = lax.optimization_barrier(
        (mamba_bc, mamba_dt, mamba_out, router_qk, zx_shard)
    )
    out_shard = split_rows(place, mamba_out)
    router_shard = split_columns(place, [router_qk[0], router_qk[1]])
    qkv_shard = split_columns(place, [attn_qkv[0], attn_qkv[1], attn_qkv[2]])
    qkv_packed = jnp.pad(qkv_shard, ((0, 0), (0, -qkv_shard.shape[1] % LANES)))
    router_shard, qkv_packed, attn_out_shard, ffn_shard, ffn_down_shard = lax.optimization_barrier(
        (
            router_shard,
            qkv_packed,
            split_rows(place, attn_out),
            split_columns(place, [ffn_gate_up[0], ffn_gate_up[1]]),
            split_rows(place, ffn_down),
        )
    )
    enc_out, w_router, w_up = gather.matrices(
        [("rows", out_shard[0]), ("columns", router_shard), ("folded", group_up)]
    )
    dt_shard = split_columns(place, [mamba_dt])
    dt_shard = jnp.concatenate([depth_swap(dt_shard, k) for k in range(place.depths)], -1)
    dt_shard = reorder(dt_shard, place.depths, place.depth)
    bc_shard = both_cores(place, mamba_bc, core_swap(mamba_bc), 1)
    fill = jnp.zeros(dt_shard.shape[:2] + (LANES - dt_shard.shape[2],), jnp.bfloat16)
    w_bcdt = gather_chips(place, jnp.concatenate([bc_shard, dt_shard, fill], -1), place.bits)
    enc_weights = (enc_zx, w_bcdt[0], enc_out)
    (w_qkv,) = gather.matrices([("columns", qkv_packed)])
    w_attn_out, w_down = gather.matrices(
        [("rows", attn_out_shard), ("columns", group_down)], filled=True
    )
    boundary_flags, segment_ids = lax.optimization_barrier(
        (boundary_flags, segment_ids, w_bcdt)
    )[:2]
    flag_row = own_row(place, boundary_flags)
    segment = own_row(place, segment_ids)

    mamba_params = []
    for layer in range(2):
        taps = own_channels(place, mamba_conv_x[layer]).astype(wide)
        width = taps.shape[1]
        bias = own_channels(place, mamba_dt_bias[layer]).astype(wide)
        rate = -jnp.exp(own_channels(place, mamba_a_log[layer]).astype(wide))
        skip = own_channels(place, mamba_skip[layer]).astype(wide)
        gain = own_channels(place, mamba_gate_norm[layer]).astype(wide)
        heads = jnp.pad(jnp.stack([bias, rate]), ((0, 6), (0, LANES - bias.shape[0])))
        channels = jnp.pad(jnp.stack([jnp.repeat(skip, HEAD_SIZE), gain]), ((0, 6), (0, 0)))
        owner = (
            jnp.arange(width)[:, None] // HEAD_SIZE == jnp.arange(LANES)[None, :]
        ).astype(jnp.bfloat16)
        mamba_params.append(
            (
                reorder(mamba_norm[layer], place.chips, place.chip).astype(wide),
                taps,
                mamba_conv_bc[layer].astype(wide),
                heads,
                channels,
                owner,
            )
        )
    items = item_columns(segment)
    norm_gains = reorder(attn_norms, place.chips, place.chip).astype(wide)

    starts = jnp.concatenate([jnp.ones((1,), jnp.bool_), segment[1:] != segment[:-1]])
    group_rank = jnp.cumsum(flag_row) - 1
    slots = jnp.arange(CAP, dtype=jnp.int32)
    marked = (group_rank[None, :] == slots[:, None]) & (flag_row[None, :] == 1)
    marked_low = marked.astype(jnp.bfloat16)
    slot_valid = jnp.any(marked, axis=1)
    encoded, enc_memory = mamba_forward(
        place, residual, enc_weights, mamba_params[0], items
    )

    (w_gate_up,) = gather.matrices([("columns", ffn_shard)], [enc_memory[4]])
    (w_ffn_down,) = gather.matrices([("rows", ffn_down_shard)], [enc_memory[1]])

    shared = to_low(encoded)
    length = shared.shape[0]
    qk = matmul(shared, w_router)
    all_dots = core_sum_exact(pair_dots(qk, place.depths))
    prob_row, prob_back = jax.vjp(lambda values: boundary_prob(values.T, starts), all_dots)


    group_rows = to_low(matmul(marked_low, shared))
    group_seg = jnp.sum(jnp.where(marked, segment[None, :] + 1, 0), axis=1) - 1
    own_rows = parity_part(place, group_rows)
    hidden = depth_to_chip(place, core_sum(matmul(own_rows, w_up)))

    dec_shard = split_columns(place, [mamba_z[1], mamba_x[1]])
    dec_zx, dec_out = gather.matrices(
        [("columns", dec_shard), ("rows", out_shard[1])], [qk]
    )
    dec_weights = (dec_zx, w_bcdt[1], dec_out)

    first_low, first_memory = norm_forward(hidden, norm_gains[0])
    qkv = matmul(first_low, w_qkv)
    tables = turn_tables(CAP)
    attended_low = attend(qkv, None, tables, group_seg, place.depths)
    hidden_one = hidden + core_sum(matmul(attended_low, w_attn_out))

    cotangent = gather.hold(cotangent, [hidden_one])
    cot_row = own_sequence(place, cotangent, other_rows(place, cotangent)).astype(wide)

    second_low, second_memory = norm_forward(hidden_one, norm_gains[1])
    gate_up = matmul(second_low, w_gate_up)
    active_low = activate(gate_up, None, place.depths)
    hidden_two = hidden_one + core_sum(matmul(active_low, w_ffn_down))
    third_low = parity_part(place, to_low(hidden_two))
    down_rows = depth_to_chip(place, core_sum(matmul(third_low, w_down)))

    group_probs = jnp.sum(jnp.where(marked, prob_row[None, :], 0.0), axis=1)
    group_probs = jnp.pad(jnp.where(slot_valid, group_probs, 1.0), (0, 8))
    confidence = jnp.where(flag_row == 1, prob_row, 1.0 - prob_row)[:, None]
    rank_column = group_rank[:, None]
    decoder_in, smooth = smooth_forward(group_probs, down_rows, encoded, confidence, rank_column)
    decoded, dec_memory = mamba_forward(
        place, decoder_in, dec_weights, mamba_params[1], items
    )
    outputs = back_to_all(place, to_low(decoded), micro)

    scatter = Scatter(place)
    gradient, dec_grads, dec_smalls, dec_maps = mamba_backward(
        place,
        cot_row,
        dec_weights,
        mamba_params[1],
        items,
        dec_memory,
        scatter,
        [],
        True,
    )
    grad_down, grad_confidence, grad_slots = smooth_backward(
        group_probs, gradient, confidence, rank_column, smooth, down_rows
    )
    grad_probs = jnp.where(flag_row == 1, grad_confidence[:, 0], -grad_confidence[:, 0])
    grad_probs = grad_probs + jnp.sum(jnp.where(marked, grad_slots, 0.0), axis=0)

    dm_rows = hidden.shape[1] // place.chips
    down_low = depth_to_chip(place, grad_down)
    grad_third = to_low(right_product(down_low, w_down))
    grad_hidden = parity_join(place, grad_third, dm_rows // 2).astype(wide)
    spread = to_low(grad_hidden)
    grad_pairs = activate(gate_up, right_product(spread, w_ffn_down), place.depths)
    (own_ffn_down,) = scatter.own(
        [("rows", spread, active_low)], [active_low.shape[1] // place.depths], [grad_pairs], True
    )
    partial = right_product(grad_pairs, w_gate_up)
    (own_gate_up,) = scatter.own(
        [("columns", second_low, grad_pairs)], [dm_rows], [partial], True
    )
    grad_second, grad_norm_two = norm_backward(core_sum(partial), second_memory, norm_gains[1])
    grad_hidden = grad_hidden + grad_second

    spread = to_low(grad_hidden)
    grad_attended = right_product(spread, w_attn_out)
    grad_qkv = attend(qkv, grad_attended, tables, group_seg, place.depths)
    own_attn_out, own_down = scatter.own(
        [("rows", spread, attended_low), ("columns", third_low, down_low)],
        [HEADS_PER_BLOCK * HEAD_SIZE, dm_rows // 2],
        [grad_qkv],
    )
    partial = right_product(grad_qkv, w_qkv)
    (own_qkv,) = scatter.own([("columns", first_low, grad_qkv)], [dm_rows], [partial])
    grad_first, grad_norm_one = norm_backward(core_sum(partial), first_memory, norm_gains[0])
    grad_hidden = grad_hidden + grad_first

    hidden_low = depth_to_chip(place, to_low(grad_hidden))
    d_rows = shared.shape[1] // place.chips
    partial = to_low(right_product(hidden_low, w_up))
    (own_up,) = scatter.own([("columns", own_rows, hidden_low)], [d_rows // 2], [partial])
    grad_rows = parity_join(place, partial, d_rows // 2)
    grad_shared = left_product(marked_low, grad_rows)
    (grad_dots,) = prob_back(grad_probs)
    grad_qk = pair_dots_back(qk, grad_dots, place.depths)
    partial = right_product(grad_qk, w_router)
    grad_shared = grad_shared + core_sum(partial)
    gradient = gradient + grad_shared

    gradient, enc_grads, enc_smalls, enc_maps = mamba_backward(
        place,
        gradient,
        enc_weights,
        mamba_params[0],
        items,
        enc_memory,
        scatter,
        [("columns", shared, grad_qk)],
        False,
    )
    grad_inputs = back_to_all(place, to_low(gradient), micro).astype(wide)

    parts = []
    for smalls in (enc_smalls, dec_smalls):
        parts += [
            reorder(smalls[0], place.chips, place.chip),
            all_channels(place, smalls[1]),
            smalls[2],
            all_channels(place, smalls[3]),
            all_channels(place, smalls[4]),
            all_channels(place, smalls[5]),
            all_channels(place, smalls[6]),
        ]
    parts.append(0.5 * reorder(grad_norm_one, place.chips, place.chip))
    parts.append(0.5 * reorder(grad_norm_two, place.chips, place.chip))
    flat = jnp.concatenate([part.reshape(-1) for part in parts])
    fill = -flat.shape[0] % 1024
    flat = jnp.pad(flat, (0, fill)).reshape(-1, 128)
    flat = held_for(lax.psum(flat, ("dp", "mp")), scatter.far[-1]).reshape(-1)
    summed = []
    offset = 0
    for part in parts:
        summed.append(flat[offset : offset + part.size].reshape(part.shape))
        offset += part.size
    smalls = [jnp.stack([summed[n], summed[7 + n]]) for n in range(7)]

    grad_bc, grad_dt = small_scatter(place, [enc_maps, dec_maps], LANES, scatter.far[-1])

    def kinds(blocks, count):
        return join_columns(place, jnp.stack(jnp.split(blocks, count, 1)))

    enc_parts = kinds(enc_grads[0], 2)
    dec_parts = kinds(dec_grads[0], 2)
    qkv_width = qkv_shard.shape[1]
    return (
        outputs,
        grad_inputs,
        smalls[0],
        jnp.stack([enc_parts[0], dec_parts[0]]),
        jnp.stack([enc_parts[1], dec_parts[1]]),
        grad_bc,
        grad_dt,
        smalls[1],
        smalls[2],
        smalls[3],
        smalls[4],
        smalls[5],
        smalls[6],
        join_rows(place, jnp.stack([enc_grads[1], dec_grads[1]])),
        kinds(enc_grads[2], 2),
        own_up,
        own_down,
        jnp.stack([summed[14], summed[15]]),
        kinds(own_qkv[:, :qkv_width], 3),
        join_rows(place, own_attn_out),
        kinds(own_gate_up, 2),
        join_rows(place, own_ffn_down),
    )


def solution(mesh):
    in_specs = (
        P(None, "dp", "mp"),
        P(None, "dp", "mp"),
        P(None, "dp"),
        P(None, "dp"),
        P(),
        P(None, "dp", "mp"),
        P(None, "dp", "mp"),
        P(None, "dp", None),
        P(None, "dp", "mp"),
        P(),
        P(),
        P(),
        P(),
        P(),
        P(),
        P(None, "mp", "dp"),
        P(None, "dp", "mp"),
        P("dp", "mp"),
        P("dp", "mp"),
        P(),
        P(None, "dp", "mp"),
        P("mp", "dp"),
        P(None, "dp", "mp"),
        P("mp", "dp"),
    )
    out_specs = (
        P(None, "dp", "mp"),
        P(None, "dp", "mp"),
        P(),
        P(None, "dp", "mp"),
        P(None, "dp", "mp"),
        P(None, "dp", None),
        P(None, "dp", "mp"),
        P(),
        P(),
        P(),
        P(),
        P(),
        P(),
        P(None, "mp", "dp"),
        P(None, "dp", "mp"),
        P("dp", "mp"),
        P("dp", "mp"),
        P(),
        P(None, "dp", "mp"),
        P("mp", "dp"),
        P(None, "dp", "mp"),
        P("mp", "dp"),
    )
    return jax.shard_map(
        one_device, mesh=mesh, in_specs=in_specs, out_specs=out_specs, check_vma=False
    )
```

```python
import functools

import jax
import jax.numpy as jnp
from jax import lax
from jax.experimental import pallas as pl
from jax.experimental.pallas import tpu as pltpu
from jax.sharding import PartitionSpec as P

DM = 1536
AHEADS = 24
CAP = 320


EPSILON = 1e-06
HIGHEST = lax.Precision.HIGHEST


def boundary_prob(all_dots, starts):
    cosine = all_dots[0] * lax.rsqrt(all_dots[1] + EPSILON) * lax.rsqrt(all_dots[2] + EPSILON)
    return jnp.where(starts, 1.0, 0.5 * (1.0 - cosine))


def to_low(values):
    return values.astype(jnp.bfloat16)


def matmul(left, right):
    return jnp.dot(left, right, preferred_element_type=jnp.float32)


def left_product(left, right):
    return lax.dot_general(
        left, right, (((0,), (0,)), ((), ())), preferred_element_type=jnp.float32
    )


def right_product(left, right):
    return lax.dot_general(
        left, right, (((1,), (1,)), ((), ())), preferred_element_type=jnp.float32
    )


BLOCK = 128
LANES = 128
HEAD_SIZE = 64


def sigmoid(values):
    return 1.0 / (1.0 + jnp.exp(-values))


def split_product(values, ones_low):
    high = to_low(values)
    rest = to_low(values - high.astype(jnp.float32))
    return matmul(high, ones_low) + matmul(rest, ones_low)


def exact_product(left, right):
    return jnp.dot(left, right, precision=HIGHEST, preferred_element_type=jnp.float32)


def shifted_down(tail, block, steps):
    joined = jnp.concatenate([tail, block], 0)
    return pltpu.roll(joined, steps, 0)[8:]


def shifted_up(block, head, steps):
    joined = jnp.concatenate([block, head], 0)
    size = joined.shape[0]
    return pltpu.roll(joined, size - steps, 0)[: size - 8]


def filtered(tail, block, taps, columns):
    result = block * taps[3:4]
    for steps in range(1, 4):
        moved = shifted_down(tail, block, steps)
        result = result + moved * columns[:, steps - 1 : steps] * taps[3 - steps : 4 - steps]
    return result


def pair_columns(values, pair, first_half):
    return jnp.where(
        first_half, values[:, 2 * pair : 2 * pair + 1], values[:, 2 * pair + 1 : 2 * pair + 2]
    )


def stacked_halves(values, first_half):
    zero = jnp.zeros_like(values)
    return jnp.concatenate(
        [jnp.where(first_half, values, zero), jnp.where(first_half, zero, values)], 0
    )


def folded_rows(values):
    return jnp.sum(values.reshape(values.shape[0] // 8, 8, values.shape[1]), axis=0)


class Decay:
    def __init__(self, dt_raw, dt_bias, rate, columns, segment_row):
        rows = lax.broadcasted_iota(jnp.int32, (BLOCK, BLOCK), 0)
        cols = lax.broadcasted_iota(jnp.int32, (BLOCK, BLOCK), 1)
        self.lower = rows >= cols
        shifted = dt_raw + dt_bias
        self.steepness = sigmoid(shifted)
        self.step = jnp.maximum(shifted, 0.0) + jnp.log(1.0 + jnp.exp(-jnp.abs(shifted)))
        self.decay = rate * self.step
        self.total = exact_product(self.lower.astype(jnp.float32), self.decay)
        self.total_rows = self.total.T
        same = self.lower & (columns[:, 3:4] == segment_row)
        self.mask = jnp.where(same, 0.0, -1e30)
        last = self.total[BLOCK - 1 : BLOCK]
        self.reach = jnp.exp(self.total) * columns[:, 4:5]
        self.to_end = jnp.exp(last - self.total) * columns[:, 5:6]
        self.kept = jnp.exp(last) * columns[BLOCK - 1 : BLOCK, 4:5]

    def factor(self, head):
        return jnp.exp(
            self.total[:, head : head + 1] - self.total_rows[head : head + 1] + self.mask
        )


def zx_lanes(pair, per_block):
    block, tile = divmod(pair, per_block)
    start = (2 * block * per_block + tile) * LANES
    shift = per_block * LANES
    return slice(start, start + LANES), slice(start + shift, start + shift + LANES)


def mix_kernel(
    per_block,
    zx_ref,
    bcdt_ref,
    columns_ref,
    segment_ref,
    taps_ref,
    map_taps_ref,
    heads_ref,
    channels_ref,
    mixed_ref,
    y_ref,
    square_ref,
    states_ref,
    state,
    tail_x,
    tail_maps,
    ends,
):
    pairs = channels_ref.shape[1] // LANES

    @pl.when(pl.program_id(0) == 0)
    def _():
        state[...] = jnp.zeros_like(state)
        tail_x[...] = jnp.zeros_like(tail_x)
        tail_maps[...] = jnp.zeros_like(tail_maps)

    columns = columns_ref[...]
    first_half = lax.broadcasted_iota(jnp.int32, (1, LANES), 1) < HEAD_SIZE
    maps_in = bcdt_ref[:, : 2 * LANES]
    maps = filtered(tail_maps[...], maps_in, map_taps_ref[...], columns)
    maps = maps * sigmoid(maps)
    in_map = to_low(maps[:, :LANES])
    out_map = to_low(maps[:, LANES:])
    heads = heads_ref[...]
    decay = Decay(
        bcdt_ref[:, 2 * LANES :], heads[0:1], heads[1:2], columns, segment_ref[0, 0:1, :]
    )
    meeting = right_product(out_map, in_map)
    low_state = to_low(state[...])
    states_ref[...] = low_state
    y_ref[...] = matmul(out_map, low_state)
    squares = jnp.zeros((BLOCK, LANES), jnp.float32)
    for pair in range(pairs):
        lanes = slice(pair * LANES, (pair + 1) * LANES)
        z_lanes, x_lanes = zx_lanes(pair, per_block)
        block = zx_ref[:, x_lanes]
        pre = filtered(tail_x[:, lanes], block, taps_ref[:, lanes], columns)
        tail_x[:, lanes] = block[BLOCK - 8 :]
        value = pre * sigmoid(pre)
        scaled = value * pair_columns(decay.step, pair, first_half)
        ends[:, lanes] = to_low(scaled * pair_columns(decay.to_end, pair, first_half))
        weights = jnp.concatenate(
            [to_low(meeting * decay.factor(2 * pair + half)) for half in range(2)], 1
        )
        y = matmul(weights, stacked_halves(to_low(scaled), first_half))
        y = y + y_ref[:, lanes] * pair_columns(decay.reach, pair, first_half)
        y_ref[:, lanes] = y
        gate_in = zx_ref[:, z_lanes]
        gated = (y + channels_ref[0:1, lanes] * value) * (gate_in * sigmoid(gate_in))
        squares = squares + gated * gated
        mixed_ref[:, lanes] = to_low(gated * channels_ref[1:2, lanes])
        state[:, lanes] = state[:, lanes] * pair_columns(decay.kept, pair, first_half)
    square_ref[...] = jnp.sum(squares, axis=1, keepdims=True)
    state[...] += left_product(in_map, ends[...])
    tail_maps[...] = bcdt_ref[BLOCK - 8 :, : 2 * LANES]


def mix_back_kernel(
    per_block,
    grad_ref,
    zx_ref,
    zx_tail_ref,
    bcdt_ref,
    maps_tail_ref,
    y_ref,
    states_ref,
    columns_ref,
    later_ref,
    segment_ref,
    taps_ref,
    map_taps_ref,
    heads_ref,
    channels_ref,
    owner_ref,
    grad_zx_ref,
    grad_maps_ref,
    grad_dt_ref,
    grad_taps_ref,
    grad_map_taps_ref,
    grad_heads_ref,
    grad_channels_ref,
    grad_state,
    head_x,
    head_maps,
    ends,
    reached,
    pulled,
    balance,
    step_part,
):
    pairs = channels_ref.shape[1] // LANES
    step = pl.program_id(0)
    first_chunk = step == pl.num_programs(0) - 1

    @pl.when(step == 0)
    def _():
        grad_state[...] = jnp.zeros_like(grad_state)
        head_x[...] = jnp.zeros_like(head_x)
        head_maps[...] = jnp.zeros_like(head_maps)
        grad_taps_ref[...] = jnp.zeros_like(grad_taps_ref)
        grad_map_taps_ref[...] = jnp.zeros_like(grad_map_taps_ref)
        grad_heads_ref[...] = jnp.zeros_like(grad_heads_ref)
        grad_channels_ref[...] = jnp.zeros_like(grad_channels_ref)

    columns = columns_ref[...]
    later = later_ref[...]
    first_half = lax.broadcasted_iota(jnp.int32, (1, LANES), 1) < HEAD_SIZE
    tail_maps = jnp.where(first_chunk, 0.0, maps_tail_ref[:, : 2 * LANES])
    maps_in = bcdt_ref[:, : 2 * LANES]
    maps_pre = filtered(tail_maps, maps_in, map_taps_ref[...], columns)
    maps_open = sigmoid(maps_pre)
    maps = maps_pre * maps_open
    in_map = to_low(maps[:, :LANES])
    out_map = to_low(maps[:, LANES:])
    heads = heads_ref[...]
    decay = Decay(
        bcdt_ref[:, 2 * LANES :], heads[0:1], heads[1:2], columns, segment_ref[0, 0:1, :]
    )
    meeting = right_product(out_map, in_map)
    low_grad_state = to_low(grad_state[...])
    pulled[...] = matmul(in_map, low_grad_state)
    scale = later[:, 3:4]
    coefficient = later[:, 4:5]
    grad_meeting = jnp.zeros((BLOCK, BLOCK), jnp.float32)
    for pair in range(pairs):
        lanes = slice(pair * LANES, (pair + 1) * LANES)
        z_lanes, x_lanes = zx_lanes(pair, per_block)
        tail = jnp.where(first_chunk, 0.0, zx_tail_ref[:, x_lanes])
        block = zx_ref[:, x_lanes]
        taps = taps_ref[:, lanes]
        pre = filtered(tail, block, taps, columns)
        opened = sigmoid(pre)
        value = pre * opened
        slope = opened + value * (1.0 - opened)
        gate_in = zx_ref[:, z_lanes]
        gate_open = sigmoid(gate_in)
        gate = gate_in * gate_open
        skip = channels_ref[0:1, lanes]
        gain = channels_ref[1:2, lanes]
        y = y_ref[:, lanes]
        whole = y + skip * value
        gated = whole * gate
        grad_mixed = grad_ref[:, lanes]
        grad_gated = scale * (grad_mixed * gain) - coefficient * gated
        grad_channels_ref[8:16, lanes] += folded_rows(grad_mixed * gated * scale)
        grad_y = grad_gated * gate
        grad_zx_ref[:, z_lanes] = to_low(
            grad_gated * whole * (gate_open + gate * (1.0 - gate_open))
        )
        grad_channels_ref[0:8, lanes] += folded_rows(grad_y * value)
        low_grad_y = to_low(grad_y)
        reached[:, lanes] = to_low(grad_y * pair_columns(decay.reach, pair, first_half))
        step_wide = pair_columns(decay.step, pair, first_half)
        scaled = value * step_wide
        low_scaled = to_low(scaled)
        end_wide = pair_columns(decay.to_end, pair, first_half)
        ends[:, lanes] = to_low(scaled * end_wide)
        stacked = stacked_halves(low_grad_y, first_half)
        grad_weights = right_product(stacked, low_scaled)
        parts = []
        for half in range(2):
            factor = decay.factor(2 * pair + half)
            grad_meeting = (
                grad_meeting + factor * grad_weights[half * BLOCK : (half + 1) * BLOCK]
            )
            parts.append(to_low(meeting * factor))
        from_end = pulled[:, lanes] * end_wide
        grad_scaled = left_product(jnp.concatenate(parts, 0), stacked) + from_end
        wide_scaled = low_scaled.astype(jnp.float32)
        balance[:BLOCK, lanes] = low_grad_y.astype(jnp.float32) * y - wide_scaled * grad_scaled
        step_part[:, lanes] = to_low(grad_scaled * value)
        kept = pair_columns(decay.kept, pair, first_half)
        kept_state = grad_state[:, lanes] * kept
        balance[BLOCK : BLOCK + 8, lanes] = folded_rows(wide_scaled * from_end) + folded_rows(
            kept_state * states_ref[:, lanes].astype(jnp.float32)
        )
        grad_state[:, lanes] = kept_state
        grad_pre = (grad_scaled * step_wide + grad_y * skip) * slope
        grad_taps_ref[24:32, lanes] += folded_rows(grad_pre * block)
        grad_x = grad_pre * taps[3:4]
        head = head_x[:, lanes]
        for steps in range(1, 4):
            moved = shifted_down(tail, block, steps)
            grad_taps_ref[24 - 8 * steps : 32 - 8 * steps, lanes] += folded_rows(
                grad_pre * columns[:, steps - 1 : steps] * moved
            )
            grad_x = grad_x + (
                shifted_up(grad_pre, head, steps)
                * later[:, steps - 1 : steps]
                * taps[3 - steps : 4 - steps]
            )
        grad_zx_ref[:, x_lanes] = to_low(grad_x)
        head_x[:, lanes] = grad_pre[:8]

    owner = owner_ref[...]
    grad_total = split_product(balance[:BLOCK, :], owner)
    end_rows = split_product(balance[BLOCK : BLOCK + 8, :], owner)
    end_total = jnp.sum(end_rows, axis=0, keepdims=True)
    rows = lax.broadcasted_iota(jnp.int32, (BLOCK, LANES), 0)
    grad_total = grad_total + jnp.where(rows == BLOCK - 1, end_total, 0.0)
    upper = jnp.where(rows <= lax.broadcasted_iota(jnp.int32, (BLOCK, LANES), 1), 1.0, 0.0)
    grad_decay = exact_product(upper, grad_total)
    grad_step = matmul(step_part[...], owner) + grad_decay * heads[1:2]
    grad_raw = grad_step * decay.steepness
    grad_dt_ref[...] = grad_raw
    grad_heads_ref[0:8, :] += folded_rows(grad_raw)
    grad_heads_ref[8:16, :] += folded_rows(grad_decay * decay.decay)

    low_meeting = to_low(grad_meeting)
    grad_out_map = matmul(low_meeting, in_map) + right_product(reached[...], states_ref[...])
    grad_in_map = left_product(low_meeting, out_map) + right_product(ends[...], low_grad_state)
    grad_state[...] += left_product(out_map, reached[...])
    grad_pre = jnp.concatenate([grad_in_map, grad_out_map], 1) * (
        maps_open + maps * (1.0 - maps_open)
    )
    map_taps = map_taps_ref[...]
    grad_map_taps_ref[24:32, :] += folded_rows(grad_pre * maps_in)
    grad_maps = grad_pre * map_taps[3:4]
    head = head_maps[...]
    for steps in range(1, 4):
        moved = shifted_down(tail_maps, maps_in, steps)
        grad_map_taps_ref[24 - 8 * steps : 32 - 8 * steps, :] += folded_rows(
            grad_pre * columns[:, steps - 1 : steps] * moved
        )
        grad_maps = grad_maps + (
            shifted_up(grad_pre, head, steps)
            * later[:, steps - 1 : steps]
            * map_taps[3 - steps : 4 - steps]
        )
    grad_maps_ref[...] = grad_maps
    head_maps[...] = grad_pre[:8]


def whole_block(*shape):
    return pl.BlockSpec(shape, lambda step: (0,) * len(shape))


def mix_settings(length, channels, work):
    return dict(
        compiler_params=pltpu.CompilerParams(
            dimension_semantics=("arbitrary",), vmem_limit_bytes=48 * 1024 * 1024
        ),
        cost_estimate=pl.CostEstimate(
            flops=work * length * channels * BLOCK,
            bytes_accessed=length * channels * 16,
            transcendentals=length * channels * 4,
        ),
    )


def mix_forward(
    per_block, zx_proj, bcdt, columns, segment_rows, taps, map_taps, heads, channels
):
    length = zx_proj.shape[0]
    width = channels.shape[1]
    chunks = length // BLOCK

    def rows(size):
        return pl.BlockSpec((BLOCK, size), lambda step: (step, 0))

    return pl.pallas_call(
        functools.partial(mix_kernel, per_block),
        grid=(chunks,),
        in_specs=[
            rows(2 * width),
            rows(3 * LANES),
            rows(8),
            pl.BlockSpec((1, 8, BLOCK), lambda step: (step, 0, 0)),
            whole_block(4, width),
            whole_block(4, 2 * LANES),
            whole_block(8, LANES),
            whole_block(8, width),
        ],
        out_specs=[rows(width), rows(width), rows(1), rows(width)],
        out_shape=[
            jax.ShapeDtypeStruct((length, width), jnp.bfloat16),
            jax.ShapeDtypeStruct((length, width), jnp.float32),
            jax.ShapeDtypeStruct((length, 1), jnp.float32),
            jax.ShapeDtypeStruct((chunks * LANES, width), jnp.bfloat16),
        ],
        scratch_shapes=[
            pltpu.VMEM((LANES, width), jnp.float32),
            pltpu.VMEM((8, width), jnp.float32),
            pltpu.VMEM((8, 2 * LANES), jnp.float32),
            pltpu.VMEM((BLOCK, width), jnp.bfloat16),
        ],
        **mix_settings(length, width, 8),
    )(zx_proj, bcdt, columns, segment_rows, taps, map_taps, heads, channels)


def mix_backward(
    per_block,
    grad_mixed,
    zx_proj,
    bcdt,
    y,
    states,
    columns,
    later,
    segment_rows,
    taps,
    map_taps,
    heads,
    channels,
    owner,
):
    length, width = grad_mixed.shape
    chunks = length // BLOCK
    eighths = BLOCK // 8

    def rows(size):
        return pl.BlockSpec((BLOCK, size), lambda step: (chunks - 1 - step, 0))

    def before(size):
        return pl.BlockSpec(
            (8, size), lambda step: (jnp.maximum((chunks - 1 - step) * eighths - 1, 0), 0)
        )

    low = jnp.bfloat16
    wide = jnp.float32
    return pl.pallas_call(
        functools.partial(mix_back_kernel, per_block),
        grid=(chunks,),
        in_specs=[
            rows(width),
            rows(2 * width),
            before(2 * width),
            rows(3 * LANES),
            before(3 * LANES),
            rows(width),
            rows(width),
            rows(8),
            rows(8),
            pl.BlockSpec((1, 8, BLOCK), lambda step: (chunks - 1 - step, 0, 0)),
            whole_block(4, width),
            whole_block(4, 2 * LANES),
            whole_block(8, LANES),
            whole_block(8, width),
            whole_block(width, LANES),
        ],
        out_specs=[
            rows(2 * width),
            rows(2 * LANES),
            rows(LANES),
            whole_block(32, width),
            whole_block(32, 2 * LANES),
            whole_block(16, LANES),
            whole_block(16, width),
        ],
        out_shape=[
            jax.ShapeDtypeStruct((length, 2 * width), low),
            jax.ShapeDtypeStruct((length, 2 * LANES), wide),
            jax.ShapeDtypeStruct((length, LANES), wide),
            jax.ShapeDtypeStruct((32, width), wide),
            jax.ShapeDtypeStruct((32, 2 * LANES), wide),
            jax.ShapeDtypeStruct((16, LANES), wide),
            jax.ShapeDtypeStruct((16, width), wide),
        ],
        scratch_shapes=[
            pltpu.VMEM((LANES, width), wide),
            pltpu.VMEM((8, width), wide),
            pltpu.VMEM((8, 2 * LANES), wide),
            pltpu.VMEM((BLOCK, width), low),
            pltpu.VMEM((BLOCK, width), low),
            pltpu.VMEM((BLOCK, width), wide),
            pltpu.VMEM((BLOCK + 8, width), wide),
            pltpu.VMEM((BLOCK, width), low),
        ],
        **mix_settings(length, width, 24),
    )(
        grad_mixed,
        zx_proj,
        zx_proj,
        bcdt,
        bcdt,
        y,
        states,
        columns,
        later,
        segment_rows,
        taps,
        map_taps,
        heads,
        channels,
        owner,
    )


def item_columns(segment):
    length = segment.shape[0]
    back = []
    ahead = []
    for steps in range(1, 4):
        same = segment[steps:] == segment[:-steps]
        none = jnp.zeros((steps,), jnp.bool_)
        back.append(jnp.concatenate([none, same]))
        ahead.append(jnp.concatenate([same, none]))
    blocks = segment.reshape(-1, BLOCK)
    last = blocks[:, BLOCK - 1]
    before = jnp.concatenate([jnp.full((1,), -1, segment.dtype), last[:-1]])
    carried = (blocks == before[:, None]).reshape(-1)
    ending = (blocks == last[:, None]).reshape(-1)
    wide = jnp.float32
    nothing = jnp.zeros((length,), wide)
    columns = jnp.stack(
        [b.astype(wide) for b in back]
        + [segment.astype(wide), carried.astype(wide), ending.astype(wide), nothing, nothing],
        1,
    )
    rows = jnp.broadcast_to(blocks.astype(wide)[:, None, :], (blocks.shape[0], 8, BLOCK))
    return columns, [a.astype(wide) for a in ahead], rows


SLOTS = 384


def smooth_kernel(probs_ref, down_ref, encoded_ref, confidence_ref, rank_ref, out_ref, smooth_ref, high, rest):
    count = down_ref.shape[0]

    @pl.when(pl.program_id(0) == 0)
    def _():
        high[count:, :] = jnp.zeros((SLOTS - count, high.shape[1]), jnp.bfloat16)
        rest[count:, :] = jnp.zeros((SLOTS - count, high.shape[1]), jnp.bfloat16)

        def tile(index, previous):
            start = pl.multiple_of(index * 8, 8)
            rows = down_ref[pl.ds(start, 8), :]
            done = []
            for r in range(8):
                prob = probs_ref[start + r]
                previous = prob * rows[r : r + 1] + (1.0 - prob) * previous
                done.append(previous)
            smooth_ref[pl.ds(start, 8), :] = jnp.concatenate(done, 0)
            return previous

        lax.fori_loop(0, count // 8, tile, jnp.zeros((1, down_ref.shape[1]), jnp.float32))
        smooth = smooth_ref[...]
        low = to_low(smooth)
        high[:count, :] = low
        rest[:count, :] = to_low(smooth - low.astype(jnp.float32))

    slots = lax.broadcasted_iota(jnp.int32, (BLOCK, SLOTS), 1)
    chosen = jnp.where(slots == rank_ref[...], 1.0, 0.0).astype(jnp.bfloat16)
    spread = matmul(chosen, high[...]) + matmul(chosen, rest[...])
    out_ref[...] = encoded_ref[...] + confidence_ref[...] * spread


def smooth_back_kernel(
    probs_ref,
    grad_ref,
    confidence_ref,
    rank_ref,
    smooth_ref,
    down_ref,
    grad_down_ref,
    grad_confidence_ref,
    grad_probs_ref,
    total,
    low,
):
    count = down_ref.shape[0]
    width = down_ref.shape[1]
    step = pl.program_id(0)

    @pl.when(step == 0)
    def _():
        total[...] = jnp.zeros_like(total)
        low[:count, :] = to_low(smooth_ref[...])
        low[count:, :] = jnp.zeros((SLOTS - count, width), jnp.bfloat16)

    slots = lax.broadcasted_iota(jnp.int32, (BLOCK, SLOTS), 1)
    chosen = jnp.where(slots == rank_ref[...], 1.0, 0.0).astype(jnp.bfloat16)
    gradient = grad_ref[...]
    total[...] += left_product(chosen, to_low(confidence_ref[...] * gradient))
    grad_confidence_ref[...] = jnp.sum(gradient * matmul(chosen, low[...]), axis=1, keepdims=True)

    @pl.when(step == pl.num_programs(0) - 1)
    def _():
        tiles = count // 16

        def tile(index, later):
            index = tiles - 1 - index
            start = pl.multiple_of(index * 16, 16)
            rows = total[pl.ds(start, 16), :]
            done = [None] * 16
            kept = [None] * 16
            for r in range(15, -1, -1):
                later = rows[r : r + 1] + (1.0 - probs_ref[start + r + 1]) * later
                kept[r] = later
                done[r] = probs_ref[start + r] * later
            grad_down_ref[pl.ds(start, 16), :] = to_low(jnp.concatenate(done, 0))
            total[pl.ds(start, 16), :] = jnp.concatenate(kept, 0)
            return later

        lax.fori_loop(0, tiles, tile, jnp.zeros((1, width), jnp.float32))
        smooth = smooth_ref[...]
        places = lax.broadcasted_iota(jnp.int32, (count, 1), 0)
        before = jnp.where(places == 0, 0.0, pltpu.roll(smooth, 1, 0))
        grad_probs_ref[...] = jnp.sum(
            total[:count, :] * (down_ref[...] - before), axis=1, keepdims=True
        )


def byte_rows(size):
    return pl.BlockSpec((BLOCK, size), lambda step: (step, 0))


def kernel_settings(flops, traffic):
    return dict(
        compiler_params=pltpu.CompilerParams(
            dimension_semantics=("arbitrary",), vmem_limit_bytes=48 * 1024 * 1024
        ),
        cost_estimate=pl.CostEstimate(flops=flops, bytes_accessed=traffic, transcendentals=0),
    )


def smooth_forward(probs, down_rows, encoded, confidence, rank):
    length, width = encoded.shape
    count = down_rows.shape[0]
    wide = jnp.float32
    return pl.pallas_call(
        smooth_kernel,
        grid=(length // BLOCK,),
        in_specs=[
            pl.BlockSpec(memory_space=pltpu.SMEM),
            whole_block(count, width),
            byte_rows(width),
            byte_rows(1),
            byte_rows(1),
        ],
        out_specs=[byte_rows(width), whole_block(count, width)],
        out_shape=[
            jax.ShapeDtypeStruct((length, width), wide),
            jax.ShapeDtypeStruct((count, width), wide),
        ],
        scratch_shapes=[pltpu.VMEM((SLOTS, width), jnp.bfloat16)] * 2,
        **kernel_settings(4 * length * SLOTS * width, length * width * 8),
    )(probs, down_rows, encoded, confidence, rank)


def smooth_backward(probs, gradient, confidence, rank, smooth, down_rows):
    length, width = gradient.shape
    count = down_rows.shape[0]
    wide = jnp.float32
    return pl.pallas_call(
        smooth_back_kernel,
        grid=(length // BLOCK,),
        in_specs=[
            pl.BlockSpec(memory_space=pltpu.SMEM),
            byte_rows(width),
            byte_rows(1),
            byte_rows(1),
            whole_block(count, width),
            whole_block(count, width),
        ],
        out_specs=[whole_block(count, width), byte_rows(1), whole_block(count, 1)],
        out_shape=[
            jax.ShapeDtypeStruct((count, width), jnp.bfloat16),
            jax.ShapeDtypeStruct((length, 1), wide),
            jax.ShapeDtypeStruct((count, 1), wide),
        ],
        scratch_shapes=[pltpu.VMEM((SLOTS, width), wide), pltpu.VMEM((SLOTS, width), jnp.bfloat16)],
        **kernel_settings(4 * length * SLOTS * width, length * width * 4),
    )(probs, gradient, confidence, rank, smooth, down_rows)


def turned(values, cosines, sines):
    lane = lax.broadcasted_iota(jnp.int32, values.shape, 1) % HEAD_SIZE
    swapped = jnp.where(
        lane < HEAD_SIZE // 2,
        pltpu.roll(values, LANES - HEAD_SIZE // 2, 1),
        pltpu.roll(values, HEAD_SIZE // 2, 1),
    )
    return values * cosines + swapped * sines


def attend_mask(items_ref, items_row_ref):
    size = items_ref.shape[0]
    rows = lax.broadcasted_iota(jnp.int32, (size, size), 0)
    cols = lax.broadcasted_iota(jnp.int32, (size, size), 1)
    return (rows >= cols) & (items_ref[...] == items_row_ref[0:1, :])


def softmaxed(queries, keys, visible):
    scores = right_product(queries, keys) * HEAD_SIZE ** (-0.5)
    scores = jnp.where(visible, scores, -1e30)
    weights = jnp.exp(scores - jnp.max(scores, axis=1, keepdims=True))
    return weights / jnp.sum(weights, axis=1, keepdims=True)


def half_lanes(values, half):
    lane = lax.broadcasted_iota(jnp.int32, (1, LANES), 1) // HEAD_SIZE
    return jnp.where(lane == half, values, jnp.zeros_like(values))


HEADS_PER_BLOCK = 3
BLOCK_WIDTH = 2 * LANES


def unpacked(block, cosines, sines):
    width = HEADS_PER_BLOCK * HEAD_SIZE
    size = block.shape[1]
    queries = block[:, :BLOCK_WIDTH]
    keys = pltpu.roll(block, size - width, 1)[:, :BLOCK_WIDTH]
    values = pltpu.roll(block, size - 2 * width, 1)[:, :BLOCK_WIDTH]
    tiles = []
    for tile in range(2):
        lanes = slice(tile * LANES, (tile + 1) * LANES)
        tiles.append(
            (
                to_low(turned(queries[:, lanes], cosines, sines)),
                to_low(turned(keys[:, lanes], cosines, sines)),
                to_low(values[:, lanes]),
            )
        )
    return tiles


def attend_kernel(qkv_ref, cos_ref, sin_ref, items_ref, items_row_ref, out_ref):
    visible = attend_mask(items_ref, items_row_ref)
    tiles = unpacked(qkv_ref[...], cos_ref[...], sin_ref[...])
    for tile, (queries, keys, values) in enumerate(tiles):
        mixed = 0.0
        for half in range(2 - tile):
            weights = softmaxed(half_lanes(queries, half), keys, visible)
            mixed = mixed + matmul(to_low(weights), half_lanes(values, half))
        out_ref[:, tile * LANES : (tile + 1) * LANES] = to_low(mixed)


def attend_back_kernel(
    qkv_ref, grad_ref, cos_ref, sin_ref, items_ref, items_row_ref, grad_qkv_ref
):
    visible = attend_mask(items_ref, items_row_ref)
    cosines = cos_ref[...]
    sines = sin_ref[...]
    scale = HEAD_SIZE ** (-0.5)
    tiles = unpacked(qkv_ref[...], cosines, sines)
    grads = ([], [], [])
    for tile, (queries, keys, values) in enumerate(tiles):
        gradient = to_low(grad_ref[:, tile * LANES : (tile + 1) * LANES])
        grad_q = 0.0
        grad_k = 0.0
        grad_v = 0.0
        for half in range(2 - tile):
            own_queries = half_lanes(queries, half)
            own_grad = half_lanes(gradient, half)
            weights = softmaxed(own_queries, keys, visible)
            grad_weights = right_product(own_grad, values)
            grad_v = grad_v + left_product(to_low(weights), own_grad)
            inner = jnp.sum(grad_weights * weights, axis=1, keepdims=True)
            grad_scores = to_low(jnp.where(visible, weights * (grad_weights - inner), 0.0))
            grad_q = grad_q + matmul(grad_scores, half_lanes(keys, half))
            grad_k = grad_k + left_product(grad_scores, own_queries)
        grads[0].append(turned(grad_q * scale, cosines, -sines))
        grads[1].append(turned(grad_k * scale, cosines, -sines))
        grads[2].append(grad_v)
    size = qkv_ref.shape[1]
    width = HEADS_PER_BLOCK * HEAD_SIZE
    filling = jnp.zeros((qkv_ref.shape[0], size - BLOCK_WIDTH), jnp.float32)
    packed = 0.0
    for kind, both in enumerate(grads):
        wide = jnp.concatenate(both + [filling], 1)
        packed = packed + (pltpu.roll(wide, kind * width, 1) if kind else wide)
    grad_qkv_ref[...] = to_low(packed)


def turn_tables(count):
    half = HEAD_SIZE // 2
    lane = jnp.arange(LANES) % HEAD_SIZE
    frequency = 10000.0 ** (-(lane % half).astype(jnp.float32) * (2.0 / HEAD_SIZE))
    angles = jnp.arange(count, dtype=jnp.float32)[:, None] * frequency[None, :]
    return jnp.cos(angles), jnp.where(lane < half, -1.0, 1.0)[None, :] * jnp.sin(angles)


def attend(qkv, gradient, tables, group_items, depths):
    count, width = qkv.shape
    size = width // depths

    def tiles(columns):
        return pl.BlockSpec((count, columns), lambda step: (0, step))

    backward = gradient is not None
    items = group_items.astype(jnp.int32)
    out = size if backward else BLOCK_WIDTH
    return pl.pallas_call(
        attend_back_kernel if backward else attend_kernel,
        grid=(depths,),
        in_specs=[tiles(size)]
        + [tiles(BLOCK_WIDTH)] * backward
        + [whole_block(count, LANES)] * 2
        + [whole_block(count, 1), whole_block(8, count)],
        out_specs=tiles(out),
        out_shape=jax.ShapeDtypeStruct((count, depths * out), jnp.bfloat16),
        **kernel_settings(8 * count * count * width, count * width * 16),
    )(
        qkv,
        *([gradient] if backward else []),
        *tables,
        items[:, None],
        jnp.broadcast_to(items[None, :], (8, count)),
    )


def active_kernel(pair_ref, out_ref):
    size = out_ref.shape[1]
    gate = pair_ref[:, :size]
    out_ref[...] = to_low(gate * sigmoid(gate) * pair_ref[:, size:])


def active_back_kernel(pair_ref, grad_ref, out_ref):
    size = grad_ref.shape[1]
    gate = pair_ref[:, :size]
    upper = pair_ref[:, size:]
    opened = sigmoid(gate)
    gradient = grad_ref[...]
    out_ref[:, :size] = to_low(
        gradient * upper * (opened + gate * opened * (1.0 - opened))
    )
    out_ref[:, size:] = to_low(gradient * gate * opened)


def activate(pairs, gradient, depths):
    count, width = pairs.shape
    size = width // depths // 2

    def tiles(columns):
        return pl.BlockSpec((count, columns), lambda step: (0, step))

    backward = gradient is not None
    out = 2 * size if backward else size
    return pl.pallas_call(
        active_back_kernel if backward else active_kernel,
        grid=(depths,),
        in_specs=[tiles(2 * size)] + [tiles(size)] * backward,
        out_specs=tiles(out),
        out_shape=jax.ShapeDtypeStruct((count, depths * out), jnp.bfloat16),
        **kernel_settings(count * width * 8, count * width * 8),
    )(pairs, *([gradient] if backward else []))


def dots_kernel(depths, qk_ref, out_ref, tail):
    size = qk_ref.shape[1] // depths // 2

    @pl.when(pl.program_id(0) == 0)
    def _():
        tail[...] = jnp.zeros_like(tail)

    sums = [0.0, 0.0, 0.0]
    for k in range(depths):
        queries = qk_ref[:, 2 * k * size : (2 * k + 1) * size]
        keys = qk_ref[:, (2 * k + 1) * size : (2 * k + 2) * size]
        lanes = slice(k * size, (k + 1) * size)
        previous = shifted_down(tail[:, lanes], keys, 1)
        tail[:, lanes] = keys[BLOCK - 8 :]
        sums[0] = sums[0] + queries * previous
        sums[1] = sums[1] + queries * queries
        sums[2] = sums[2] + previous * previous
    for kind in range(3):
        out_ref[:, kind : kind + 1] = jnp.sum(sums[kind], axis=1, keepdims=True)
    out_ref[:, 3:] = jnp.zeros((BLOCK, 5), jnp.float32)


def dots_back_kernel(depths, qk_ref, tail_ref, grad_ref, later_ref, out_ref, head):
    size = qk_ref.shape[1] // depths // 2
    step = pl.program_id(0)
    first_block = step == pl.num_programs(0) - 1

    @pl.when(step == 0)
    def _():
        head[...] = jnp.zeros_like(head)

    for k in range(depths):
        query_lanes = slice(2 * k * size, (2 * k + 1) * size)
        key_lanes = slice((2 * k + 1) * size, (2 * k + 2) * size)
        lanes = slice(k * size, (k + 1) * size)
        queries = qk_ref[:, query_lanes]
        keys = qk_ref[:, key_lanes]
        tail = jnp.where(first_block, 0.0, tail_ref[:, key_lanes])
        previous = shifted_down(tail, keys, 1)
        following = shifted_up(queries, head[:, lanes], 1)
        head[:, lanes] = queries[:8]
        out_ref[:, query_lanes] = to_low(
            grad_ref[:, 0:1] * previous + 2.0 * grad_ref[:, 1:2] * queries
        )
        out_ref[:, key_lanes] = to_low(
            later_ref[:, 0:1] * following + 2.0 * later_ref[:, 2:3] * keys
        )


def pair_dots(qk, depths):
    length, width = qk.shape
    return pl.pallas_call(
        functools.partial(dots_kernel, depths),
        grid=(length // BLOCK,),
        in_specs=[byte_rows(width)],
        out_specs=byte_rows(8),
        out_shape=jax.ShapeDtypeStruct((length, 8), jnp.float32),
        scratch_shapes=[pltpu.VMEM((8, width // 2), jnp.float32)],
        **kernel_settings(length * width * 4, length * width * 4),
    )(qk)


def pair_dots_back(qk, gradient, depths):
    length, width = qk.shape
    chunks = length // BLOCK
    eighths = BLOCK // 8
    later = jnp.concatenate([gradient[1:], jnp.zeros((1, 8), jnp.float32)], 0)

    def rows(size):
        return pl.BlockSpec((BLOCK, size), lambda step: (chunks - 1 - step, 0))

    return pl.pallas_call(
        functools.partial(dots_back_kernel, depths),
        grid=(chunks,),
        in_specs=[
            rows(width),
            pl.BlockSpec(
                (8, width), lambda step: (jnp.maximum((chunks - 1 - step) * eighths - 1, 0), 0)
            ),
            rows(8),
            rows(8),
        ],
        out_specs=rows(width),
        out_shape=jax.ShapeDtypeStruct((length, width), jnp.bfloat16),
        scratch_shapes=[pltpu.VMEM((8, width // 2), jnp.float32)],
        **kernel_settings(length * width * 4, length * width * 8),
    )(qk, qk, gradient, later)


def core_swap(values):
    size = lax.axis_size("dp")
    return lax.ppermute(values, "dp", [(d, d ^ 1) for d in range(size)])


def chip_swap(values, bit):
    size = lax.axis_size("dp")
    return lax.ppermute(values, "dp", [(d, d ^ (bit * 2)) for d in range(size)])


def depth_swap(values, offset):
    if offset == 0:
        return values
    size = lax.axis_size("mp")
    return lax.ppermute(values, "mp", [(d, d ^ offset) for d in range(size)])


class Place:
    def __init__(self):
        dp_index = lax.axis_index("dp")
        self.core = dp_index % 2
        self.chip = dp_index // 2
        self.depth = lax.axis_index("mp")
        self.chips = lax.axis_size("dp") // 2
        self.depths = lax.axis_size("mp")
        bits = []
        while 2 ** len(bits) < self.chips:
            bits.append(2 ** len(bits))
        self.bits = bits


def both_cores(place, own, other, axis):
    first = place.core == 0
    return jnp.concatenate([jnp.where(first, own, other), jnp.where(first, other, own)], axis)


def pick(values, index, size, axis):
    return lax.dynamic_slice_in_dim(values, index * size, size, axis)


def reorder(values, count, shift, axis=-1):
    axis = axis % values.ndim
    size = values.shape[axis] // count
    return jnp.concatenate([pick(values, r ^ shift, size, axis) for r in range(count)], axis)


def relative_to_chip(place, values):
    if place.chips == place.depths:
        return reorder(values, place.chips, place.chip ^ place.depth)
    return reorder(reorder(values, place.depths, place.depth), place.chips, place.chip)


def chip_to_relative(place, values):
    if place.chips == place.depths:
        return reorder(values, place.chips, place.chip ^ place.depth)
    return reorder(reorder(values, place.chips, place.chip), place.depths, place.depth)


def depth_to_chip(place, values):
    return reorder(values, place.chips, place.chip)


def split_columns(place, shards):
    axis = shards[0].ndim - 1

    def columns(core):
        return jnp.concatenate([pick(s, core, s.shape[-1] // 2, axis) for s in shards], axis)

    other = core_swap(columns(1 - place.core))
    return both_cores(place, columns(place.core), other, axis - 1)


def split_rows(place, shard):
    half = shard.shape[-2] // 2
    own = pick(shard, place.core, half, shard.ndim - 2)
    other = core_swap(pick(shard, 1 - place.core, half, shard.ndim - 2))
    return both_cores(place, own, other, shard.ndim - 1)


def join_columns(place, block):
    half = block.shape[-2] // 2
    own = pick(block, place.core, half, block.ndim - 2)
    other = core_swap(pick(block, 1 - place.core, half, block.ndim - 2))
    return both_cores(place, own, other, block.ndim - 1)


def join_rows(place, block):
    half = block.shape[-1] // 2
    own = pick(block, place.core, half, block.ndim - 1)
    other = core_swap(pick(block, 1 - place.core, half, block.ndim - 1))
    return both_cores(place, own, other, block.ndim - 2)


def padded_rows(rows):
    return -(-rows // LANES) * LANES


def assemble_kernel(places, items, size, *refs):
    sources = refs[: len(places)]
    outs = refs[len(places) :]
    rows = sources[0].shape[1]
    for (r, first, count), ref in zip(places, sources):

        @pl.when(pl.program_id(0) == r)
        def _(first=first, count=count, ref=ref):
            offset = 0
            for (kind, width), out_ref in zip(items, outs):
                if kind == "folded":
                    half = rows // 2
                    for k in range(count):
                        j = (first + k) * (width + width // 2)
                        out_ref[:, j : j + width] = ref[k, :half, offset : offset + width]
                        out_ref[:, j + width : j + width + width // 2] = ref[
                            k, half:, offset : offset + width // 2
                        ]
                    offset += width
                    continue
                for k in range(count):
                    i = (first + k) * size if kind == "rows" else 0
                    j = (first + k) * width if kind == "columns" else 0
                    out_ref[i : i + rows, j : j + width] = ref[k, :, offset : offset + width]
                    if size > rows:
                        out_ref[i + rows : i + size, j : j + width] = jnp.zeros(
                            (size - rows, width), jnp.bfloat16
                        )
                offset += width


def assemble(place, pieces, items, filled):
    chips, depths = place.chips, place.depths
    rows = pieces[0][2].shape[1]
    size = padded_rows(rows) if filled else rows
    if any(width % LANES for _, width in items):
        matrices = []
        offset = 0
        for kind, width in items:
            arrays = [
                jnp.pad(a[:, :, offset : offset + width], ((0, 0), (0, size - rows), (0, 0)))
                for _, _, a in pieces
            ]
            if kind == "rows":
                arrays = [a.reshape(depths * size, width) for a in arrays]
                matrices.append(jnp.concatenate(arrays, 1))
            else:
                arrays = [jnp.concatenate([a[k] for k in range(depths)], 1) for a in arrays]
                matrices.append(jnp.concatenate(arrays, 0))
            offset += width
        return matrices
    shapes = []
    blocks = []
    for kind, width in items:
        if kind == "rows":
            shapes.append((depths * size, chips * width))
            blocks.append(pl.BlockSpec((depths * size, width), lambda i: (0, i)))
        elif kind == "folded":
            whole = depths * (width + width // 2)
            shapes.append((chips * size // 2, whole))
            blocks.append(pl.BlockSpec((size // 2, whole), lambda i: (i, 0)))
        else:
            shapes.append((chips * size, depths * width))
            blocks.append(pl.BlockSpec((size, depths * width), lambda i: (i, 0)))
    places = [(r, first, array.shape[0]) for r, first, array in pieces]
    return pl.pallas_call(
        functools.partial(assemble_kernel, places, items, size),
        grid=(chips,),
        in_specs=[whole_block(*array.shape) for _, _, array in pieces],
        out_specs=blocks,
        out_shape=[jax.ShapeDtypeStruct(shape, jnp.bfloat16) for shape in shapes],
        **kernel_settings(0, sum(4 * a * b for a, b in shapes)),
    )(*[array for _, _, array in pieces])


def held_for(values, earlier):
    if not earlier:
        return values
    return lax.optimization_barrier((values, *earlier))[0]


class Gather:
    def __init__(self, place):
        self.place = place
        self.near = []
        self.far = []

    def hold(self, values, waits=()):
        return held_for(values, sum(self.near[-1:] + self.far[-2:-1], list(waits)))

    def pieces(self, shard, waits):
        place = self.place
        shard = self.hold(shard, waits)
        stack = lax.all_gather(shard, "mp", axis=0)
        if place.chips == 4:
            half = place.depths // 2
            along = [chip_swap(stack, bit) for bit in (1, 2)]
            across = [chip_swap(along[0][:half], 2), chip_swap(along[1][half:], 1)]
            self.near.append([stack])
            self.far.append(along)
            return [
                (0, 0, stack),
                (1, 0, along[0]),
                (2, 0, along[1]),
                (3, 0, across[0]),
                (3, half, across[1]),
            ]
        pieces = {0: stack}
        for bit in place.bits:
            for r, piece in list(pieces.items()):
                pieces[r ^ bit] = chip_swap(piece, bit)
        self.near.append([stack])
        return [(r, 0, pieces[r]) for r in range(place.chips)]

    def matrices(self, shards, waits=(), filled=False):
        rows = shards[0][1].shape[0]
        folded = [kind == "folded" for kind, _ in shards]
        for index, (kind, shard) in enumerate(shards):
            if kind == "folded":
                third = shard.shape[1] // 3
                if 2 * shard.shape[0] == rows and third % LANES == 0:
                    last = jnp.pad(shard[:, 2 * third :], ((0, 0), (0, third)))
                    shard = jnp.concatenate([shard[:, : 2 * third], last], 0)
                else:
                    kind = "columns"
                shards = shards[:index] + [(kind, shard)] + shards[index + 1 :]
        if len({shard.shape[0] for _, shard in shards}) > 1:
            return [
                self.matrices([item], waits, filled or flag)[0]
                for item, flag in zip(shards, folded)
            ]
        items = [(kind, shard.shape[1]) for kind, shard in shards]
        packed = jnp.concatenate([shard for _, shard in shards], 1)
        return assemble(self.place, self.pieces(packed, waits), items, filled)


def gather_chips(place, shard, bits):
    pieces = {0: shard}
    for bit in bits:
        for r, piece in list(pieces.items()):
            pieces[r ^ bit] = chip_swap(piece, bit)
    return jnp.concatenate([pieces[r] for r in range(place.chips)], -2)


def send_order(place, bits):
    order = [0]
    for bit in reversed(bits):
        order = order + [r ^ bit for r in order]
    return order


def chosen(step, values):
    result = 0
    for index, value in enumerate(values):
        result = result + jnp.where(step == index, value, 0)
    return result


def products_kernel(kinds, rows, *refs):
    out_ref = refs[-1]
    offset = 0
    for index, kind in enumerate(kinds):
        chip_side = refs[2 * index][...]
        depth_side = refs[2 * index + 1][...]
        if kind == "columns":
            block = left_product(chip_side, depth_side)
        else:
            block = left_product(depth_side, chip_side)
        width = block.shape[1]
        out_ref[0, :, offset : offset + width] = to_low(block[:rows])
        offset += width


class Scatter:
    def __init__(self, place):
        self.place = place
        self.near = []
        self.far = []

    def blocks(self, items, rows, chips, depths):
        place = self.place
        steps = [(r, k) for r in chips for k in depths]
        sizes = []
        aligned = True
        for kind, chip_side, depth_side in items:
            a = chip_side.shape[1] // place.chips
            b = depth_side.shape[1] // place.depths
            sizes.append((a, b, b if kind == "columns" else a))
            aligned = aligned and a % LANES == 0 and b % LANES == 0
        if not aligned:
            parts = []
            for (kind, chip_side, depth_side), (a, b, _) in zip(items, sizes):
                if kind == "columns":
                    whole = left_product(chip_side, depth_side)
                    whole = whole.reshape(place.chips, a, place.depths, b).transpose(0, 2, 1, 3)
                else:
                    whole = left_product(depth_side, chip_side)
                    whole = whole.reshape(place.depths, b, place.chips, a).transpose(2, 0, 1, 3)
                parts.append(to_low(whole[:, :, :rows]))
            whole = jnp.concatenate(parts, 3)
            return jnp.stack([jnp.stack([whole[r, k] for k in depths]) for r in chips])
        width = sum(size[2] for size in sizes)
        specs = []
        for (kind, chip_side, depth_side), (a, b, _) in zip(items, sizes):
            count = chip_side.shape[0]
            specs.append(
                pl.BlockSpec((count, a), lambda s: (0, chosen(s, [r for r, _ in steps])))
            )
            specs.append(
                pl.BlockSpec((count, b), lambda s: (0, chosen(s, [k for _, k in steps])))
            )
        count = items[0][1].shape[0]
        out = pl.pallas_call(
            functools.partial(products_kernel, [kind for kind, _, _ in items], rows),
            grid=(len(steps),),
            in_specs=specs,
            out_specs=pl.BlockSpec((1, rows, width), lambda s: (s, 0, 0)),
            out_shape=jax.ShapeDtypeStruct((len(steps), rows, width), jnp.bfloat16),
            **kernel_settings(
                2 * len(steps) * count * rows * width, len(steps) * (rows + count) * width * 2
            ),
        )(*[side for _, *sides in items for side in sides])
        return out.reshape(len(chips), len(depths), rows, width)

    def own(self, items, all_rows, waits=(), reduced=False):
        if len(set(all_rows)) > 1:
            parts = [self.own([item], [n], waits, reduced)[0] for item, n in zip(items, all_rows)]
            return parts
        place = self.place
        rows = all_rows[0]
        kind, chip_side, depth_side = items[0]
        chip_side = held_for(chip_side, sum(self.near[-2:-1] + self.far[-3:-2], list(waits)))
        items = [(kind, chip_side, depth_side)] + list(items[1:])
        half = place.depths // 2
        orders = (place.bits[::-1], place.bits)
        depth_sets = (range(half), range(half, place.depths))
        middle = place.chips // 2
        order_lists = [send_order(place, bits) for bits in orders]
        sents = [
            self.blocks(items, rows, order[middle:], ks)
            for order, ks in zip(order_lists, depth_sets)
        ]
        kepts = [
            self.blocks(items, rows, order[:middle], ks)
            for order, ks in zip(order_lists, depth_sets)
        ]
        got = []
        for step in range(len(place.bits)):
            got = [chip_swap(sent, bits[step]) for sent, bits in zip(sents, orders)]
            sums = [a.astype(jnp.float32) + b.astype(jnp.float32) for a, b in zip(kepts, got)]
            middle = middle // 2
            sents = [to_low(total[middle:]) for total in sums]
            kepts = [total[:middle] for total in sums] if middle else sums
            if step == 0:
                self.near.append(sents)
        by_depth = jnp.concatenate([total[0] for total in kepts], 0)
        if reduced:
            going = to_low(by_depth)
            self.far.append([going])
            total = lax.psum_scatter(going, "mp", scatter_dimension=0).astype(jnp.float32)
        else:
            blocks = [
                lax.dynamic_index_in_dim(by_depth, place.depth ^ k, 0, keepdims=False)
                for k in range(place.depths)
            ]
            going = [to_low(block) for block in blocks[1:]]
            arrived = [depth_swap(block, k + 1) for k, block in enumerate(going)]
            self.far.append(going)
            total = blocks[0]
            for values in arrived:
                total = total + values.astype(jnp.float32)
        parts = []
        offset = 0
        for kind, chip_side, depth_side in items:
            side = (depth_side, place.depths) if kind == "columns" else (chip_side, place.chips)
            width = side[0].shape[1] // side[1]
            parts.append(total[:, offset : offset + width])
            offset += width
        return parts


def core_sum(partial):
    return partial + core_swap(to_low(partial)).astype(jnp.float32)


def core_sum_exact(partial):
    return partial + core_swap(partial)


def parity_part(place, values):
    size = values.shape[1] // (2 * place.chips)
    split = values.reshape(values.shape[0], place.chips, 2, size)
    own = lax.dynamic_index_in_dim(split, place.core, 2, keepdims=False)
    own = jnp.pad(own, ((0, 0), (0, 0), (0, padded_rows(size) - size)))
    return own.reshape(values.shape[0], -1)


def parity_join(place, own, size):
    rows = own.shape[0]
    own = own.reshape(rows, place.chips, -1)[:, :, :size]
    other = core_swap(own)
    return both_cores(place, own[:, :, None], other[:, :, None], 2).reshape(rows, -1)


def other_rows(place, values):
    micro, length, width = values.shape
    halves = values.reshape(micro, 2, length // 2, width)
    return core_swap(lax.dynamic_index_in_dim(halves, 1 - place.core, 1, keepdims=True))


def own_sequence(place, values, other):
    micro, length, width = values.shape
    halves = values.reshape(micro, 2, length // 2, width)
    own = lax.dynamic_index_in_dim(halves, place.core, 1, keepdims=True)
    half = both_cores(place, own, other, 1).reshape(micro * 2, length // 2, width)
    blocks = [
        depth_swap(lax.dynamic_index_in_dim(half, place.depth ^ k, 0, keepdims=False), k)
        for k in range(place.depths)
    ]
    rows = relative_to_chip(place, jnp.concatenate(blocks, 1))
    return both_cores(place, rows, core_swap(rows), 0)


def back_to_all(place, values, micro):
    length = values.shape[0]
    rows = chip_to_relative(place, pick(values, place.core, length // 2, 0))
    width = rows.shape[1] // place.depths
    blocks = [
        depth_swap(rows[:, k * width : (k + 1) * width], k)[None] for k in range(place.depths)
    ]
    by_sequence = reorder(jnp.concatenate(blocks, 0), place.depths, place.depth, 0)
    by_sequence = by_sequence.reshape(micro, 2, length // 2, width)
    own = lax.dynamic_index_in_dim(by_sequence, place.core, 1, keepdims=False)
    other = core_swap(lax.dynamic_index_in_dim(by_sequence, 1 - place.core, 1, keepdims=False))
    return both_cores(place, own, other, 1)


def own_row(place, values):
    both = both_cores(place, values[None], core_swap(values)[None], 0)
    both = jnp.swapaxes(both, 0, 1).reshape((-1,) + values.shape[1:])
    return lax.dynamic_index_in_dim(both, place.depth, 0, keepdims=False)


def own_channels(place, values):
    size = values.shape[-1] // (2 * place.depths)
    return jnp.concatenate(
        [
            pick(values, k * 2 + place.core, size, values.ndim - 1)
            for k in range(place.depths)
        ],
        -1,
    )


def all_channels(place, values):
    size = values.shape[-1] // place.depths
    full = jnp.zeros(values.shape[:-1] + (2 * values.shape[-1],), values.dtype)
    for k in range(place.depths):
        block = values[..., k * size : (k + 1) * size]
        full = lax.dynamic_update_slice_in_dim(
            full, block, (k * 2 + place.core) * size, values.ndim - 1
        )
    return full


def norm_forward(values, gain):
    low = to_low(values)
    wide = low.astype(jnp.float32)
    scale = lax.rsqrt(jnp.mean(wide * wide, axis=-1, keepdims=True) + EPSILON)
    return to_low(wide * scale * gain), (low, scale)


def norm_backward(gradient, memory, gain):
    low, scale = memory
    wide = low.astype(jnp.float32)
    weighted = gradient * gain
    inner = jnp.mean(weighted * wide, axis=-1, keepdims=True)
    grad_gain = jnp.sum(gradient * (wide * scale), axis=0)
    return scale * weighted - wide * (scale * scale * scale * inner), grad_gain


def mamba_forward(place, residual, weights, params, items):
    w_zx, w_bcdt, w_out = weights
    norm, taps, map_taps, heads, channels, owner = params
    columns, ahead, segment_rows = items
    normed_low, norm_memory = norm_forward(residual, norm)
    zx_proj = matmul(normed_low, w_zx)
    bcdt = matmul(normed_low, w_bcdt)
    per_block = channels.shape[1] // place.depths // LANES
    mixed, y, squares, states = mix_forward(
        per_block, zx_proj, bcdt, columns, segment_rows, taps, map_taps, heads, channels
    )
    scale = lax.rsqrt(core_sum_exact(squares) / (2 * mixed.shape[1]) + EPSILON)
    result = residual + core_sum(matmul(mixed, w_out)) * scale
    return (result, (normed_low, mixed, norm_memory, scale, zx_proj, bcdt, y, states))


def mamba_backward(place, gradient, weights, params, items, memory, scatter, more, reduced):
    w_zx, w_bcdt, w_out = weights
    norm, taps, map_taps, heads, channels, owner = params
    columns, ahead, segment_rows = items
    normed_low, mixed, norm_memory, scale, zx_proj, bcdt, y, states = memory
    spread = to_low(gradient)
    grad_mixed = right_product(spread, w_out)
    width = mixed.shape[1]
    inner = core_sum_exact(
        jnp.sum(grad_mixed * mixed.astype(jnp.float32), axis=1, keepdims=True)
    )
    coefficient = scale * scale * scale * inner / (2 * width)
    nothing = jnp.zeros_like(scale[:, 0])
    later = jnp.stack(ahead + [scale[:, 0], coefficient[:, 0], nothing, nothing, nothing], 1)
    grad_zx, grad_maps, grad_dt, grad_taps, grad_map_taps, grad_heads, grad_channels = (
        mix_backward(
            width // place.depths // LANES,
            grad_mixed,
            zx_proj,
            bcdt,
            y,
            states,
            columns,
            later,
            segment_rows,
            taps,
            map_taps,
            heads,
            channels,
            owner,
        )
    )
    head_count = width // HEAD_SIZE
    grad_maps = core_sum_exact(grad_maps)
    own_maps = to_low(pick(grad_maps, place.core, LANES, 1))
    low_dt = to_low(grad_dt)
    grad_bcdt = jnp.concatenate([own_maps, low_dt], 1)
    own_bcdt = jnp.concatenate([pick(w_bcdt, place.core, LANES, 1), w_bcdt[:, 2 * LANES :]], 1)
    partial = right_product(grad_zx, w_zx) + right_product(grad_bcdt, own_bcdt)
    grad_in, grad_norm = norm_backward(core_sum(partial), norm_memory, norm)
    small_from = jnp.concatenate([own_maps, low_dt[:, :head_count]], 1)
    scaled = to_low(spread.astype(jnp.float32) * scale)
    rows = normed_low.shape[1] // place.chips
    weight_grads = scatter.own(
        [("columns", normed_low, grad_zx), ("rows", scaled, mixed)] + more,
        [rows, width // place.depths] + [rows] * len(more),
        [partial],
        reduced,
    )
    by_tap = grad_taps.reshape(4, 8, -1).sum(1)
    map_by_tap = grad_map_taps.reshape(4, 8, -1).sum(1)
    head_sums = grad_heads.reshape(2, 8, -1).sum(1)[:, :head_count]
    channel_sums = grad_channels.reshape(2, 8, -1).sum(1)
    small_grads = (
        0.5 * grad_norm,
        by_tap,
        map_by_tap,
        head_sums[0],
        head_sums[1],
        channel_sums[0].reshape(head_count, HEAD_SIZE).sum(1),
        channel_sums[1],
    )
    return (gradient + grad_in, weight_grads, small_grads, (normed_low, small_from))


def small_scatter(place, pairs, half_maps, waits):
    wholes = []
    for normed, small_from in pairs:
        whole = left_product(normed, small_from)
        maps = jnp.zeros((whole.shape[0], 2 * half_maps), jnp.float32)
        maps = lax.dynamic_update_slice_in_dim(
            maps, whole[:, :half_maps], place.core * half_maps, 1
        )
        wholes += [maps, all_channels(place, whole[:, half_maps:])]
    rows = reorder(jnp.concatenate(wholes, 1), place.chips, place.chip, 0)
    rows = lax.psum(lax.psum_scatter(rows, "dp", scatter_dimension=0, tiled=True), "mp")
    rows = held_for(rows, waits)
    width = rows.shape[1] // 2
    layers = jnp.stack([rows[:, :width], rows[:, width:]])
    steps = layers[:, :, 2 * half_maps :]
    return layers[:, :, : 2 * half_maps], pick(
        steps, place.depth, steps.shape[2] // place.depths, 2
    )


def one_device(
    inputs,
    cotangent,
    boundary_flags,
    segment_ids,
    mamba_norm,
    mamba_z,
    mamba_x,
    mamba_bc,
    mamba_dt,
    mamba_conv_x,
    mamba_conv_bc,
    mamba_dt_bias,
    mamba_a_log,
    mamba_skip,
    mamba_gate_norm,
    mamba_out,
    router_qk,
    group_up,
    group_down,
    attn_norms,
    attn_qkv,
    attn_out,
    ffn_gate_up,
    ffn_down,
):
    place = Place()
    micro = inputs.shape[0]
    wide = jnp.float32

    zx_shard = split_columns(place, [mamba_z[0], mamba_x[0]])
    gather = Gather(place)
    (enc_zx,) = gather.matrices([("columns", zx_shard)])
    residual_low = own_sequence(place, inputs, other_rows(place, inputs))
    residual = residual_low.astype(wide)

    mamba_bc, mamba_dt, mamba_out, router_qk, _ = lax.optimization_barrier(
        (mamba_bc, mamba_dt, mamba_out, router_qk, zx_shard)
    )
    out_shard = split_rows(place, mamba_out)
    router_shard = split_columns(place, [router_qk[0], router_qk[1]])
    qkv_shard = split_columns(place, [attn_qkv[0], attn_qkv[1], attn_qkv[2]])
    qkv_packed = jnp.pad(qkv_shard, ((0, 0), (0, -qkv_shard.shape[1] % LANES)))
    router_shard, qkv_packed, attn_out_shard, ffn_shard, ffn_down_shard = lax.optimization_barrier(
        (
            router_shard,
            qkv_packed,
            split_rows(place, attn_out),
            split_columns(place, [ffn_gate_up[0], ffn_gate_up[1]]),
            split_rows(place, ffn_down),
        )
    )
    enc_out, w_router, w_up = gather.matrices(
        [("rows", out_shard[0]), ("columns", router_shard), ("folded", group_up)]
    )
    dt_shard = split_columns(place, [mamba_dt])
    dt_shard = jnp.concatenate([depth_swap(dt_shard, k) for k in range(place.depths)], -1)
    dt_shard = reorder(dt_shard, place.depths, place.depth)
    bc_shard = both_cores(place, mamba_bc, core_swap(mamba_bc), 1)
    fill = jnp.zeros(dt_shard.shape[:2] + (LANES - dt_shard.shape[2],), jnp.bfloat16)
    w_bcdt = gather_chips(place, jnp.concatenate([bc_shard, dt_shard, fill], -1), place.bits)
    enc_weights = (enc_zx, w_bcdt[0], enc_out)
    (w_qkv,) = gather.matrices([("columns", qkv_packed)])
    w_attn_out, w_down = gather.matrices(
        [("rows", attn_out_shard), ("columns", group_down)], filled=True
    )
    boundary_flags, segment_ids = lax.optimization_barrier(
        (boundary_flags, segment_ids, w_bcdt)
    )[:2]
    flag_row = own_row(place, boundary_flags)
    segment = own_row(place, segment_ids)

    mamba_params = []
    for layer in range(2):
        taps = own_channels(place, mamba_conv_x[layer]).astype(wide)
        width = taps.shape[1]
        bias = own_channels(place, mamba_dt_bias[layer]).astype(wide)
        rate = -jnp.exp(own_channels(place, mamba_a_log[layer]).astype(wide))
        skip = own_channels(place, mamba_skip[layer]).astype(wide)
        gain = own_channels(place, mamba_gate_norm[layer]).astype(wide)
        heads = jnp.pad(jnp.stack([bias, rate]), ((0, 6), (0, LANES - bias.shape[0])))
        channels = jnp.pad(jnp.stack([jnp.repeat(skip, HEAD_SIZE), gain]), ((0, 6), (0, 0)))
        owner = (
            jnp.arange(width)[:, None] // HEAD_SIZE == jnp.arange(LANES)[None, :]
        ).astype(jnp.bfloat16)
        mamba_params.append(
            (
                reorder(mamba_norm[layer], place.chips, place.chip).astype(wide),
                taps,
                mamba_conv_bc[layer].astype(wide),
                heads,
                channels,
                owner,
            )
        )
    items = item_columns(segment)
    norm_gains = reorder(attn_norms, place.chips, place.chip).astype(wide)

    starts = jnp.concatenate([jnp.ones((1,), jnp.bool_), segment[1:] != segment[:-1]])
    group_rank = jnp.cumsum(flag_row) - 1
    slots = jnp.arange(CAP, dtype=jnp.int32)
    marked = (group_rank[None, :] == slots[:, None]) & (flag_row[None, :] == 1)
    marked_low = marked.astype(jnp.bfloat16)
    slot_valid = jnp.any(marked, axis=1)
    encoded, enc_memory = mamba_forward(
        place, residual, enc_weights, mamba_params[0], items
    )

    (w_gate_up,) = gather.matrices([("columns", ffn_shard)], [enc_memory[4]])
    (w_ffn_down,) = gather.matrices([("rows", ffn_down_shard)], [enc_memory[1]])

    shared = to_low(encoded)
    length = shared.shape[0]
    qk = matmul(shared, w_router)
    all_dots = core_sum_exact(pair_dots(qk, place.depths))
    prob_row, prob_back = jax.vjp(lambda values: boundary_prob(values.T, starts), all_dots)


    group_rows = to_low(matmul(marked_low, shared))
    group_seg = jnp.sum(jnp.where(marked, segment[None, :] + 1, 0), axis=1) - 1
    own_rows = parity_part(place, group_rows)
    hidden = depth_to_chip(place, core_sum(matmul(own_rows, w_up)))

    dec_shard = split_columns(place, [mamba_z[1], mamba_x[1]])
    dec_zx, dec_out = gather.matrices(
        [("columns", dec_shard), ("rows", out_shard[1])], [qk]
    )
    dec_weights = (dec_zx, w_bcdt[1], dec_out)

    first_low, first_memory = norm_forward(hidden, norm_gains[0])
    qkv = matmul(first_low, w_qkv)
    tables = turn_tables(CAP)
    attended_low = attend(qkv, None, tables, group_seg, place.depths)
    hidden_one = hidden + core_sum(matmul(attended_low, w_attn_out))

    cotangent = gather.hold(cotangent, [hidden_one])
    cot_row = own_sequence(place, cotangent, other_rows(place, cotangent)).astype(wide)

    second_low, second_memory = norm_forward(hidden_one, norm_gains[1])
    gate_up = matmul(second_low, w_gate_up)
    active_low = activate(gate_up, None, place.depths)
    hidden_two = hidden_one + core_sum(matmul(active_low, w_ffn_down))
    third_low = parity_part(place, to_low(hidden_two))
    down_rows = depth_to_chip(place, core_sum(matmul(third_low, w_down)))

    group_probs = jnp.sum(jnp.where(marked, prob_row[None, :], 0.0), axis=1)
    group_probs = jnp.pad(jnp.where(slot_valid, group_probs, 1.0), (0, 8))
    confidence = jnp.where(flag_row == 1, prob_row, 1.0 - prob_row)[:, None]
    rank_column = group_rank[:, None]
    decoder_in, smooth = smooth_forward(group_probs, down_rows, encoded, confidence, rank_column)
    decoded, dec_memory = mamba_forward(
        place, decoder_in, dec_weights, mamba_params[1], items
    )
    outputs = back_to_all(place, to_low(decoded), micro)

    scatter = Scatter(place)
    gradient, dec_grads, dec_smalls, dec_maps = mamba_backward(
        place,
        cot_row,
        dec_weights,
        mamba_params[1],
        items,
        dec_memory,
        scatter,
        [],
        True,
    )
    grad_down, grad_confidence, grad_slots = smooth_backward(
        group_probs, gradient, confidence, rank_column, smooth, down_rows
    )
    grad_probs = jnp.where(flag_row == 1, grad_confidence[:, 0], -grad_confidence[:, 0])
    grad_probs = grad_probs + jnp.sum(jnp.where(marked, grad_slots, 0.0), axis=0)

    dm_rows = hidden.shape[1] // place.chips
    down_low = depth_to_chip(place, grad_down)
    grad_third = to_low(right_product(down_low, w_down))
    grad_hidden = parity_join(place, grad_third, dm_rows // 2).astype(wide)
    spread = to_low(grad_hidden)
    grad_pairs = activate(gate_up, right_product(spread, w_ffn_down), place.depths)
    (own_ffn_down,) = scatter.own(
        [("rows", spread, active_low)], [active_low.shape[1] // place.depths], [grad_pairs], True
    )
    partial = right_product(grad_pairs, w_gate_up)
    (own_gate_up,) = scatter.own(
        [("columns", second_low, grad_pairs)], [dm_rows], [partial], True
    )
    grad_second, grad_norm_two = norm_backward(core_sum(partial), second_memory, norm_gains[1])
    grad_hidden = grad_hidden + grad_second

    spread = to_low(grad_hidden)
    grad_attended = right_product(spread, w_attn_out)
    grad_qkv = attend(qkv, grad_attended, tables, group_seg, place.depths)
    own_attn_out, own_down = scatter.own(
        [("rows", spread, attended_low), ("columns", third_low, down_low)],
        [HEADS_PER_BLOCK * HEAD_SIZE, dm_rows // 2],
        [grad_qkv],
    )
    partial = right_product(grad_qkv, w_qkv)
    (own_qkv,) = scatter.own([("columns", first_low, grad_qkv)], [dm_rows], [partial])
    grad_first, grad_norm_one = norm_backward(core_sum(partial), first_memory, norm_gains[0])
    grad_hidden = grad_hidden + grad_first

    hidden_low = depth_to_chip(place, to_low(grad_hidden))
    d_rows = shared.shape[1] // place.chips
    partial = to_low(right_product(hidden_low, w_up))
    (own_up,) = scatter.own([("columns", own_rows, hidden_low)], [d_rows // 2], [partial])
    grad_rows = parity_join(place, partial, d_rows // 2)
    grad_shared = left_product(marked_low, grad_rows)
    (grad_dots,) = prob_back(grad_probs)
    grad_qk = pair_dots_back(qk, grad_dots, place.depths)
    partial = right_product(grad_qk, w_router)
    (own_router,) = scatter.own([("columns", shared, grad_qk)], [d_rows], [partial])
    grad_shared = grad_shared + core_sum(partial)
    gradient = gradient + grad_shared

    gradient, enc_grads, enc_smalls, enc_maps = mamba_backward(
        place,
        gradient,
        enc_weights,
        mamba_params[0],
        items,
        enc_memory,
        scatter,
        [],
        False,
    )
    grad_inputs = back_to_all(place, to_low(gradient), micro).astype(wide)

    parts = []
    for smalls in (enc_smalls, dec_smalls):
        parts += [
            reorder(smalls[0], place.chips, place.chip),
            all_channels(place, smalls[1]),
            smalls[2],
            all_channels(place, smalls[3]),
            all_channels(place, smalls[4]),
            all_channels(place, smalls[5]),
            all_channels(place, smalls[6]),
        ]
    parts.append(0.5 * reorder(grad_norm_one, place.chips, place.chip))
    parts.append(0.5 * reorder(grad_norm_two, place.chips, place.chip))
    flat = jnp.concatenate([part.reshape(-1) for part in parts])
    fill = -flat.shape[0] % 1024
    flat = jnp.pad(flat, (0, fill)).reshape(-1, 128)
    flat = held_for(lax.psum(flat, ("dp", "mp")), scatter.far[-1]).reshape(-1)
    summed = []
    offset = 0
    for part in parts:
        summed.append(flat[offset : offset + part.size].reshape(part.shape))
        offset += part.size
    smalls = [jnp.stack([summed[n], summed[7 + n]]) for n in range(7)]

    grad_bc, grad_dt = small_scatter(place, [enc_maps, dec_maps], LANES, scatter.far[-1])

    def kinds(blocks, count):
        return join_columns(place, jnp.stack(jnp.split(blocks, count, 1)))

    enc_parts = kinds(enc_grads[0], 2)
    dec_parts = kinds(dec_grads[0], 2)
    qkv_width = qkv_shard.shape[1]
    return (
        outputs,
        grad_inputs,
        smalls[0],
        jnp.stack([enc_parts[0], dec_parts[0]]),
        jnp.stack([enc_parts[1], dec_parts[1]]),
        grad_bc,
        grad_dt,
        smalls[1],
        smalls[2],
        smalls[3],
        smalls[4],
        smalls[5],
        smalls[6],
        join_rows(place, jnp.stack([enc_grads[1], dec_grads[1]])),
        kinds(own_router, 2),
        own_up,
        own_down,
        jnp.stack([summed[14], summed[15]]),
        kinds(own_qkv[:, :qkv_width], 3),
        join_rows(place, own_attn_out),
        kinds(own_gate_up, 2),
        join_rows(place, own_ffn_down),
    )


def solution(mesh):
    in_specs = (
        P(None, "dp", "mp"),
        P(None, "dp", "mp"),
        P(None, "dp"),
        P(None, "dp"),
        P(),
        P(None, "dp", "mp"),
        P(None, "dp", "mp"),
        P(None, "dp", None),
        P(None, "dp", "mp"),
        P(),
        P(),
        P(),
        P(),
        P(),
        P(),
        P(None, "mp", "dp"),
        P(None, "dp", "mp"),
        P("dp", "mp"),
        P("dp", "mp"),
        P(),
        P(None, "dp", "mp"),
        P("mp", "dp"),
        P(None, "dp", "mp"),
        P("mp", "dp"),
    )
    out_specs = (
        P(None, "dp", "mp"),
        P(None, "dp", "mp"),
        P(),
        P(None, "dp", "mp"),
        P(None, "dp", "mp"),
        P(None, "dp", None),
        P(None, "dp", "mp"),
        P(),
        P(),
        P(),
        P(),
        P(),
        P(),
        P(None, "mp", "dp"),
        P(None, "dp", "mp"),
        P("dp", "mp"),
        P("dp", "mp"),
        P(),
        P(None, "dp", "mp"),
        P("mp", "dp"),
        P(None, "dp", "mp"),
        P("mp", "dp"),
    )
    return jax.shard_map(
        one_device, mesh=mesh, in_specs=in_specs, out_specs=out_specs, check_vma=False
    )
```
